32 devices in a mesh: shard: 8 (over y, x, core), group: 4 (over z).
Axes of the slice: x: 2, y: 2, z: 4, core: 2. Of those that a mesh axis runs over, the one named last changes fastest.
Arguments:
- embeddings: bfloat16 [16384, 768], P(('shard', 'group')), may hold values from -64 to 64
- row_group: int32 [16384, 1], P(('shard', 'group')), may hold values from 0 to 3; in each aligned block of 512 rows (0 to 511, 512 to 1023, ...) at most 128 rows name the same one
- row_cluster: int32 [16384], P(('shard', 'group')), may hold values from 0 to 5, as said below
Outputs:
- best_cosine: float32 [16384], P(('shard', 'group'))
The draws below stay inside these ranges and needn't reach their ends.
Inputs may be any that keep to these rules, and one draw needn't show every extreme that they name: `row_group`: among the 512 rows of one device at most 128 name one group, and in every draw some device has exactly 128 rows for some group. `row_cluster`: exactly 4 rows carry a label of 2 or more, each a different label; every other row carries a label below 2.
All inputs are finite; a program needn't handle non-finite values.
Results may differ from the reference program's by a relative error of at most 0.00068.
Values may be sent and summed in bfloat16 or wider, within the bound.
No kernel may reach another device: no remote copies, remote signals or barrier semaphores. Data moves between devices by JAX's collectives and lax.ppermute only.
A program may use at most 128 MiB of HBM per device.

```python
import math
import jax
import jax.numpy as jnp
import numpy as np
from jax import lax

D = 768
ROW_DEV = 512
CPG = 2
LONE = 4
CAP = 128
ROWS = 16384
N_SHARD = 8
N_GROUP = 4


family_size = 8


def draw_embeddings(key, part):
    key = jax.random.fold_in(key, 11)
    keys = jax.random.split(key, 4)
    order = jax.random.permutation(keys[0], ROWS)
    family = order // family_size
    base = jax.random.normal(keys[1], (ROWS // family_size, D), jnp.float32)
    spread = jnp.exp(jax.random.uniform(keys[2], (ROWS, 1), jnp.float32, math.log(0.25), math.log(3.0)))
    noise = jax.random.normal(keys[3], (ROWS, D), jnp.float32)
    values = base[family] + spread * noise
    return jnp.clip(values, -64.0, 64.0).astype(jnp.bfloat16)


def draw_row_cluster(key, part):
    key = jax.random.fold_in(key, 23)
    keys = jax.random.split(key, 2)
    ranking = jax.random.permutation(keys[0], ROWS).astype(jnp.int32)
    common_labels = jax.random.randint(keys[1], (ROWS,), 0, CPG, dtype=jnp.int32)
    return jnp.where(ranking < LONE, CPG + ranking, common_labels).astype(jnp.int32)


def deal_out(stream_key, own, number, rows, amount, top, limit, lean):
    sequence = jax.random.permutation(stream_key, amount)
    packed, usual = load_shares(amount, rows * top, limit, lean, True), load_shares(amount, rows * top, limit, lean, False)
    places = jnp.arange(amount)

    def named(tallies, turn):
        used = int((tallies > 0).sum())
        fixed = max(1, used // 4)
        passed = fixed + (places - fixed + turn * (used - fixed)) % max(1, amount - fixed)
        return jnp.zeros((amount,), jnp.int32).at[sequence[jnp.where(places < fixed, places, passed)]].set(jnp.asarray(tallies, jnp.int32))

    tallies = jnp.where(number % 4 == 0, named(packed, number // 4), named(usual, number - number // 4 - 1))
    mixed = jax.random.permutation(jax.random.fold_in(own, 3), amount)
    source_of, sink = mixed[0:amount // 2 * 2:2], mixed[1:amount // 2 * 2:2]
    margin = jnp.minimum(tallies[source_of] - 1, limit - tallies[sink]) // 2
    margin = jnp.where((source_of == sequence[0]) | (sink == sequence[0]) | (tallies[sink] == 0), 0, jnp.maximum(margin, 0))
    passed = jax.random.randint(jax.random.fold_in(own, 4), (amount // 2,), 0, 1 << 20) % (margin + 1)
    tallies = tallies.at[source_of].add(-passed).at[sink].add(passed)
    items = jnp.searchsorted(jnp.cumsum(tallies), jnp.arange(rows * top), side="right").astype(jnp.int32)
    table = items.reshape(top, rows).T
    table = table[jax.random.permutation(jax.random.fold_in(own, 1), rows)]
    turn = jax.random.randint(jax.random.fold_in(own, 2), (rows, 1), 0, top)
    return jnp.take_along_axis(table, (jnp.arange(top)[None, :] + turn) % top, axis=1)


def load_shares(amount, total, reach, skew, full):
    weights = [(1 << 20) // math.isqrt(standing ** skew) + 1 for standing in range(1, amount + 1)]
    largest = reach if full else min(reach, max(-(-total // amount), total * weights[0] // sum(weights)))
    least = 1 if total - largest >= amount - 1 else 0
    given, rest = [largest] + [least] * (amount - 1), total - largest - least * (amount - 1)
    while rest > 0:
        candidates = [i for i in range(1, amount) if given[i] < largest] or [i for i in range(1, amount) if given[i] < reach]
        pool, budget = sum([weights[i] for i in candidates]), rest
        for i in candidates:
            addition = min(reach - given[i], max(1, budget * weights[i] // pool), rest)
            given[i] = given[i] + addition
            rest = rest - addition
    return np.array(given)


def setup_inputs(seed: int = 0) -> dict:
    key_list = jax.random.split(jax.random.key(seed), 4)
    embeddings = draw_embeddings(jax.random.fold_in(key_list[3], 71), 0)
    row_group_keys = jax.random.split(jax.random.fold_in(key_list[1], 1), ROWS // ROW_DEV)
    row_group_turns = jax.random.permutation(jax.random.fold_in(key_list[1], 3), ROWS // ROW_DEV)
    row_group = jax.vmap(lambda own, number: deal_out(jax.random.fold_in(key_list[1], 2), own, number, ROW_DEV, N_GROUP, 1, CAP, 1))(row_group_keys, row_group_turns).reshape((ROWS, 1))
    row_cluster = draw_row_cluster(jax.random.fold_in(key_list[3], 71), 0)
    return dict(embeddings=embeddings, row_group=row_group, row_cluster=row_cluster)


def reference(embeddings, row_group, row_cluster):
    feats = embeddings.astype(jnp.float32)
    squares = lax.optimization_barrier(jnp.sum(feats * feats, axis=1, keepdims=True)) + 1e-06
    units = (feats * lax.rsqrt(squares)).astype(jnp.bfloat16)
    dest = row_group[:, 0].astype(jnp.int32)
    order = jnp.argsort(dest, stable=True).astype(jnp.int32)
    onehot = (dest[:, None] == jnp.arange(N_GROUP, dtype=jnp.int32)[None, :]).astype(jnp.int32)
    counts = lax.optimization_barrier(jnp.sum(onehot, axis=0)).astype(jnp.int32)
    offsets = (jnp.cumsum(counts) - counts).astype(jnp.int32)
    gcap = CAP * N_SHARD * N_GROUP
    block = math.gcd(gcap, 512)
    sorted_units = jnp.pad(units[order], ((0, gcap), (0, 0)))
    sorted_labels = jnp.pad(row_cluster[order].astype(jnp.int32), (0, gcap), constant_values=-1)
    position = jnp.arange(gcap, dtype=jnp.int32)

    def per_group(index):
        start = offsets[index]
        group_units = lax.dynamic_slice_in_dim(sorted_units, start, gcap, 0)
        group_labels = lax.dynamic_slice_in_dim(sorted_labels, start, gcap, 0)
        group_labels = jnp.where(position < counts[index], group_labels, -1)

        def per_block(pieces):
            block_units, block_labels, block_pos = pieces
            scores = lax.dot_general(block_units, group_units, (((1,), (1,)), ((), ())), preferred_element_type=jnp.float32)
            same = (block_labels[:, None] == group_labels[None, :]) & (group_labels[None, :] >= 0)
            same = same & (block_pos[:, None] != position[None, :])
            masked = jnp.where(same, scores, jnp.float32(-2.0))
            return jnp.maximum(lax.optimization_barrier(jnp.max(masked, axis=1)), jnp.float32(-1.0))
        result = lax.map(per_block, (group_units.reshape(gcap // block, block, -1), group_labels.reshape(gcap // block, block), position.reshape(gcap // block, block)))
        return result.reshape(gcap)
    best = lax.map(per_group, jnp.arange(N_GROUP, dtype=jnp.int32))
    sorted_dest = dest[order]
    within = jnp.arange(ROWS, dtype=jnp.int32) - offsets[sorted_dest]
    values = best[sorted_dest, within]
    return jnp.zeros((ROWS,), jnp.float32).at[order].set(values)
```

```python
import jax
import jax.numpy as jnp
from jax import lax
from jax.experimental import pallas as pl
from jax.experimental.pallas import tpu as pltpu
from jax.sharding import PartitionSpec as P

LANES = 128
TAIL = 16
LOW = -2.0
VMEM_LIMIT = 48 * 1024 * 1024


def ring_order(size):
    if size % 2:
        return list(range(size))
    half = size // 2
    chips = [i ^ (i >> 1) for i in range(half)]
    if sorted(chips) != list(range(half)):
        chips = list(range(half))
    return [2 * chip + core for core in range(2) for chip in chips]


def offset_cover(size):
    offsets = list(dict.fromkeys([0, 1 % size, (size - 1) % size, size // 2]))

    def missing(chosen):
        have = {(a - b) % size for a in chosen for b in chosen}
        return [d for d in range(size) if d not in have]

    while missing(offsets):
        offsets.append(min(range(size), key=lambda x: len(missing(offsets + [x]))))
    pairs = []
    for diff in range(1, size // 2 + 1):
        found = [
            (a, b)
            for b in [1 % size] + offsets
            for a in offsets
            if (a - b) % size in (diff, size - diff)
        ]
        if 2 * diff == size:
            found = [(a, b) for a, b in found if b == 0] + found
        a, b = found[0]
        pairs.append((a, b, b != 0 or 2 * diff != size))
    return offsets, pairs


def column_of(row):
    size = row.shape[1]
    return jnp.transpose(jnp.broadcast_to(row, (size, size)))


def sort_kernel(axis, emb_ref, dest_ref, label_ref, *out_refs):
    *block_refs, place_ref = out_refs
    rows, width = emb_ref.shape
    groups = len(block_refs)
    capacity = (block_refs[0].shape[0] - TAIL) * LANES // width
    slots = groups * capacity
    chunks = width // LANES
    rel = dest_ref[...] ^ lax.axis_index(axis)
    lines = max(8, groups)
    onehot = lax.broadcasted_iota(jnp.int32, (lines, rows), 0) == rel
    before = lax.broadcasted_iota(jnp.int32, (rows, rows), 0) < lax.broadcasted_iota(
        jnp.int32, (rows, rows), 1
    )
    ranks = jnp.dot(
        jnp.where(onehot, 1.0, 0.0).astype(jnp.bfloat16),
        jnp.where(before, 1.0, 0.0).astype(jnp.bfloat16),
        preferred_element_type=jnp.float32,
    )
    rank = jnp.sum(jnp.where(onehot, ranks, 0.0), axis=0, keepdims=True)
    place = rel * capacity + rank.astype(jnp.int32)
    place_ref[...] = place
    move = jnp.where(
        lax.broadcasted_iota(jnp.int32, (slots, rows), 0) == place, 1.0, 0.0
    ).astype(jnp.bfloat16)
    feats = emb_ref[...].astype(jnp.float32)
    squares = jnp.sum(feats * feats, axis=1, keepdims=True) + 1e-06
    units = (feats * lax.rsqrt(squares)).astype(jnp.bfloat16)
    labels = jnp.broadcast_to(label_ref[...] + 1, (TAIL, rows)).astype(jnp.bfloat16)
    sorted_labels = (
        lax.dot_general(
            labels, move, (((1,), (1,)), ((), ())), preferred_element_type=jnp.float32
        )
        - 1.0
    ).astype(jnp.bfloat16)
    for k, block_ref in enumerate(block_refs):
        part = slice(k * capacity, (k + 1) * capacity)
        block = jnp.dot(move[part], units, preferred_element_type=jnp.float32).astype(jnp.bfloat16)
        for c in range(chunks):
            block_ref[pl.ds(c * capacity, capacity), :] = block[:, c * LANES : (c + 1) * LANES]
        block_ref[pl.ds(chunks * capacity, TAIL), :] = sorted_labels[:, part]


def score_kernel(offsets, pairs, groups, *refs):
    roles = len(offsets)
    blocks = [refs[r * groups : (r + 1) * groups] for r in range(roles)]
    out_refs = refs[roles * groups : roles * (groups + 1)]
    flat_ref, row_ref, column_ref = refs[roles * (groups + 1) :]
    height = blocks[0][0].shape[0] - TAIL
    capacity = LANES
    chunks = height // capacity
    slots = groups * capacity
    lane_labels = []
    for r in range(roles):
        for k in range(groups):
            for c in range(chunks):
                flat_ref[r, pl.ds(k * capacity, capacity), pl.ds(c * LANES, LANES)] = blocks[r][k][
                    pl.ds(c * capacity, capacity), :
                ]
        lane_labels.append(
            [b[pl.ds(height, TAIL), :][0:1].astype(jnp.float32) for b in blocks[r]]
        )
    low = jnp.float32(LOW)
    row_ref[...] = jnp.full(row_ref.shape, low)
    column_ref[...] = jnp.full(column_ref.shape, low)
    plan = [(0, 0, False)]
    plan += [(offsets.index(a), offsets.index(b), both) for a, b, both in pairs]
    for left, right, want_rows in plan:
        column_labels = jnp.concatenate(lane_labels[right], axis=1)
        for k in range(groups):
            rows = pl.ds(k * capacity, capacity)
            scores = lax.dot_general(
                flat_ref[left, rows, :],
                flat_ref[right],
                (((1,), (1,)), ((), ())),
                preferred_element_type=jnp.float32,
            )
            row_labels = jnp.concatenate([column_of(lane_labels[left][k])] * groups, axis=1)
            same = row_labels == column_labels
            if left == right:
                same = same & (
                    lax.broadcasted_iota(jnp.int32, (capacity, slots), 0) + k * capacity
                    != lax.broadcasted_iota(jnp.int32, (capacity, slots), 1)
                )
            scores = jnp.where(same, scores, low)
            if want_rows:
                best = scores[:, :LANES]
                for c in range(1, groups):
                    best = jnp.maximum(best, scores[:, c * LANES : (c + 1) * LANES])
                row_ref[left, rows, :] = jnp.maximum(row_ref[left, rows, :], best)
            best = jnp.max(scores.reshape(capacity // 8, 8, slots), axis=0)
            column_ref[right] = jnp.maximum(column_ref[right], best)
    for r in range(roles):
        best = jnp.max(column_ref[r], axis=0, keepdims=True)
        turned = jnp.concatenate(
            [
                jnp.max(
                    jnp.transpose(row_ref[r, pl.ds(k * capacity, capacity), :]),
                    axis=0,
                    keepdims=True,
                )
                for k in range(groups)
            ],
            axis=1,
        )
        out_refs[r][...] = jnp.maximum(best, turned)


def merge_kernel(roles, *refs):
    best = refs[0][...]
    for r in range(1, roles):
        best = jnp.maximum(best, refs[r][...])
    best = jnp.maximum(best, jnp.float32(-1.0))
    for k, out_ref in enumerate(refs[roles:]):
        out_ref[...] = best[:, k * LANES : (k + 1) * LANES]


def place_kernel(groups, *refs):
    place = refs[groups][...]
    rows = place.shape[1]
    best = jnp.full((1, rows), jnp.float32(LOW))
    for k in range(groups):
        values = jnp.concatenate([column_of(refs[k][...])] * (rows // LANES), axis=1)
        here = lax.broadcasted_iota(jnp.int32, (LANES, rows), 0) + k * LANES == place
        best = jnp.maximum(
            best, jnp.max(jnp.where(here, values, jnp.float32(LOW)), axis=0, keepdims=True)
        )
    refs[groups + 1][...] = best


def in_vmem(count):
    return [pl.BlockSpec(memory_space=pltpu.VMEM)] * count


def call(kernel, out_shape, scratch, args, flops, bytes_accessed):
    return pl.pallas_call(
        kernel,
        out_shape=out_shape,
        in_specs=in_vmem(len(args)),
        out_specs=in_vmem(len(out_shape)),
        scratch_shapes=scratch,
        compiler_params=pltpu.CompilerParams(vmem_limit_bytes=VMEM_LIMIT),
        cost_estimate=pl.CostEstimate(
            flops=flops, bytes_accessed=bytes_accessed, transcendentals=0
        ),
    )(*args)


def per_device(embeddings, row_group, row_cluster):
    rows, width = embeddings.shape
    groups = lax.axis_size("group")
    shards = lax.axis_size("shard")
    capacity = rows // 4
    slots = groups * capacity
    ring = ring_order(shards)
    offsets, pairs = offset_cover(shards)
    roles = len(offsets)
    height = width * capacity // LANES + TAIL

    def from_offset(x, offset):
        perm = [(ring[(e + offset) % shards], ring[e]) for e in range(shards)]
        return lax.ppermute(x, "shard", perm)

    def across(x, k):
        return lax.ppermute(x, "group", [(z, z ^ k) for z in range(groups)])

    *send, place = call(
        lambda *refs: sort_kernel("group", *refs),
        [jax.ShapeDtypeStruct((height, LANES), jnp.bfloat16)] * groups
        + [jax.ShapeDtypeStruct((1, rows), jnp.int32)],
        [],
        (embeddings, row_group.reshape(1, rows), row_cluster.reshape(1, rows)),
        2 * rows * slots * width,
        4 * rows * width,
    )
    own = [send[0]] + [across(send[k], k) for k in range(1, groups)]
    held = [own] + [[None] * groups for _ in offsets[1:]]
    for k in range(groups):
        for r in range(1, roles):
            held[r][k] = from_offset(own[k], offsets[r])
    partial = call(
        lambda *refs: score_kernel(offsets, pairs, groups, *refs),
        [jax.ShapeDtypeStruct((1, slots), jnp.float32)] * roles,
        [
            pltpu.VMEM((roles, slots, width), jnp.bfloat16),
            pltpu.VMEM((roles, slots, LANES), jnp.float32),
            pltpu.VMEM((roles, 8, slots), jnp.float32),
        ],
        [block for role in held for block in role],
        2 * slots * slots * width * (len(pairs) + 1),
        2 * roles * slots * width,
    )
    others = [from_offset(partial[r], -offsets[r]) for r in range(1, roles)]
    best = call(
        lambda *refs: merge_kernel(roles, *refs),
        [jax.ShapeDtypeStruct((1, capacity), jnp.float32)] * groups,
        [],
        [partial[0]] + others,
        roles * slots,
        4 * roles * slots,
    )
    back = [best[0]] + [across(best[k], k) for k in range(1, groups)]
    (result,) = call(
        lambda *refs: place_kernel(groups, *refs),
        [jax.ShapeDtypeStruct((1, rows), jnp.float32)],
        [],
        back + [place],
        rows * slots,
        4 * slots,
    )
    return result.reshape(rows)


def solution(mesh):
    placed = (P(("shard", "group"), None), P(("shard", "group"), None), P(("shard", "group")))
    return jax.shard_map(
        per_device, mesh=mesh, in_specs=placed, out_specs=P(("shard", "group")), check_vma=False
    )
```

```python
import jax
import jax.numpy as jnp
from jax import lax
from jax.experimental import pallas as pl
from jax.experimental.pallas import tpu as pltpu
from jax.sharding import PartitionSpec as P

LANES = 128
TAIL = 16
LOW = -2.0
VMEM_LIMIT = 48 * 1024 * 1024


def ring_order(size):
    if size % 2:
        return list(range(size))
    half = size // 2
    chips = [i ^ (i >> 1) for i in range(half)]
    if sorted(chips) != list(range(half)):
        chips = list(range(half))
    return [2 * chip + core for core in range(2) for chip in chips]


def offset_cover(size):
    offsets = list(dict.fromkeys([0, 1 % size, (size - 1) % size, size // 2]))

    def missing(chosen):
        have = {(a - b) % size for a in chosen for b in chosen}
        return [d for d in range(size) if d not in have]

    while missing(offsets):
        offsets.append(min(range(size), key=lambda x: len(missing(offsets + [x]))))
    pairs = []
    for diff in range(1, size // 2 + 1):
        found = [
            (a, b)
            for b in [1 % size] + offsets
            for a in offsets
            if (a - b) % size in (diff, size - diff)
        ]
        if 2 * diff == size:
            found = [(a, b) for a, b in found if b == 0] + found
        a, b = found[0]
        pairs.append((a, b, b != 0 or 2 * diff != size))
    return offsets, pairs


def column_of(row):
    size = row.shape[1]
    return jnp.transpose(jnp.broadcast_to(row, (size, size)))


def sort_kernel(axis, emb_ref, dest_ref, label_ref, *out_refs):
    *block_refs, place_ref = out_refs
    rows, width = emb_ref.shape
    groups = len(block_refs)
    capacity = (block_refs[0].shape[0] - TAIL) * LANES // width
    slots = groups * capacity
    chunks = width // LANES
    rel = dest_ref[...] ^ lax.axis_index(axis)
    lines = max(8, groups)
    onehot = lax.broadcasted_iota(jnp.int32, (lines, rows), 0) == rel
    before = lax.broadcasted_iota(jnp.int32, (rows, rows), 0) < lax.broadcasted_iota(
        jnp.int32, (rows, rows), 1
    )
    ranks = jnp.dot(
        jnp.where(onehot, 1.0, 0.0).astype(jnp.bfloat16),
        jnp.where(before, 1.0, 0.0).astype(jnp.bfloat16),
        preferred_element_type=jnp.float32,
    )
    rank = jnp.sum(jnp.where(onehot, ranks, 0.0), axis=0, keepdims=True)
    place = rel * capacity + rank.astype(jnp.int32)
    place_ref[...] = place
    move = jnp.where(
        lax.broadcasted_iota(jnp.int32, (slots, rows), 0) == place, 1.0, 0.0
    ).astype(jnp.bfloat16)
    feats = emb_ref[...].astype(jnp.float32)
    squares = jnp.sum(feats * feats, axis=1, keepdims=True) + 1e-06
    units = (feats * lax.rsqrt(squares)).astype(jnp.bfloat16)
    labels = jnp.broadcast_to(label_ref[...] + 1, (TAIL, rows)).astype(jnp.bfloat16)
    sorted_labels = (
        lax.dot_general(
            labels, move, (((1,), (1,)), ((), ())), preferred_element_type=jnp.float32
        )
        - 1.0
    ).astype(jnp.bfloat16)
    for k, block_ref in enumerate(block_refs):
        part = slice(k * capacity, (k + 1) * capacity)
        block = jnp.dot(move[part], units, preferred_element_type=jnp.float32).astype(jnp.bfloat16)
        for c in range(chunks):
            block_ref[pl.ds(c * capacity, capacity), :] = block[:, c * LANES : (c + 1) * LANES]
        block_ref[pl.ds(chunks * capacity, TAIL), :] = sorted_labels[:, part]


def stack_kernel(*refs):
    for k, ref in enumerate(refs[:-1]):
        refs[-1][k] = ref[...]


def score_kernel(offsets, pairs, groups, *refs):
    roles = len(offsets)
    *refs, flat_ref, row_ref, column_ref = refs
    refs, out_refs = refs[:-roles], refs[-roles:]
    blocks = []
    while refs:
        if len(refs[0].shape) == 3:
            blocks.append([refs[0].at[k] for k in range(groups)])
            refs = refs[1:]
        else:
            blocks.append(refs[:groups])
            refs = refs[groups:]
    height = blocks[0][0].shape[0] - TAIL
    capacity = LANES
    chunks = height // capacity
    slots = groups * capacity
    lane_labels = []
    for r in range(roles):
        for k in range(groups):
            for c in range(chunks):
                flat_ref[r, pl.ds(k * capacity, capacity), pl.ds(c * LANES, LANES)] = blocks[r][k][
                    pl.ds(c * capacity, capacity), :
                ]
        lane_labels.append(
            [b[pl.ds(height, TAIL), :][0:1].astype(jnp.float32) for b in blocks[r]]
        )
    low = jnp.float32(LOW)
    row_ref[...] = jnp.full(row_ref.shape, low)
    column_ref[...] = jnp.full(column_ref.shape, low)
    plan = [(0, 0, False)]
    plan += [(offsets.index(a), offsets.index(b), both) for a, b, both in pairs]
    for left, right, want_rows in plan:
        column_labels = jnp.concatenate(lane_labels[right], axis=1)
        for k in range(groups):
            rows = pl.ds(k * capacity, capacity)
            scores = lax.dot_general(
                flat_ref[left, rows, :],
                flat_ref[right],
                (((1,), (1,)), ((), ())),
                preferred_element_type=jnp.float32,
            )
            row_labels = jnp.concatenate([column_of(lane_labels[left][k])] * groups, axis=1)
            same = row_labels == column_labels
            if left == right:
                same = same & (
                    lax.broadcasted_iota(jnp.int32, (capacity, slots), 0) + k * capacity
                    != lax.broadcasted_iota(jnp.int32, (capacity, slots), 1)
                )
            scores = jnp.where(same, scores, low)
            if want_rows:
                best = scores[:, :LANES]
                for c in range(1, groups):
                    best = jnp.maximum(best, scores[:, c * LANES : (c + 1) * LANES])
                row_ref[left, rows, :] = jnp.maximum(row_ref[left, rows, :], best)
            best = jnp.max(scores.reshape(capacity // 8, 8, slots), axis=0)
            column_ref[right] = jnp.maximum(column_ref[right], best)
    for r in range(roles):
        best = jnp.max(column_ref[r], axis=0, keepdims=True)
        turned = jnp.concatenate(
            [
                jnp.max(
                    jnp.transpose(row_ref[r, pl.ds(k * capacity, capacity), :]),
                    axis=0,
                    keepdims=True,
                )
                for k in range(groups)
            ],
            axis=1,
        )
        out_refs[r][...] = jnp.maximum(best, turned)


def merge_kernel(roles, *refs):
    best = refs[0][...]
    for r in range(1, roles):
        best = jnp.maximum(best, refs[r][...])
    best = jnp.maximum(best, jnp.float32(-1.0))
    for k, out_ref in enumerate(refs[roles:]):
        out_ref[...] = best[:, k * LANES : (k + 1) * LANES]


def place_kernel(groups, *refs):
    place = refs[groups][...]
    rows = place.shape[1]
    best = jnp.full((1, rows), jnp.float32(LOW))
    for k in range(groups):
        values = jnp.concatenate([column_of(refs[k][...])] * (rows // LANES), axis=1)
        here = lax.broadcasted_iota(jnp.int32, (LANES, rows), 0) + k * LANES == place
        best = jnp.maximum(
            best, jnp.max(jnp.where(here, values, jnp.float32(LOW)), axis=0, keepdims=True)
        )
    refs[groups + 1][...] = best


def in_vmem(count):
    return [pl.BlockSpec(memory_space=pltpu.VMEM)] * count


def call(kernel, out_shape, scratch, args, flops, bytes_accessed):
    return pl.pallas_call(
        kernel,
        out_shape=out_shape,
        in_specs=in_vmem(len(args)),
        out_specs=in_vmem(len(out_shape)),
        scratch_shapes=scratch,
        compiler_params=pltpu.CompilerParams(vmem_limit_bytes=VMEM_LIMIT),
        cost_estimate=pl.CostEstimate(
            flops=flops, bytes_accessed=bytes_accessed, transcendentals=0
        ),
    )(*args)


def per_device(embeddings, row_group, row_cluster):
    rows, width = embeddings.shape
    groups = lax.axis_size("group")
    shards = lax.axis_size("shard")
    capacity = rows // 4
    slots = groups * capacity
    ring = ring_order(shards)
    offsets, pairs = offset_cover(shards)
    roles = len(offsets)
    height = width * capacity // LANES + TAIL

    def from_offset(x, offset):
        perm = [(ring[(e + offset) % shards], ring[e]) for e in range(shards)]
        return lax.ppermute(x, "shard", perm)

    def across(x, k):
        return lax.ppermute(x, "group", [(z, z ^ k) for z in range(groups)])

    *send, place = call(
        lambda *refs: sort_kernel("group", *refs),
        [jax.ShapeDtypeStruct((height, LANES), jnp.bfloat16)] * groups
        + [jax.ShapeDtypeStruct((1, rows), jnp.int32)],
        [],
        (embeddings, row_group.reshape(1, rows), row_cluster.reshape(1, rows)),
        2 * rows * slots * width,
        4 * rows * width,
    )
    def after(x, *earlier):
        return lax.optimization_barrier((x, *earlier))[0]

    own = [send[0]] + [None] * (groups - 1)
    held = [own] + [[None] * groups for _ in offsets[1:]]
    near = [r for r in range(1, roles) if 2 * offsets[r] != shards]
    for r in near:
        held[r][0] = from_offset(own[0], offsets[r])
    for k in range(1, groups):
        own[k] = across(after(send[k], held[near[-1]][0]) if k > 2 and near else send[k], k)
    for k in range(1, groups):
        for r in near:
            held[r][k] = from_offset(after(own[k], held[r][k - 1]), offsets[r])
    for r in range(1, roles):
        if r not in near:
            (stack,) = call(
                stack_kernel,
                [jax.ShapeDtypeStruct((groups, height, LANES), jnp.bfloat16)],
                [],
                [after(x, *[held[q][groups - 2] for q in near]) for x in own],
                0,
                4 * groups * height * LANES,
            )
            held[r] = [from_offset(stack, offsets[r])]
    partial = call(
        lambda *refs: score_kernel(offsets, pairs, groups, *refs),
        [jax.ShapeDtypeStruct((1, slots), jnp.float32)] * roles,
        [
            pltpu.VMEM((roles, slots, width), jnp.bfloat16),
            pltpu.VMEM((roles, slots, LANES), jnp.float32),
            pltpu.VMEM((roles, 8, slots), jnp.float32),
        ],
        [block for role in held for block in role],
        2 * slots * slots * width * (len(pairs) + 1),
        2 * roles * slots * width,
    )
    others = [from_offset(partial[r], -offsets[r]) for r in range(1, roles)]
    best = call(
        lambda *refs: merge_kernel(roles, *refs),
        [jax.ShapeDtypeStruct((1, capacity), jnp.float32)] * groups,
        [],
        [partial[0]] + others,
        roles * slots,
        4 * roles * slots,
    )
    back = [best[0]] + [across(best[k], k) for k in range(1, groups)]
    (result,) = call(
        lambda *refs: place_kernel(groups, *refs),
        [jax.ShapeDtypeStruct((1, rows), jnp.float32)],
        [],
        back + [place],
        rows * slots,
        4 * slots,
    )
    return result.reshape(rows)


def solution(mesh):
    placed = (P(("shard", "group"), None), P(("shard", "group"), None), P(("shard", "group")))
    return jax.shard_map(
        per_device, mesh=mesh, in_specs=placed, out_specs=P(("shard", "group")), check_vma=False
    )
```

```python
import jax
import jax.numpy as jnp
from jax import lax
from jax.experimental import pallas as pl
from jax.experimental.pallas import tpu as pltpu
from jax.sharding import PartitionSpec as P

LANES = 128
TAIL = 16
LOW = -2.0
MIB = 1024 * 1024
WAIT = 2 * 10**10


def ring_order(size):
    if size % 2:
        return list(range(size))
    half = size // 2
    chips = [i ^ (i >> 1) for i in range(half)]
    if sorted(chips) != list(range(half)):
        chips = list(range(half))
    return [2 * chip + core for core in range(2) for chip in chips]


def offset_cover(size):
    offsets = list(dict.fromkeys([0, 1 % size, (size - 1) % size, size // 2]))

    def missing(chosen):
        have = {(a - b) % size for a in chosen for b in chosen}
        return [d for d in range(size) if d not in have]

    while missing(offsets):
        offsets.append(min(range(size), key=lambda x: len(missing(offsets + [x]))))
    pairs = []
    for diff in range(1, size // 2 + 1):
        found = [
            (a, b)
            for b in [1 % size] + offsets
            for a in offsets
            if (a - b) % size in (diff, size - diff)
        ]
        if 2 * diff == size:
            found = [(a, b) for a, b in found if b == 0] + found
        a, b = found[0]
        pairs.append((a, b, b != 0 or 2 * diff != size))
    return offsets, pairs


def column_of(row):
    size = row.shape[1]
    return jnp.transpose(jnp.broadcast_to(row, (size, size)))


def sort_kernel(axis, far_ref, code_ref, *refs):
    *block_refs, place_ref, near_ref, unit_ref, sems = refs
    rows, width = near_ref.shape
    groups = len(block_refs)
    capacity = (block_refs[0].shape[0] - TAIL) * LANES // width
    slots = groups * capacity
    chunks = width // LANES
    parts = sems.shape[0]
    size = rows // parts
    copies = [
        pltpu.make_async_copy(
            far_ref.at[pl.ds(i * size, size), :], near_ref.at[pl.ds(i * size, size), :], sems.at[i]
        )
        for i in range(parts)
    ]
    for copy in copies:
        copy.start()
    code = code_ref[...]
    rel = (code & (groups - 1)) ^ lax.axis_index(axis)
    label = code >> (groups.bit_length() - 1)
    lines = max(8, groups)
    onehot = lax.broadcasted_iota(jnp.int32, (lines, rows), 0) == rel
    before = lax.broadcasted_iota(jnp.int32, (rows, rows), 0) < lax.broadcasted_iota(
        jnp.int32, (rows, rows), 1
    )
    ranks = jnp.dot(
        jnp.where(onehot, 1.0, 0.0).astype(jnp.bfloat16),
        jnp.where(before, 1.0, 0.0).astype(jnp.bfloat16),
        preferred_element_type=jnp.float32,
    )
    rank = jnp.sum(jnp.where(onehot, ranks, 0.0), axis=0, keepdims=True)
    place = rel * capacity + rank.astype(jnp.int32)
    place_ref[...] = place
    move = jnp.where(
        lax.broadcasted_iota(jnp.int32, (slots, rows), 0) == place, 1.0, 0.0
    ).astype(jnp.bfloat16)
    labels = jnp.broadcast_to(label + 1, (TAIL, rows)).astype(jnp.bfloat16)
    sorted_labels = (
        lax.dot_general(
            labels, move, (((1,), (1,)), ((), ())), preferred_element_type=jnp.float32
        )
        - 1.0
    ).astype(jnp.bfloat16)
    for i, copy in enumerate(copies):
        copy.wait()
        feats = near_ref[pl.ds(i * size, size), :].astype(jnp.float32)
        squares = jnp.sum(feats * feats, axis=1, keepdims=True) + 1e-06
        unit_ref[pl.ds(i * size, size), :] = (feats * lax.rsqrt(squares)).astype(jnp.bfloat16)
    for k, block_ref in enumerate(block_refs):
        part = slice(k * capacity, (k + 1) * capacity)
        block = jnp.dot(
            move[part], unit_ref[...], preferred_element_type=jnp.float32
        ).astype(jnp.bfloat16)
        for c in range(chunks):
            block_ref[pl.ds(c * capacity, capacity), :] = block[:, c * LANES : (c + 1) * LANES]
        block_ref[pl.ds(chunks * capacity, TAIL), :] = sorted_labels[:, part]


def stack_kernel(*refs):
    for k, ref in enumerate(refs[:-1]):
        refs[-1][k] = ref[...]


def score_kernel(sources, tasks, groups, roles, first, last, *refs):
    *refs, flat_ref, side_ref = refs
    outs = 2 + (roles if last else 0)
    inputs, (row_ref, column_ref, *out_refs) = refs[:-outs], refs[-outs:]
    capacity = LANES
    slots = groups * capacity
    low = jnp.float32(LOW)
    if first:
        row_ref[...] = jnp.full(row_ref.shape, low)
        column_ref[...] = jnp.full(column_ref.shape, low)
    else:
        *inputs, old_rows, old_columns = inputs
        row_ref[...] = old_rows[...]
        column_ref[...] = old_columns[...]
    tops = {}
    for (role, k), (index, part) in sources.items():
        ref = inputs[index] if part is None else inputs[index].at[part]
        height = ref.shape[0] - TAIL
        rows = pl.ds(k * capacity, capacity)
        for c in range(height // capacity):
            flat_ref[role, rows, pl.ds(c * LANES, LANES)] = ref[pl.ds(c * capacity, capacity), :]
        tops[role, k] = ref[pl.ds(height, TAIL), :][0:1].astype(jnp.float32)
    for role, k in sorted({(left, k) for left, ks, _, _, _ in tasks for k in ks}):
        side_ref[role, pl.ds(k * capacity, capacity), :] = column_of(tops[role, k])
    for left, left_ks, right, right_ks, want_rows in tasks:
        start, count = left_ks[0] * capacity, len(left_ks) * capacity
        rows = pl.ds(start, count)
        for i in range(0, len(right_ks), 2):
            some = right_ks[i : i + 2]
            width = len(some) * capacity
            columns = pl.ds(some[0] * capacity, width)
            scores = lax.dot_general(
                flat_ref[left, rows, :],
                flat_ref[right, columns, :],
                (((1,), (1,)), ((), ())),
                preferred_element_type=jnp.float32,
            )
            top = jnp.concatenate([tops[right, k] for k in some], axis=1)
            same = jnp.concatenate([side_ref[left, rows, :]] * len(some), axis=1) == top
            if left == right:
                same = same & (
                    lax.broadcasted_iota(jnp.int32, (count, width), 0) + start
                    != lax.broadcasted_iota(jnp.int32, (count, width), 1) + some[0] * capacity
                )
            scores = jnp.where(same, scores, low)
            if want_rows:
                best = row_ref[left, rows, :]
                for c in range(len(some)):
                    best = jnp.maximum(best, scores[:, c * LANES : (c + 1) * LANES])
                row_ref[left, rows, :] = best
            best = jnp.max(scores.reshape(count // 8, 8, width), axis=0)
            column_ref[right, :, columns] = jnp.maximum(column_ref[right, :, columns], best)
    for role, out_ref in enumerate(out_refs):
        best = jnp.max(column_ref[role], axis=0, keepdims=True)
        turned = [
            jnp.max(
                jnp.transpose(row_ref[role, pl.ds(k * capacity, capacity), :]),
                axis=0,
                keepdims=True,
            )
            for k in range(groups)
        ]
        out_ref[...] = jnp.maximum(best, jnp.concatenate(turned, axis=1))


def merge_kernel(roles, *refs):
    best = refs[0][...]
    for r in range(1, roles):
        best = jnp.maximum(best, refs[r][...])
    best = jnp.maximum(best, jnp.float32(-1.0))
    for k, out_ref in enumerate(refs[roles:]):
        out_ref[...] = best[:, k * LANES : (k + 1) * LANES]


def place_kernel(groups, *refs):
    place = refs[groups][...]
    rows = place.shape[1]
    best = jnp.full((1, rows), jnp.float32(LOW))
    for k in range(groups):
        values = jnp.concatenate([column_of(refs[k][...])] * (rows // LANES), axis=1)
        here = lax.broadcasted_iota(jnp.int32, (LANES, rows), 0) + k * LANES == place
        best = jnp.maximum(
            best, jnp.max(jnp.where(here, values, jnp.float32(LOW)), axis=0, keepdims=True)
        )
    refs[groups + 1][...] = best


def in_vmem(count):
    return [pl.BlockSpec(memory_space=pltpu.VMEM)] * count


def call(
    kernel, out_shape, scratch, args, flops, bytes_accessed, in_specs=None, limit=48 * MIB, aliases=None
):
    return pl.pallas_call(
        kernel,
        out_shape=out_shape,
        in_specs=in_specs or in_vmem(len(args)),
        out_specs=in_vmem(len(out_shape)),
        scratch_shapes=scratch,
        input_output_aliases=aliases or {},
        compiler_params=pltpu.CompilerParams(vmem_limit_bytes=limit),
        cost_estimate=pl.CostEstimate(
            flops=flops, bytes_accessed=bytes_accessed, transcendentals=0
        ),
    )(*args)


def after(x, *earlier):
    return lax.optimization_barrier((x, *earlier))[0]


def stack(parts, wait):
    return call(
        stack_kernel,
        [jax.ShapeDtypeStruct((len(parts), *parts[0].shape), parts[0].dtype)],
        [],
        parts,
        wait,
        4 * len(parts) * parts[0].size,
    )[0]


def score(held, tasks, acc, last, slots, width):
    roles, groups = len(held), len(held[0])
    used = sorted(
        {(left, k) for left, ks, _, _, _ in tasks for k in ks}
        | {(right, k) for _, _, right, ks, _ in tasks for k in ks}
    )
    arrays, sources = [], {}
    for role, k in used:
        array, part = held[role][k]
        index = next((i for i, x in enumerate(arrays) if x is array), len(arrays))
        if index == len(arrays):
            arrays.append(array)
        sources[role, k] = (index, part)
    states = [
        jax.ShapeDtypeStruct((roles, slots, LANES), jnp.float32),
        jax.ShapeDtypeStruct((roles, 8, slots), jnp.float32),
    ]
    ends = [jax.ShapeDtypeStruct((1, slots), jnp.float32)] * roles if last else []
    tiles = sum(len(task[1]) * len(task[3]) for task in tasks)
    count = len(arrays)
    got = call(
        lambda *refs: score_kernel(sources, tasks, groups, roles, not acc, last, *refs),
        states + ends,
        [
            pltpu.VMEM((roles, slots, width), jnp.bfloat16),
            pltpu.VMEM((roles, slots, LANES), jnp.float32),
        ],
        arrays + list(acc),
        2 * tiles * LANES * LANES * width,
        2 * len(used) * LANES * width,
        aliases={count: 0, count + 1: 1} if acc else {},
    )
    return got[:2], got[2:]


def per_device(embeddings, row_group, row_cluster):
    rows, width = embeddings.shape
    groups = lax.axis_size("group")
    shards = lax.axis_size("shard")
    capacity = rows // 4
    slots = groups * capacity
    ring = ring_order(shards)
    offsets, pairs = offset_cover(shards)
    roles = len(offsets)
    height = width * capacity // LANES + TAIL

    def from_offset(x, offset):
        perm = [(ring[(e + offset) % shards], ring[e]) for e in range(shards)]
        return lax.ppermute(x, "shard", perm)

    def across(x, k):
        return lax.ppermute(x, "group", [(z, z ^ k) for z in range(groups)])

    code = row_cluster * groups + row_group[:, 0]
    *send, place = call(
        lambda *refs: sort_kernel("group", *refs),
        [jax.ShapeDtypeStruct((height, LANES), jnp.bfloat16)] * groups
        + [jax.ShapeDtypeStruct((1, rows), jnp.int32)],
        [
            pltpu.VMEM((rows, width), embeddings.dtype),
            pltpu.VMEM((rows, width), jnp.bfloat16),
            pltpu.SemaphoreType.DMA((4,)),
        ],
        (embeddings, code.reshape(1, rows)),
        2 * rows * slots * width,
        4 * rows * width,
        [pl.BlockSpec(memory_space=pltpu.HBM), pl.BlockSpec(memory_space=pltpu.VMEM)],
        53 * MIB,
    )

    early = list(range(min(2, groups)))
    late = list(range(len(early), groups))
    near = [r for r in range(1, roles) if 2 * offsets[r] != shards]
    far = [r for r in range(1, roles) if r not in near]
    own = [send[0]] + [across(send[k], k) for k in range(1, groups)]
    held = [[None] * groups for _ in offsets]
    packs = [stack([own[k] for k in ks], wait) for ks, wait in ((early, 0), (late, WAIT)) if ks]
    sent = {}
    for pack, ks in zip(packs, (early, late)):
        for r in near + far:
            if ks is late and r in near:
                pack_now = after(pack, sent[r])
            else:
                pack_now = pack
            sent[r] = from_offset(pack_now, offsets[r])
            for i, k in enumerate(ks):
                held[r][k] = (sent[r], i)
    held[0] = [(x, None) for x in own]

    everything = [(0, 0, False)]
    everything += [(offsets.index(a), offsets.index(b), both) for a, b, both in pairs]
    steps = [[], [], []]
    for left, right, both in everything:
        for left_ks in (early, late):
            for right_ks in (early, late):
                if left_ks and right_ks:
                    step = 0
                    if left_ks is late:
                        step = 1 if left == 0 else 2
                    if right_ks is late:
                        step = max(step, 1 if right == 0 else 2)
                    steps[step].append((left, left_ks, right, right_ks, both))
    steps = [tasks for tasks in steps if tasks]
    acc = []
    for i, tasks in enumerate(steps):
        acc, partial = score(held, tasks, acc, i == len(steps) - 1, slots, width)

    others = [from_offset(partial[r], -offsets[r]) for r in range(1, roles)]
    best = call(
        lambda *refs: merge_kernel(roles, *refs),
        [jax.ShapeDtypeStruct((1, capacity), jnp.float32)] * groups,
        [],
        [partial[0]] + others,
        roles * slots,
        4 * roles * slots,
    )
    back = [best[0]] + [across(best[k], k) for k in range(1, groups)]
    (result,) = call(
        lambda *refs: place_kernel(groups, *refs),
        [jax.ShapeDtypeStruct((1, rows), jnp.float32)],
        [],
        back + [place],
        rows * slots,
        4 * slots,
    )
    return result.reshape(rows)


def solution(mesh):
    placed = (P(("shard", "group"), None), P(("shard", "group"), None), P(("shard", "group")))
    return jax.shard_map(
        per_device, mesh=mesh, in_specs=placed, out_specs=P(("shard", "group")), check_vma=False
    )
```

```python
import jax
import jax.numpy as jnp
from jax import lax
from jax.experimental import pallas as pl
from jax.experimental.pallas import tpu as pltpu
from jax.sharding import PartitionSpec as P

LANES = 128
TAIL = 16
LOW = -2.0
MIB = 1024 * 1024
WAIT = 2 * 10**10


def ring_order(size):
    if size % 2:
        return list(range(size))
    half = size // 2
    chips = [i ^ (i >> 1) for i in range(half)]
    if sorted(chips) != list(range(half)):
        chips = list(range(half))
    return [2 * chip + core for core in range(2) for chip in chips]


def offset_cover(size):
    offsets = list(dict.fromkeys([0, size // 2, 1 % size, (size - 1) % size]))

    def missing(chosen):
        have = {(a - b) % size for a in chosen for b in chosen}
        return [d for d in range(size) if d not in have]

    while missing(offsets):
        offsets.append(min(range(size), key=lambda x: len(missing(offsets + [x]))))
    pairs = []
    for diff in range(1, size // 2 + 1):
        found = [
            (a, b)
            for b in [1 % size] + offsets
            for a in offsets
            if (a - b) % size in (diff, size - diff)
        ]
        if 2 * diff == size:
            found = [(a, b) for a, b in found if b == 0] + found
        a, b = found[0]
        pairs.append((a, b, b != 0 or 2 * diff != size))
    return offsets, pairs


def column_of(row):
    size = row.shape[1]
    return jnp.transpose(jnp.broadcast_to(row, (size, size)))


def sort_kernel(axis, far_ref, code_ref, *refs):
    *block_refs, place_ref, near_ref, unit_ref, sems = refs
    rows, width = near_ref.shape
    groups = len(block_refs)
    capacity = (block_refs[0].shape[0] - TAIL) * LANES // width
    slots = groups * capacity
    chunks = width // LANES
    parts = sems.shape[0]
    size = rows // parts
    copies = [
        pltpu.make_async_copy(
            far_ref.at[pl.ds(i * size, size), :], near_ref.at[pl.ds(i * size, size), :], sems.at[i]
        )
        for i in range(parts)
    ]
    for copy in copies:
        copy.start()
    code = code_ref[...]
    rel = (code & (groups - 1)) ^ lax.axis_index(axis)
    label = code >> (groups.bit_length() - 1)
    lines = max(8, groups)
    onehot = lax.broadcasted_iota(jnp.int32, (lines, rows), 0) == rel
    before = lax.broadcasted_iota(jnp.int32, (rows, rows), 0) < lax.broadcasted_iota(
        jnp.int32, (rows, rows), 1
    )
    ranks = jnp.dot(
        jnp.where(onehot, 1.0, 0.0).astype(jnp.bfloat16),
        jnp.where(before, 1.0, 0.0).astype(jnp.bfloat16),
        preferred_element_type=jnp.float32,
    )
    rank = jnp.sum(jnp.where(onehot, ranks, 0.0), axis=0, keepdims=True)
    place = rel * capacity + rank.astype(jnp.int32)
    place_ref[...] = place
    move = jnp.where(
        lax.broadcasted_iota(jnp.int32, (slots, rows), 0) == place, 1.0, 0.0
    ).astype(jnp.bfloat16)
    labels = jnp.broadcast_to(label + 1, (TAIL, rows)).astype(jnp.bfloat16)
    sorted_labels = (
        lax.dot_general(
            labels, move, (((1,), (1,)), ((), ())), preferred_element_type=jnp.float32
        )
        - 1.0
    ).astype(jnp.bfloat16)
    for i, copy in enumerate(copies):
        copy.wait()
        feats = near_ref[pl.ds(i * size, size), :].astype(jnp.float32)
        squares = jnp.sum(feats * feats, axis=1, keepdims=True) + 1e-06
        unit_ref[pl.ds(i * size, size), :] = (feats * lax.rsqrt(squares)).astype(jnp.bfloat16)
    for k, block_ref in enumerate(block_refs):
        part = slice(k * capacity, (k + 1) * capacity)
        block = jnp.dot(
            move[part], unit_ref[...], preferred_element_type=jnp.float32
        ).astype(jnp.bfloat16)
        for c in range(chunks):
            block_ref[pl.ds(c * capacity, capacity), :] = block[:, c * LANES : (c + 1) * LANES]
        block_ref[pl.ds(chunks * capacity, TAIL), :] = sorted_labels[:, part]


def stack_kernel(*refs):
    for k, ref in enumerate(refs[:-1]):
        refs[-1][k] = ref[...]


def score_kernel(sources, tasks, groups, roles, first, last, *refs):
    *refs, flat_ref, side_ref = refs
    outs = 2 + (roles if last else 0)
    inputs, (row_ref, column_ref, *out_refs) = refs[:-outs], refs[-outs:]
    capacity = LANES
    slots = groups * capacity
    low = jnp.float32(LOW)
    if first:
        row_ref[...] = jnp.full(row_ref.shape, low)
        column_ref[...] = jnp.full(column_ref.shape, low)
    else:
        *inputs, old_rows, old_columns = inputs
        row_ref[...] = old_rows[...]
        column_ref[...] = old_columns[...]
    tops = {}
    for (role, k), (index, part) in sources.items():
        ref = inputs[index] if part is None else inputs[index].at[part]
        height = ref.shape[0] - TAIL
        rows = pl.ds(k * capacity, capacity)
        for c in range(height // capacity):
            flat_ref[role, rows, pl.ds(c * LANES, LANES)] = ref[pl.ds(c * capacity, capacity), :]
        tops[role, k] = ref[pl.ds(height, TAIL), :][0:1].astype(jnp.float32)
    for role, k in sorted({(left, k) for left, ks, _, _, _ in tasks for k in ks}):
        side_ref[role, pl.ds(k * capacity, capacity), :] = column_of(tops[role, k])
    for left, left_ks, right, right_ks, want_rows in tasks:
        start, count = left_ks[0] * capacity, len(left_ks) * capacity
        rows = pl.ds(start, count)
        for i in range(0, len(right_ks), 2):
            some = right_ks[i : i + 2]
            width = len(some) * capacity
            columns = pl.ds(some[0] * capacity, width)
            scores = lax.dot_general(
                flat_ref[left, rows, :],
                flat_ref[right, columns, :],
                (((1,), (1,)), ((), ())),
                preferred_element_type=jnp.float32,
            )
            top = jnp.concatenate([tops[right, k] for k in some], axis=1)
            same = jnp.concatenate([side_ref[left, rows, :]] * len(some), axis=1) == top
            if left == right:
                same = same & (
                    lax.broadcasted_iota(jnp.int32, (count, width), 0) + start
                    != lax.broadcasted_iota(jnp.int32, (count, width), 1) + some[0] * capacity
                )
            scores = jnp.where(same, scores, low)
            if want_rows:
                best = row_ref[left, rows, :]
                for c in range(len(some)):
                    best = jnp.maximum(best, scores[:, c * LANES : (c + 1) * LANES])
                row_ref[left, rows, :] = best
            best = jnp.max(scores.reshape(count // 8, 8, width), axis=0)
            column_ref[right, :, columns] = jnp.maximum(column_ref[right, :, columns], best)
    for role, out_ref in enumerate(out_refs):
        best = jnp.max(column_ref[role], axis=0, keepdims=True)
        turned = [
            jnp.max(
                jnp.transpose(row_ref[role, pl.ds(k * capacity, capacity), :]),
                axis=0,
                keepdims=True,
            )
            for k in range(groups)
        ]
        out_ref[...] = jnp.maximum(best, jnp.concatenate(turned, axis=1))


def merge_kernel(roles, *refs):
    best = refs[0][...]
    for r in range(1, roles):
        best = jnp.maximum(best, refs[r][...])
    best = jnp.maximum(best, jnp.float32(-1.0))
    for k, out_ref in enumerate(refs[roles:]):
        out_ref[...] = best[:, k * LANES : (k + 1) * LANES]


def place_kernel(groups, *refs):
    place = refs[groups][...]
    rows = place.shape[1]
    best = jnp.full((1, rows), jnp.float32(LOW))
    for k in range(groups):
        values = jnp.concatenate([column_of(refs[groups - 1 - k][...])] * (rows // LANES), axis=1)
        here = lax.broadcasted_iota(jnp.int32, (LANES, rows), 0) + k * LANES == place
        best = jnp.maximum(
            best, jnp.max(jnp.where(here, values, jnp.float32(LOW)), axis=0, keepdims=True)
        )
    refs[groups + 1][...] = best


def in_vmem(count):
    return [pl.BlockSpec(memory_space=pltpu.VMEM)] * count


def call(
    kernel, out_shape, scratch, args, flops, bytes_accessed, in_specs=None, limit=48 * MIB, aliases=None
):
    return pl.pallas_call(
        kernel,
        out_shape=out_shape,
        in_specs=in_specs or in_vmem(len(args)),
        out_specs=in_vmem(len(out_shape)),
        scratch_shapes=scratch,
        input_output_aliases=aliases or {},
        compiler_params=pltpu.CompilerParams(vmem_limit_bytes=limit),
        cost_estimate=pl.CostEstimate(
            flops=flops, bytes_accessed=bytes_accessed, transcendentals=0
        ),
    )(*args)


def after(x, *earlier):
    return lax.optimization_barrier((x, *earlier))[0]


def stack(parts, wait):
    return call(
        stack_kernel,
        [jax.ShapeDtypeStruct((len(parts), *parts[0].shape), parts[0].dtype)],
        [],
        parts,
        wait,
        4 * len(parts) * parts[0].size,
    )[0]


def score(held, tasks, acc, last, slots, width):
    roles, groups = len(held), len(held[0])
    used = sorted(
        {(left, k) for left, ks, _, _, _ in tasks for k in ks}
        | {(right, k) for _, _, right, ks, _ in tasks for k in ks},
        key=lambda x: (x[0], -x[1]),
    )
    arrays, sources = [], {}
    for role, k in used:
        array, part = held[role][k]
        index = next((i for i, x in enumerate(arrays) if x is array), len(arrays))
        if index == len(arrays):
            arrays.append(array)
        sources[role, k] = (index, part)
    states = [
        jax.ShapeDtypeStruct((roles, slots, LANES), jnp.float32),
        jax.ShapeDtypeStruct((roles, 8, slots), jnp.float32),
    ]
    ends = [jax.ShapeDtypeStruct((1, slots), jnp.float32)] * roles if last else []
    tiles = sum(len(task[1]) * len(task[3]) for task in tasks)
    count = len(arrays)
    got = call(
        lambda *refs: score_kernel(sources, tasks, groups, roles, not acc, last, *refs),
        states + ends,
        [
            pltpu.VMEM((roles, slots, width), jnp.bfloat16),
            pltpu.VMEM((roles, slots, LANES), jnp.float32),
        ],
        arrays + list(acc),
        2 * tiles * LANES * LANES * width,
        2 * len(used) * LANES * width,
        aliases={count: 0, count + 1: 1} if acc else {},
    )
    return got[:2], got[2:]


def per_device(embeddings, row_group, row_cluster):
    rows, width = embeddings.shape
    groups = lax.axis_size("group")
    shards = lax.axis_size("shard")
    capacity = rows // 4
    slots = groups * capacity
    ring = ring_order(shards)
    offsets, pairs = offset_cover(shards)
    roles = len(offsets)
    height = width * capacity // LANES + TAIL

    def from_offset(x, offset):
        perm = [(ring[(e + offset) % shards], ring[e]) for e in range(shards)]
        return lax.ppermute(x, "shard", perm)

    def exchange(blocks, stagger=False):
        got = list(blocks)
        for k in range(1, groups):
            block = after(blocks[k], got[1]) if k > 2 and stagger else blocks[k]
            got[k] = lax.ppermute(block, "group", [(z, z ^ k) for z in range(groups)])
        return got

    code = row_cluster * groups + row_group[:, 0]
    *send, place = call(
        lambda *refs: sort_kernel("group", *refs),
        [jax.ShapeDtypeStruct((height, LANES), jnp.bfloat16)] * groups
        + [jax.ShapeDtypeStruct((1, rows), jnp.int32)],
        [
            pltpu.VMEM((rows, width), embeddings.dtype),
            pltpu.VMEM((rows, width), jnp.bfloat16),
            pltpu.SemaphoreType.DMA((4,)),
        ],
        (embeddings, code.reshape(1, rows)),
        2 * rows * slots * width,
        4 * rows * width,
        [pl.BlockSpec(memory_space=pltpu.HBM), pl.BlockSpec(memory_space=pltpu.VMEM)],
        53 * MIB,
    )

    late = [groups - 1] if groups > 1 else []
    early = list(range(groups - len(late)))
    near = [r for r in range(1, roles) if 2 * offsets[r] != shards]
    far = [r for r in range(1, roles) if r not in near]
    own = exchange(send, True)
    held = [[None] * groups for _ in offsets]
    held[0] = [(x, None) for x in own]
    for k in range(groups):
        block = own[k]
        if k > 1:
            passed = [held[r][k - 2][0] for r in near]
            block = stack([after(block, *passed)], WAIT)
        for r in near:
            ready = after(block, held[near[0]][0][0]) if k == 1 else block
            held[r][k] = (from_offset(ready, offsets[r]), 0 if k > 1 else None)
    got = {r: from_offset(stack(own, 0), offsets[r]) for r in far}
    everything = [(0, 0, False)]
    everything += [(offsets.index(a), offsets.index(b), both) for a, b, both in pairs]
    steps = [[], [], []]
    for left, right, both in everything:
        for left_ks in (early, late):
            for right_ks in (early, late):
                if left_ks and right_ks:
                    step = 0
                    for role, ks in ((left, left_ks), (right, right_ks)):
                        if role in far:
                            step = max(step, 1)
                        elif ks is late:
                            step = max(step, 2 if role else 1)
                    steps[step].append((left, left_ks, right, right_ks, both))
    steps = [tasks for tasks in steps if tasks]
    acc = []
    for i, tasks in enumerate(steps):
        if i == 1:
            for r in far:
                held[r] = [(got[r], k) for k in range(groups)]
        acc, partial = score(held, tasks, acc, i == len(steps) - 1, slots, width)

    others = [from_offset(partial[r], -offsets[r]) for r in range(1, roles)]
    best = call(
        lambda *refs: merge_kernel(roles, *refs),
        [jax.ShapeDtypeStruct((1, capacity), jnp.float32)] * groups,
        [],
        [partial[0]] + others,
        roles * slots,
        4 * roles * slots,
    )
    back = exchange(best)
    (result,) = call(
        lambda *refs: place_kernel(groups, *refs),
        [jax.ShapeDtypeStruct((1, rows), jnp.float32)],
        [],
        back[::-1] + [place],
        rows * slots,
        4 * slots,
    )
    return result.reshape(rows)


def solution(mesh):
    placed = (P(("shard", "group"), None), P(("shard", "group"), None), P(("shard", "group")))
    return jax.shard_map(
        per_device, mesh=mesh, in_specs=placed, out_specs=P(("shard", "group")), check_vma=False
    )
```

```python
import jax
import jax.numpy as jnp
from jax import lax
from jax.experimental import pallas as pl
from jax.experimental.pallas import tpu as pltpu
from jax.sharding import PartitionSpec as P

LANES = 128
TAIL = 16
LOW = -2.0
MIB = 1024 * 1024
WAIT = 2 * 10**10


def ring_order(size):
    if size % 2:
        return list(range(size))
    half = size // 2
    chips = [i ^ (i >> 1) for i in range(half)]
    if sorted(chips) != list(range(half)):
        chips = list(range(half))
    return [2 * chip + core for core in range(2) for chip in chips]


def offset_cover(size):
    offsets = list(dict.fromkeys([0, size // 2, 1 % size, (size - 1) % size]))

    def missing(chosen):
        have = {(a - b) % size for a in chosen for b in chosen}
        return [d for d in range(size) if d not in have]

    while missing(offsets):
        offsets.append(min(range(size), key=lambda x: len(missing(offsets + [x]))))
    pairs = []
    for diff in range(1, size // 2 + 1):
        found = [
            (a, b)
            for b in [1 % size] + offsets
            for a in offsets
            if (a - b) % size in (diff, size - diff)
        ]
        if 2 * diff == size:
            found = [(a, b) for a, b in found if b == 0] + found
        a, b = found[0]
        pairs.append((a, b, b != 0 or 2 * diff != size))
    return offsets, pairs


def column_of(row):
    size = row.shape[1]
    return jnp.transpose(jnp.broadcast_to(row, (size, size)))


def sort_kernel(axis, far_ref, code_ref, *refs):
    *block_refs, place_ref, near_ref, unit_ref, sems = refs
    rows, width = near_ref.shape
    groups = len(block_refs)
    capacity = (block_refs[0].shape[0] - TAIL) * LANES // width
    slots = groups * capacity
    chunks = width // LANES
    parts = sems.shape[0]
    size = rows // parts
    copies = [
        pltpu.make_async_copy(
            far_ref.at[pl.ds(i * size, size), :], near_ref.at[pl.ds(i * size, size), :], sems.at[i]
        )
        for i in range(parts)
    ]
    for copy in copies:
        copy.start()
    code = code_ref[...]
    rel = (code & (groups - 1)) ^ lax.axis_index(axis)
    label = code >> (groups.bit_length() - 1)
    lines = max(8, groups)
    onehot = lax.broadcasted_iota(jnp.int32, (lines, rows), 0) == rel
    before = lax.broadcasted_iota(jnp.int32, (rows, rows), 0) < lax.broadcasted_iota(
        jnp.int32, (rows, rows), 1
    )
    ranks = jnp.dot(
        jnp.where(onehot, 1.0, 0.0).astype(jnp.bfloat16),
        jnp.where(before, 1.0, 0.0).astype(jnp.bfloat16),
        preferred_element_type=jnp.float32,
    )
    rank = jnp.sum(jnp.where(onehot, ranks, 0.0), axis=0, keepdims=True)
    place = rel * capacity + rank.astype(jnp.int32)
    place_ref[...] = place
    move = jnp.where(
        lax.broadcasted_iota(jnp.int32, (slots, rows), 0) == place, 1.0, 0.0
    ).astype(jnp.bfloat16)
    labels = jnp.broadcast_to(label + 1, (TAIL, rows)).astype(jnp.bfloat16)
    sorted_labels = (
        lax.dot_general(
            labels, move, (((1,), (1,)), ((), ())), preferred_element_type=jnp.float32
        )
        - 1.0
    ).astype(jnp.bfloat16)
    for i, copy in enumerate(copies):
        copy.wait()
        feats = near_ref[pl.ds(i * size, size), :].astype(jnp.float32)
        squares = jnp.sum(feats * feats, axis=1, keepdims=True) + 1e-06
        unit_ref[pl.ds(i * size, size), :] = (feats * lax.rsqrt(squares)).astype(jnp.bfloat16)
    for k, block_ref in enumerate(block_refs):
        part = slice(k * capacity, (k + 1) * capacity)
        block = jnp.dot(
            move[part], unit_ref[...], preferred_element_type=jnp.float32
        ).astype(jnp.bfloat16)
        for c in range(chunks):
            block_ref[pl.ds(c * capacity, capacity), :] = block[:, c * LANES : (c + 1) * LANES]
        block_ref[pl.ds(chunks * capacity, TAIL), :] = sorted_labels[:, part]


def stack_kernel(*refs):
    for k, ref in enumerate(refs[:-1]):
        refs[-1][k] = ref[...]


def score_kernel(sources, tasks, groups, roles, first, last, *refs):
    *refs, flat_ref, side_ref = refs
    outs = 2 + (roles if last else 0)
    inputs, (row_ref, column_ref, *out_refs) = refs[:-outs], refs[-outs:]
    capacity = LANES
    slots = groups * capacity
    low = jnp.float32(LOW)
    if first:
        row_ref[...] = jnp.full(row_ref.shape, low)
        column_ref[...] = jnp.full(column_ref.shape, low)
    else:
        *inputs, old_rows, old_columns = inputs
        row_ref[...] = old_rows[...]
        column_ref[...] = old_columns[...]
    tops = {}
    for (role, k), (index, part) in sources.items():
        ref = inputs[index] if part is None else inputs[index].at[part]
        height = ref.shape[0] - TAIL
        rows = pl.ds(k * capacity, capacity)
        for c in range(height // capacity):
            flat_ref[role, rows, pl.ds(c * LANES, LANES)] = ref[pl.ds(c * capacity, capacity), :]
        tops[role, k] = ref[pl.ds(height, TAIL), :][0:1].astype(jnp.float32)
    for role, k in sorted({(left, k) for left, ks, _, _, _ in tasks for k in ks}):
        side_ref[role, pl.ds(k * capacity, capacity), :] = column_of(tops[role, k])
    for left, left_ks, right, right_ks, want_rows in tasks:
        start, count = left_ks[0] * capacity, len(left_ks) * capacity
        rows = pl.ds(start, count)
        for i in range(0, len(right_ks), 2):
            some = right_ks[i : i + 2]
            width = len(some) * capacity
            columns = pl.ds(some[0] * capacity, width)
            scores = lax.dot_general(
                flat_ref[left, rows, :],
                flat_ref[right, columns, :],
                (((1,), (1,)), ((), ())),
                preferred_element_type=jnp.float32,
            )
            top = jnp.concatenate([tops[right, k] for k in some], axis=1)
            same = jnp.concatenate([side_ref[left, rows, :]] * len(some), axis=1) == top
            if left == right:
                same = same & (
                    lax.broadcasted_iota(jnp.int32, (count, width), 0) + start
                    != lax.broadcasted_iota(jnp.int32, (count, width), 1) + some[0] * capacity
                )
            scores = jnp.where(same, scores, low)
            if want_rows:
                best = row_ref[left, rows, :]
                for c in range(len(some)):
                    best = jnp.maximum(best, scores[:, c * LANES : (c + 1) * LANES])
                row_ref[left, rows, :] = best
            best = jnp.max(scores.reshape(count // 8, 8, width), axis=0)
            column_ref[right, :, columns] = jnp.maximum(column_ref[right, :, columns], best)
    for role, out_ref in enumerate(out_refs):
        best = jnp.max(column_ref[role], axis=0, keepdims=True)
        turned = [
            jnp.max(
                jnp.transpose(row_ref[role, pl.ds(k * capacity, capacity), :]),
                axis=0,
                keepdims=True,
            )
            for k in range(groups)
        ]
        out_ref[...] = jnp.maximum(best, jnp.concatenate(turned, axis=1))


def merge_kernel(roles, *refs):
    best = refs[0][...]
    for r in range(1, roles):
        best = jnp.maximum(best, refs[r][...])
    best = jnp.maximum(best, jnp.float32(-1.0))
    for k, out_ref in enumerate(refs[roles:]):
        out_ref[...] = best[:, k * LANES : (k + 1) * LANES]


def place_kernel(groups, *refs):
    place = refs[groups][...]
    rows = place.shape[1]
    best = jnp.full((1, rows), jnp.float32(LOW))
    for k in range(groups):
        values = jnp.concatenate([column_of(refs[groups - 1 - k][...])] * (rows // LANES), axis=1)
        here = lax.broadcasted_iota(jnp.int32, (LANES, rows), 0) + k * LANES == place
        best = jnp.maximum(
            best, jnp.max(jnp.where(here, values, jnp.float32(LOW)), axis=0, keepdims=True)
        )
    refs[groups + 1][...] = best


def in_vmem(count):
    return [pl.BlockSpec(memory_space=pltpu.VMEM)] * count


def call(
    kernel, out_shape, scratch, args, flops, bytes_accessed, in_specs=None, limit=48 * MIB, aliases=None
):
    return pl.pallas_call(
        kernel,
        out_shape=out_shape,
        in_specs=in_specs or in_vmem(len(args)),
        out_specs=in_vmem(len(out_shape)),
        scratch_shapes=scratch,
        input_output_aliases=aliases or {},
        compiler_params=pltpu.CompilerParams(vmem_limit_bytes=limit),
        cost_estimate=pl.CostEstimate(
            flops=flops, bytes_accessed=bytes_accessed, transcendentals=0
        ),
    )(*args)


def after(x, *earlier):
    return lax.optimization_barrier((x, *earlier))[0]


def stack(parts, wait):
    return call(
        stack_kernel,
        [jax.ShapeDtypeStruct((len(parts), *parts[0].shape), parts[0].dtype)],
        [],
        parts,
        wait,
        4 * len(parts) * parts[0].size,
    )[0]


def score(held, tasks, acc, last, slots, width):
    roles, groups = len(held), len(held[0])
    used = sorted(
        {(left, k) for left, ks, _, _, _ in tasks for k in ks}
        | {(right, k) for _, _, right, ks, _ in tasks for k in ks},
        key=lambda x: (x[0], -x[1]),
    )
    arrays, sources = [], {}
    for role, k in used:
        array, part = held[role][k]
        index = next((i for i, x in enumerate(arrays) if x is array), len(arrays))
        if index == len(arrays):
            arrays.append(array)
        sources[role, k] = (index, part)
    states = [
        jax.ShapeDtypeStruct((roles, slots, LANES), jnp.float32),
        jax.ShapeDtypeStruct((roles, 8, slots), jnp.float32),
    ]
    ends = [jax.ShapeDtypeStruct((1, slots), jnp.float32)] * roles if last else []
    tiles = sum(len(task[1]) * len(task[3]) for task in tasks)
    count = len(arrays)
    got = call(
        lambda *refs: score_kernel(sources, tasks, groups, roles, not acc, last, *refs),
        states + ends,
        [
            pltpu.VMEM((roles, slots, width), jnp.bfloat16),
            pltpu.VMEM((roles, slots, LANES), jnp.float32),
        ],
        arrays + list(acc),
        2 * tiles * LANES * LANES * width,
        2 * len(used) * LANES * width,
        aliases={count: 0, count + 1: 1} if acc else {},
    )
    return got[:2], got[2:]


def per_device(embeddings, row_group, row_cluster):
    rows, width = embeddings.shape
    groups = lax.axis_size("group")
    shards = lax.axis_size("shard")
    capacity = rows // 4
    slots = groups * capacity
    ring = ring_order(shards)
    offsets, pairs = offset_cover(shards)
    roles = len(offsets)
    height = width * capacity // LANES + TAIL

    def from_offset(x, offset):
        perm = [(ring[(e + offset) % shards], ring[e]) for e in range(shards)]
        return lax.ppermute(x, "shard", perm)

    def exchange(blocks, last=()):
        got = list(blocks)
        for k in range(1, groups):
            block = after(blocks[k], *last) if k == groups - 1 else blocks[k]
            got[k] = lax.ppermute(block, "group", [(z, z ^ k) for z in range(groups)])
        return got

    code = row_cluster * groups + row_group[:, 0]
    *send, place = call(
        lambda *refs: sort_kernel("group", *refs),
        [jax.ShapeDtypeStruct((height, LANES), jnp.bfloat16)] * groups
        + [jax.ShapeDtypeStruct((1, rows), jnp.int32)],
        [
            pltpu.VMEM((rows, width), embeddings.dtype),
            pltpu.VMEM((rows, width), jnp.bfloat16),
            pltpu.SemaphoreType.DMA((4,)),
        ],
        (embeddings, code.reshape(1, rows)),
        2 * rows * slots * width,
        4 * rows * width,
        [pl.BlockSpec(memory_space=pltpu.HBM), pl.BlockSpec(memory_space=pltpu.VMEM)],
        53 * MIB,
    )

    late = [groups - 1] if groups > 1 else []
    early = list(range(groups - len(late)))
    near = [r for r in range(1, roles) if 2 * offsets[r] != shards]
    far = [r for r in range(1, roles) if r not in near]
    first = {r: from_offset(send[0], offsets[r]) for r in near}
    own = exchange(send, [first[r] for r in near[:1]])
    held = [[None] * groups for _ in offsets]
    held[0] = [(x, None) for x in own]
    for r in near:
        held[r][0] = (first[r], None)
    for ks, wait in ((early[1:], WAIT), (late, WAIT)):
        if ks:
            passed = []
            block = stack([after(own[k], *passed) for k in ks], wait)
            for r in near:
                got = from_offset(block, offsets[r])
                for i, k in enumerate(ks):
                    held[r][k] = (got, i)
    got = {r: from_offset(stack(own, 0), offsets[r]) for r in far}
    everything = [(0, 0, False)]
    everything += [(offsets.index(a), offsets.index(b), both) for a, b, both in pairs]
    steps = [[], [], []]
    for left, right, both in everything:
        for left_ks in (early, late):
            for right_ks in (early, late):
                if left_ks and right_ks:
                    step = 0
                    for role, ks in ((left, left_ks), (right, right_ks)):
                        if role in far:
                            step = max(step, 1)
                        elif ks is late:
                            step = max(step, 2 if role else 1)
                    steps[step].append((left, left_ks, right, right_ks, both))
    steps = [tasks for tasks in steps if tasks]
    acc = []
    for i, tasks in enumerate(steps):
        if i == 1:
            for r in far:
                held[r] = [(got[r], k) for k in range(groups)]
        acc, partial = score(held, tasks, acc, i == len(steps) - 1, slots, width)

    others = [from_offset(partial[r], -offsets[r]) for r in range(1, roles)]
    best = call(
        lambda *refs: merge_kernel(roles, *refs),
        [jax.ShapeDtypeStruct((1, capacity), jnp.float32)] * groups,
        [],
        [partial[0]] + others,
        roles * slots,
        4 * roles * slots,
    )
    back = exchange(best)
    (result,) = call(
        lambda *refs: place_kernel(groups, *refs),
        [jax.ShapeDtypeStruct((1, rows), jnp.float32)],
        [],
        back[::-1] + [place],
        rows * slots,
        4 * slots,
    )
    return result.reshape(rows)


def solution(mesh):
    placed = (P(("shard", "group"), None), P(("shard", "group"), None), P(("shard", "group")))
    return jax.shard_map(
        per_device, mesh=mesh, in_specs=placed, out_specs=P(("shard", "group")), check_vma=False
    )
```

```python
import jax
import jax.numpy as jnp
from jax import lax
from jax.experimental import pallas as pl
from jax.experimental.pallas import tpu as pltpu
from jax.sharding import PartitionSpec as P

LANES = 128
TAIL = 16
LOW = -2.0
MIB = 1024 * 1024
WAIT = 2 * 10**10


def ring_order(size):
    if size % 2:
        return list(range(size))
    half = size // 2
    chips = [i ^ (i >> 1) for i in range(half)]
    if sorted(chips) != list(range(half)):
        chips = list(range(half))
    return [2 * chip + core for core in range(2) for chip in chips]


def offset_cover(size):
    offsets = list(dict.fromkeys([0, size // 2, 1 % size, (size - 1) % size]))

    def missing(chosen):
        have = {(a - b) % size for a in chosen for b in chosen}
        return [d for d in range(size) if d not in have]

    while missing(offsets):
        offsets.append(min(range(size), key=lambda x: len(missing(offsets + [x]))))
    pairs = []
    for diff in range(1, size // 2 + 1):
        found = [
            (a, b)
            for b in [1 % size] + offsets
            for a in offsets
            if (a - b) % size in (diff, size - diff)
        ]
        if 2 * diff == size:
            found = [(a, b) for a, b in found if b == 0] + found
        a, b = found[0]
        pairs.append((a, b, b != 0 or 2 * diff != size))
    return offsets, pairs


def column_of(row):
    size = row.shape[1]
    return jnp.transpose(jnp.broadcast_to(row, (size, size)))


def sort_kernel(axis, far_ref, code_ref, *refs):
    *block_refs, place_ref, near_ref, unit_ref, sems = refs
    rows, width = near_ref.shape
    groups = len(block_refs)
    capacity = (block_refs[0].shape[0] - TAIL) * LANES // width
    slots = groups * capacity
    chunks = width // LANES
    parts = sems.shape[0]
    size = rows // parts
    copies = [
        pltpu.make_async_copy(
            far_ref.at[pl.ds(i * size, size), :], near_ref.at[pl.ds(i * size, size), :], sems.at[i]
        )
        for i in range(parts)
    ]
    for copy in copies:
        copy.start()
    code = code_ref[...]
    rel = (code & (groups - 1)) ^ lax.axis_index(axis)
    label = code >> (groups.bit_length() - 1)
    lines = max(8, groups)
    onehot = lax.broadcasted_iota(jnp.int32, (lines, rows), 0) == rel
    before = lax.broadcasted_iota(jnp.int32, (rows, rows), 0) < lax.broadcasted_iota(
        jnp.int32, (rows, rows), 1
    )
    ranks = jnp.dot(
        jnp.where(onehot, 1.0, 0.0).astype(jnp.bfloat16),
        jnp.where(before, 1.0, 0.0).astype(jnp.bfloat16),
        preferred_element_type=jnp.float32,
    )
    rank = jnp.sum(jnp.where(onehot, ranks, 0.0), axis=0, keepdims=True)
    place = rel * capacity + rank.astype(jnp.int32)
    place_ref[...] = place
    move = jnp.where(
        lax.broadcasted_iota(jnp.int32, (slots, rows), 0) == place, 1.0, 0.0
    ).astype(jnp.bfloat16)
    labels = jnp.broadcast_to(label + 1, (TAIL, rows)).astype(jnp.bfloat16)
    sorted_labels = (
        lax.dot_general(
            labels, move, (((1,), (1,)), ((), ())), preferred_element_type=jnp.float32
        )
        - 1.0
    ).astype(jnp.bfloat16)
    for i, copy in enumerate(copies):
        copy.wait()
        feats = near_ref[pl.ds(i * size, size), :].astype(jnp.float32)
        squares = jnp.sum(feats * feats, axis=1, keepdims=True) + 1e-06
        unit_ref[pl.ds(i * size, size), :] = (feats * lax.rsqrt(squares)).astype(jnp.bfloat16)
    for k, block_ref in enumerate(block_refs):
        part = slice(k * capacity, (k + 1) * capacity)
        block = jnp.dot(
            move[part], unit_ref[...], preferred_element_type=jnp.float32
        ).astype(jnp.bfloat16)
        for c in range(chunks):
            block_ref[pl.ds(c * capacity, capacity), :] = block[:, c * LANES : (c + 1) * LANES]
        block_ref[pl.ds(chunks * capacity, TAIL), :] = sorted_labels[:, part]


def stack_kernel(*refs):
    for k, ref in enumerate(refs[:-1]):
        refs[-1][k] = ref[...]


def score_kernel(sources, tasks, groups, roles, first, last, *refs):
    *refs, flat_ref, side_ref = refs
    outs = 2 + (roles if last else 0)
    inputs, (row_ref, column_ref, *out_refs) = refs[:-outs], refs[-outs:]
    capacity = LANES
    slots = groups * capacity
    low = jnp.float32(LOW)
    if first:
        row_ref[...] = jnp.full(row_ref.shape, low)
        column_ref[...] = jnp.full(column_ref.shape, low)
    else:
        *inputs, old_rows, old_columns = inputs
        row_ref[...] = old_rows[...]
        column_ref[...] = old_columns[...]
    tops = {}
    for (role, k), (index, part) in sources.items():
        ref = inputs[index] if part is None else inputs[index].at[part]
        height = ref.shape[0] - TAIL
        rows = pl.ds(k * capacity, capacity)
        for c in range(height // capacity):
            flat_ref[role, rows, pl.ds(c * LANES, LANES)] = ref[pl.ds(c * capacity, capacity), :]
        tops[role, k] = ref[pl.ds(height, TAIL), :][0:1].astype(jnp.float32)
    for role, k in sorted({(left, k) for left, ks, _, _, _ in tasks for k in ks}):
        side_ref[role, pl.ds(k * capacity, capacity), :] = column_of(tops[role, k])
    for left, left_ks, right, right_ks, want_rows in tasks:
        start, count = left_ks[0] * capacity, len(left_ks) * capacity
        rows = pl.ds(start, count)
        for i in range(0, len(right_ks), 2):
            some = right_ks[i : i + 2]
            width = len(some) * capacity
            columns = pl.ds(some[0] * capacity, width)
            scores = lax.dot_general(
                flat_ref[left, rows, :],
                flat_ref[right, columns, :],
                (((1,), (1,)), ((), ())),
                preferred_element_type=jnp.float32,
            )
            top = jnp.concatenate([tops[right, k] for k in some], axis=1)
            same = jnp.concatenate([side_ref[left, rows, :]] * len(some), axis=1) == top
            if left == right:
                same = same & (
                    lax.broadcasted_iota(jnp.int32, (count, width), 0) + start
                    != lax.broadcasted_iota(jnp.int32, (count, width), 1) + some[0] * capacity
                )
            scores = jnp.where(same, scores, low)
            if want_rows:
                best = row_ref[left, rows, :]
                for c in range(len(some)):
                    best = jnp.maximum(best, scores[:, c * LANES : (c + 1) * LANES])
                row_ref[left, rows, :] = best
            best = jnp.max(scores.reshape(count // 8, 8, width), axis=0)
            column_ref[right, :, columns] = jnp.maximum(column_ref[right, :, columns], best)
    for role, out_ref in enumerate(out_refs):
        best = jnp.max(column_ref[role], axis=0, keepdims=True)
        turned = [
            jnp.max(
                jnp.transpose(row_ref[role, pl.ds(k * capacity, capacity), :]),
                axis=0,
                keepdims=True,
            )
            for k in range(groups)
        ]
        out_ref[...] = jnp.maximum(best, jnp.concatenate(turned, axis=1))


def merge_kernel(roles, *refs):
    best = refs[0][...]
    for r in range(1, roles):
        best = jnp.maximum(best, refs[r][...])
    best = jnp.maximum(best, jnp.float32(-1.0))
    for k, out_ref in enumerate(refs[roles:]):
        out_ref[...] = best[:, k * LANES : (k + 1) * LANES]


def place_kernel(groups, *refs):
    place = refs[groups][...]
    rows = place.shape[1]
    best = jnp.full((1, rows), jnp.float32(LOW))
    for k in range(groups):
        values = jnp.concatenate([column_of(refs[groups - 1 - k][...])] * (rows // LANES), axis=1)
        here = lax.broadcasted_iota(jnp.int32, (LANES, rows), 0) + k * LANES == place
        best = jnp.maximum(
            best, jnp.max(jnp.where(here, values, jnp.float32(LOW)), axis=0, keepdims=True)
        )
    refs[groups + 1][...] = best


def in_vmem(count):
    return [pl.BlockSpec(memory_space=pltpu.VMEM)] * count


def call(
    kernel, out_shape, scratch, args, flops, bytes_accessed, in_specs=None, limit=48 * MIB, aliases=None
):
    return pl.pallas_call(
        kernel,
        out_shape=out_shape,
        in_specs=in_specs or in_vmem(len(args)),
        out_specs=in_vmem(len(out_shape)),
        scratch_shapes=scratch,
        input_output_aliases=aliases or {},
        compiler_params=pltpu.CompilerParams(vmem_limit_bytes=limit),
        cost_estimate=pl.CostEstimate(
            flops=flops, bytes_accessed=bytes_accessed, transcendentals=0
        ),
    )(*args)


def after(x, *earlier):
    return lax.optimization_barrier((x, *earlier))[0]


def stack(parts, wait):
    return call(
        stack_kernel,
        [jax.ShapeDtypeStruct((len(parts), *parts[0].shape), parts[0].dtype)],
        [],
        parts,
        wait,
        4 * len(parts) * parts[0].size,
    )[0]


def score(held, tasks, acc, last, slots, width):
    roles, groups = len(held), len(held[0])
    used = sorted(
        {(left, k) for left, ks, _, _, _ in tasks for k in ks}
        | {(right, k) for _, _, right, ks, _ in tasks for k in ks},
        key=lambda x: (x[0], -x[1]),
    )
    arrays, sources = [], {}
    for role, k in used:
        array, part = held[role][k]
        index = next((i for i, x in enumerate(arrays) if x is array), len(arrays))
        if index == len(arrays):
            arrays.append(array)
        sources[role, k] = (index, part)
    states = [
        jax.ShapeDtypeStruct((roles, slots, LANES), jnp.float32),
        jax.ShapeDtypeStruct((roles, 8, slots), jnp.float32),
    ]
    ends = [jax.ShapeDtypeStruct((1, slots), jnp.float32)] * roles if last else []
    tiles = sum(len(task[1]) * len(task[3]) for task in tasks)
    count = len(arrays)
    got = call(
        lambda *refs: score_kernel(sources, tasks, groups, roles, not acc, last, *refs),
        states + ends,
        [
            pltpu.VMEM((roles, slots, width), jnp.bfloat16),
            pltpu.VMEM((roles, slots, LANES), jnp.float32),
        ],
        arrays + list(acc),
        2 * tiles * LANES * LANES * width,
        2 * len(used) * LANES * width,
        aliases={count: 0, count + 1: 1} if acc else {},
    )
    return got[:2], got[2:]


def per_device(embeddings, row_group, row_cluster):
    rows, width = embeddings.shape
    groups = lax.axis_size("group")
    shards = lax.axis_size("shard")
    capacity = rows // 4
    slots = groups * capacity
    ring = ring_order(shards)
    offsets, pairs = offset_cover(shards)
    roles = len(offsets)
    height = width * capacity // LANES + TAIL

    def from_offset(x, offset):
        perm = [(ring[(e + offset) % shards], ring[e]) for e in range(shards)]
        return lax.ppermute(x, "shard", perm)

    def exchange(blocks, stagger=False):
        got = list(blocks)
        for k in range(1, groups):
            block = after(blocks[k], got[1]) if k > 2 and stagger else blocks[k]
            got[k] = lax.ppermute(block, "group", [(z, z ^ k) for z in range(groups)])
        return got

    code = row_cluster * groups + row_group[:, 0]
    *send, place = call(
        lambda *refs: sort_kernel("group", *refs),
        [jax.ShapeDtypeStruct((height, LANES), jnp.bfloat16)] * groups
        + [jax.ShapeDtypeStruct((1, rows), jnp.int32)],
        [
            pltpu.VMEM((rows, width), embeddings.dtype),
            pltpu.VMEM((rows, width), jnp.bfloat16),
            pltpu.SemaphoreType.DMA((4,)),
        ],
        (embeddings, code.reshape(1, rows)),
        2 * rows * slots * width,
        4 * rows * width,
        [pl.BlockSpec(memory_space=pltpu.HBM), pl.BlockSpec(memory_space=pltpu.VMEM)],
        53 * MIB,
    )

    late = [groups - 1] if groups > 1 else []
    early = list(range(groups - len(late)))
    near = [r for r in range(1, roles) if 2 * offsets[r] != shards]
    far = [r for r in range(1, roles) if r not in near]
    own = exchange(send, True)
    held = [[None] * groups for _ in offsets]
    held[0] = [(x, None) for x in own]
    for k in range(groups):
        block = own[k]
        if k > 1:
            passed = [held[r][k - 2][0] for r in near]
            block = stack([after(block, *passed)], WAIT if k == groups - 1 else WAIT // 20)
        for r in near:
            ready = after(block, held[near[0]][0][0]) if k == 1 else block
            held[r][k] = (from_offset(ready, offsets[r]), 0 if k > 1 else None)
    got = {r: from_offset(stack(own, 0), offsets[r]) for r in far}
    everything = [(0, 0, False)]
    everything += [(offsets.index(a), offsets.index(b), both) for a, b, both in pairs]
    steps = [[], [], []]
    for left, right, both in everything:
        for left_ks in (early, late):
            for right_ks in (early, late):
                if left_ks and right_ks:
                    step = 0
                    for role, ks in ((left, left_ks), (right, right_ks)):
                        if role in far:
                            step = max(step, 1)
                        elif ks is late:
                            step = max(step, 2 if role else 1)
                    steps[step].append((left, left_ks, right, right_ks, both))
    steps = [tasks for tasks in steps if tasks]
    acc = []
    for i, tasks in enumerate(steps):
        if i == 1:
            for r in far:
                held[r] = [(got[r], k) for k in range(groups)]
        acc, partial = score(held, tasks, acc, i == len(steps) - 1, slots, width)

    others = [from_offset(partial[r], -offsets[r]) for r in range(1, roles)]
    best = call(
        lambda *refs: merge_kernel(roles, *refs),
        [jax.ShapeDtypeStruct((1, capacity), jnp.float32)] * groups,
        [],
        [partial[0]] + others,
        roles * slots,
        4 * roles * slots,
    )
    back = exchange(best)
    (result,) = call(
        lambda *refs: place_kernel(groups, *refs),
        [jax.ShapeDtypeStruct((1, rows), jnp.float32)],
        [],
        back[::-1] + [place],
        rows * slots,
        4 * slots,
    )
    return result.reshape(rows)


def solution(mesh):
    placed = (P(("shard", "group"), None), P(("shard", "group"), None), P(("shard", "group")))
    return jax.shard_map(
        per_device, mesh=mesh, in_specs=placed, out_specs=P(("shard", "group")), check_vma=False
    )
```

```python
import jax
import jax.numpy as jnp
from jax import lax
from jax.experimental import pallas as pl
from jax.experimental.pallas import tpu as pltpu
from jax.sharding import PartitionSpec as P

LANES = 128
TAIL = 16
LOW = -2.0
MIB = 1024 * 1024
WAIT = 2 * 10**10


def ring_order(size):
    if size % 2:
        return list(range(size))
    half = size // 2
    chips = [i ^ (i >> 1) for i in range(half)]
    if sorted(chips) != list(range(half)):
        chips = list(range(half))
    return [2 * chip + core for core in range(2) for chip in chips]


def offset_cover(size):
    offsets = list(dict.fromkeys([0, size // 2, 1 % size, (size - 1) % size]))

    def missing(chosen):
        have = {(a - b) % size for a in chosen for b in chosen}
        return [d for d in range(size) if d not in have]

    while missing(offsets):
        offsets.append(min(range(size), key=lambda x: len(missing(offsets + [x]))))
    pairs = []
    for diff in range(1, size // 2 + 1):
        found = [
            (a, b)
            for b in [1 % size] + offsets
            for a in offsets
            if (a - b) % size in (diff, size - diff)
        ]
        if 2 * diff == size:
            found = [(a, b) for a, b in found if b == 0] + found
        a, b = found[0]
        pairs.append((a, b, b != 0 or 2 * diff != size))
    return offsets, pairs


def column_of(row):
    size = row.shape[1]
    return jnp.transpose(jnp.broadcast_to(row, (size, size)))


def sort_kernel(axis, far_ref, code_ref, *refs):
    *block_refs, place_ref, near_ref, unit_ref, sems = refs
    rows, width = near_ref.shape
    groups = len(block_refs)
    capacity = (block_refs[0].shape[0] - TAIL) * LANES // width
    slots = groups * capacity
    chunks = width // LANES
    parts = sems.shape[0]
    size = rows // parts
    copies = [
        pltpu.make_async_copy(
            far_ref.at[pl.ds(i * size, size), :], near_ref.at[pl.ds(i * size, size), :], sems.at[i]
        )
        for i in range(parts)
    ]
    for copy in copies:
        copy.start()
    code = code_ref[...]
    rel = (code & (groups - 1)) ^ lax.axis_index(axis)
    label = code >> (groups.bit_length() - 1)
    lines = max(8, groups)
    onehot = lax.broadcasted_iota(jnp.int32, (lines, rows), 0) == rel
    before = lax.broadcasted_iota(jnp.int32, (rows, rows), 0) < lax.broadcasted_iota(
        jnp.int32, (rows, rows), 1
    )
    ranks = jnp.dot(
        jnp.where(onehot, 1.0, 0.0).astype(jnp.bfloat16),
        jnp.where(before, 1.0, 0.0).astype(jnp.bfloat16),
        preferred_element_type=jnp.float32,
    )
    rank = jnp.sum(jnp.where(onehot, ranks, 0.0), axis=0, keepdims=True)
    place = rel * capacity + rank.astype(jnp.int32)
    place_ref[...] = place
    move = jnp.where(
        lax.broadcasted_iota(jnp.int32, (slots, rows), 0) == place, 1.0, 0.0
    ).astype(jnp.bfloat16)
    labels = jnp.broadcast_to(label + 1, (TAIL, rows)).astype(jnp.bfloat16)
    sorted_labels = (
        lax.dot_general(
            labels, move, (((1,), (1,)), ((), ())), preferred_element_type=jnp.float32
        )
        - 1.0
    ).astype(jnp.bfloat16)
    for i, copy in enumerate(copies):
        copy.wait()
        feats = near_ref[pl.ds(i * size, size), :].astype(jnp.float32)
        squares = jnp.sum(feats * feats, axis=1, keepdims=True) + 1e-06
        unit_ref[pl.ds(i * size, size), :] = (feats * lax.rsqrt(squares)).astype(jnp.bfloat16)
    for k, block_ref in enumerate(block_refs):
        part = slice(k * capacity, (k + 1) * capacity)
        block = jnp.dot(
            move[part], unit_ref[...], preferred_element_type=jnp.float32
        ).astype(jnp.bfloat16)
        for c in range(chunks):
            block_ref[pl.ds(c * capacity, capacity), :] = block[:, c * LANES : (c + 1) * LANES]
        block_ref[pl.ds(chunks * capacity, TAIL), :] = sorted_labels[:, part]


def stack_kernel(*refs):
    for k, ref in enumerate(refs[:-1]):
        refs[-1][k] = ref[...]


def score_kernel(sources, tasks, groups, roles, first, last, *refs):
    *refs, flat_ref, side_ref = refs
    outs = 2 + (roles if last else 0)
    inputs, (row_ref, column_ref, *out_refs) = refs[:-outs], refs[-outs:]
    capacity = LANES
    slots = groups * capacity
    low = jnp.float32(LOW)
    if first:
        row_ref[...] = jnp.full(row_ref.shape, low)
        column_ref[...] = jnp.full(column_ref.shape, low)
    else:
        *inputs, old_rows, old_columns = inputs
        row_ref[...] = old_rows[...]
        column_ref[...] = old_columns[...]
    tops = {}
    for (role, k), (index, part) in sources.items():
        ref = inputs[index] if part is None else inputs[index].at[part]
        height = ref.shape[0] - TAIL
        rows = pl.ds(k * capacity, capacity)
        for c in range(height // capacity):
            flat_ref[role, rows, pl.ds(c * LANES, LANES)] = ref[pl.ds(c * capacity, capacity), :]
        tops[role, k] = ref[pl.ds(height, TAIL), :][0:1].astype(jnp.float32)
    for role, k in sorted({(left, k) for left, ks, _, _, _ in tasks for k in ks}):
        side_ref[role, pl.ds(k * capacity, capacity), :] = column_of(tops[role, k])
    for left, left_ks, right, right_ks, want_rows in tasks:
        start, count = left_ks[0] * capacity, len(left_ks) * capacity
        rows = pl.ds(start, count)
        for i in range(0, len(right_ks), 2):
            some = right_ks[i : i + 2]
            width = len(some) * capacity
            columns = pl.ds(some[0] * capacity, width)
            scores = lax.dot_general(
                flat_ref[left, rows, :],
                flat_ref[right, columns, :],
                (((1,), (1,)), ((), ())),
                preferred_element_type=jnp.float32,
            )
            top = jnp.concatenate([tops[right, k] for k in some], axis=1)
            same = jnp.concatenate([side_ref[left, rows, :]] * len(some), axis=1) == top
            if left == right:
                same = same & (
                    lax.broadcasted_iota(jnp.int32, (count, width), 0) + start
                    != lax.broadcasted_iota(jnp.int32, (count, width), 1) + some[0] * capacity
                )
            scores = jnp.where(same, scores, low)
            if want_rows:
                best = row_ref[left, rows, :]
                for c in range(len(some)):
                    best = jnp.maximum(best, scores[:, c * LANES : (c + 1) * LANES])
                row_ref[left, rows, :] = best
            best = jnp.max(scores.reshape(count // 8, 8, width), axis=0)
            column_ref[right, :, columns] = jnp.maximum(column_ref[right, :, columns], best)
    for role, out_ref in enumerate(out_refs):
        best = jnp.max(column_ref[role], axis=0, keepdims=True)
        turned = [
            jnp.max(
                jnp.transpose(row_ref[role, pl.ds(k * capacity, capacity), :]),
                axis=0,
                keepdims=True,
            )
            for k in range(groups)
        ]
        out_ref[...] = jnp.maximum(best, jnp.concatenate(turned, axis=1))


def merge_kernel(roles, *refs):
    best = refs[0][...]
    for r in range(1, roles):
        best = jnp.maximum(best, refs[r][...])
    best = jnp.maximum(best, jnp.float32(-1.0))
    for k, out_ref in enumerate(refs[roles:]):
        out_ref[...] = best[:, k * LANES : (k + 1) * LANES]


def place_kernel(groups, *refs):
    place = refs[groups][...]
    rows = place.shape[1]
    best = jnp.full((1, rows), jnp.float32(LOW))
    for k in range(groups):
        values = jnp.concatenate([column_of(refs[groups - 1 - k][...])] * (rows // LANES), axis=1)
        here = lax.broadcasted_iota(jnp.int32, (LANES, rows), 0) + k * LANES == place
        best = jnp.maximum(
            best, jnp.max(jnp.where(here, values, jnp.float32(LOW)), axis=0, keepdims=True)
        )
    refs[groups + 1][...] = best


def in_vmem(count):
    return [pl.BlockSpec(memory_space=pltpu.VMEM)] * count


def call(
    kernel, out_shape, scratch, args, flops, bytes_accessed, in_specs=None, limit=48 * MIB, aliases=None
):
    return pl.pallas_call(
        kernel,
        out_shape=out_shape,
        in_specs=in_specs or in_vmem(len(args)),
        out_specs=in_vmem(len(out_shape)),
        scratch_shapes=scratch,
        input_output_aliases=aliases or {},
        compiler_params=pltpu.CompilerParams(vmem_limit_bytes=limit),
        cost_estimate=pl.CostEstimate(
            flops=flops, bytes_accessed=bytes_accessed, transcendentals=0
        ),
    )(*args)


def after(x, *earlier):
    return lax.optimization_barrier((x, *earlier))[0]


def stack(parts, wait):
    return call(
        stack_kernel,
        [jax.ShapeDtypeStruct((len(parts), *parts[0].shape), parts[0].dtype)],
        [],
        parts,
        wait,
        4 * len(parts) * parts[0].size,
    )[0]


def score(held, tasks, acc, last, slots, width):
    roles, groups = len(held), len(held[0])
    used = sorted(
        {(left, k) for left, ks, _, _, _ in tasks for k in ks}
        | {(right, k) for _, _, right, ks, _ in tasks for k in ks},
        key=lambda x: (x[0], -x[1]),
    )
    arrays, sources = [], {}
    for role, k in used:
        array, part = held[role][k]
        index = next((i for i, x in enumerate(arrays) if x is array), len(arrays))
        if index == len(arrays):
            arrays.append(array)
        sources[role, k] = (index, part)
    states = [
        jax.ShapeDtypeStruct((roles, slots, LANES), jnp.float32),
        jax.ShapeDtypeStruct((roles, 8, slots), jnp.float32),
    ]
    ends = [jax.ShapeDtypeStruct((1, slots), jnp.float32)] * roles if last else []
    tiles = sum(len(task[1]) * len(task[3]) for task in tasks)
    count = len(arrays)
    got = call(
        lambda *refs: score_kernel(sources, tasks, groups, roles, not acc, last, *refs),
        states + ends,
        [
            pltpu.VMEM((roles, slots, width), jnp.bfloat16),
            pltpu.VMEM((roles, slots, LANES), jnp.float32),
        ],
        arrays + list(acc),
        2 * tiles * LANES * LANES * width,
        2 * len(used) * LANES * width,
        aliases={count: 0, count + 1: 1} if acc else {},
    )
    return got[:2], got[2:]


def per_device(embeddings, row_group, row_cluster):
    rows, width = embeddings.shape
    groups = lax.axis_size("group")
    shards = lax.axis_size("shard")
    capacity = rows // 4
    slots = groups * capacity
    ring = ring_order(shards)
    offsets, pairs = offset_cover(shards)
    roles = len(offsets)
    height = width * capacity // LANES + TAIL

    def from_offset(x, offset):
        perm = [(ring[(e + offset) % shards], ring[e]) for e in range(shards)]
        return lax.ppermute(x, "shard", perm)

    def exchange(blocks, last=()):
        got = list(blocks)
        for k in range(1, groups):
            block = after(blocks[k], got[2]) if k > 2 and last else blocks[k]
            got[k] = lax.ppermute(block, "group", [(z, z ^ k) for z in range(groups)])
        return got

    code = row_cluster * groups + row_group[:, 0]
    *send, place = call(
        lambda *refs: sort_kernel("group", *refs),
        [jax.ShapeDtypeStruct((height, LANES), jnp.bfloat16)] * groups
        + [jax.ShapeDtypeStruct((1, rows), jnp.int32)],
        [
            pltpu.VMEM((rows, width), embeddings.dtype),
            pltpu.VMEM((rows, width), jnp.bfloat16),
            pltpu.SemaphoreType.DMA((4,)),
        ],
        (embeddings, code.reshape(1, rows)),
        2 * rows * slots * width,
        4 * rows * width,
        [pl.BlockSpec(memory_space=pltpu.HBM), pl.BlockSpec(memory_space=pltpu.VMEM)],
        53 * MIB,
    )

    late = [groups - 1] if groups > 1 else []
    early = list(range(groups - len(late)))
    near = [r for r in range(1, roles) if 2 * offsets[r] != shards]
    far = [r for r in range(1, roles) if r not in near]
    first = {r: from_offset(send[0], offsets[r]) for r in near}
    own = exchange(send, True)
    held = [[None] * groups for _ in offsets]
    held[0] = [(x, None) for x in own]
    for r in near:
        held[r][0] = (first[r], None)
    for ks, wait in ((early[1:], WAIT), (late, WAIT)):
        if ks:
            passed = []
            block = stack([after(own[k], *passed) for k in ks], wait)
            for r in near:
                got = from_offset(block, offsets[r])
                for i, k in enumerate(ks):
                    held[r][k] = (got, i)
    got = {r: from_offset(stack(own, 0), offsets[r]) for r in far}
    everything = [(0, 0, False)]
    everything += [(offsets.index(a), offsets.index(b), both) for a, b, both in pairs]
    steps = [[], [], []]
    for left, right, both in everything:
        for left_ks in (early, late):
            for right_ks in (early, late):
                if left_ks and right_ks:
                    step = 0
                    for role, ks in ((left, left_ks), (right, right_ks)):
                        if role in far:
                            step = max(step, 1)
                        elif ks is late:
                            step = max(step, 2 if role else 1)
                    steps[step].append((left, left_ks, right, right_ks, both))
    steps = [tasks for tasks in steps if tasks]
    acc = []
    for i, tasks in enumerate(steps):
        if i == 1:
            for r in far:
                held[r] = [(got[r], k) for k in range(groups)]
        acc, partial = score(held, tasks, acc, i == len(steps) - 1, slots, width)

    others = [from_offset(partial[r], -offsets[r]) for r in range(1, roles)]
    best = call(
        lambda *refs: merge_kernel(roles, *refs),
        [jax.ShapeDtypeStruct((1, capacity), jnp.float32)] * groups,
        [],
        [partial[0]] + others,
        roles * slots,
        4 * roles * slots,
    )
    back = exchange(best)
    (result,) = call(
        lambda *refs: place_kernel(groups, *refs),
        [jax.ShapeDtypeStruct((1, rows), jnp.float32)],
        [],
        back[::-1] + [place],
        rows * slots,
        4 * slots,
    )
    return result.reshape(rows)


def solution(mesh):
    placed = (P(("shard", "group"), None), P(("shard", "group"), None), P(("shard", "group")))
    return jax.shard_map(
        per_device, mesh=mesh, in_specs=placed, out_specs=P(("shard", "group")), check_vma=False
    )
```

```python
import jax
import jax.numpy as jnp
from jax import lax
from jax.experimental import pallas as pl
from jax.experimental.pallas import tpu as pltpu
from jax.sharding import PartitionSpec as P

LANES = 128
TAIL = 16
LOW = -2.0
MIB = 1024 * 1024
WAIT = 2 * 10**10


def ring_order(size):
    if size % 2:
        return list(range(size))
    half = size // 2
    chips = [i ^ (i >> 1) for i in range(half)]
    if sorted(chips) != list(range(half)):
        chips = list(range(half))
    return [2 * chip + core for core in range(2) for chip in chips]


def offset_cover(size):
    offsets = list(dict.fromkeys([0, size // 2, 1 % size, (size - 1) % size]))

    def missing(chosen):
        have = {(a - b) % size for a in chosen for b in chosen}
        return [d for d in range(size) if d not in have]

    while missing(offsets):
        offsets.append(min(range(size), key=lambda x: len(missing(offsets + [x]))))
    pairs = []
    for diff in range(1, size // 2 + 1):
        found = [
            (a, b)
            for b in [(size - 1) % size] + offsets
            for a in offsets
            if (a - b) % size in (diff, size - diff)
        ]
        if 2 * diff == size:
            found = [(a, b) for a, b in found if b == 0] + found
        a, b = found[0]
        pairs.append((a, b, b != 0 or 2 * diff != size))
    return offsets, pairs


def column_of(row):
    size = row.shape[1]
    return jnp.transpose(jnp.broadcast_to(row, (size, size)))


def sort_kernel(axis, far_ref, code_ref, *refs):
    *block_refs, place_ref, near_ref, unit_ref, sems = refs
    rows, width = near_ref.shape
    groups = len(block_refs)
    capacity = (block_refs[0].shape[0] - TAIL) * LANES // width
    slots = groups * capacity
    chunks = width // LANES
    parts = sems.shape[0]
    size = rows // parts
    copies = [
        pltpu.make_async_copy(
            far_ref.at[pl.ds(i * size, size), :], near_ref.at[pl.ds(i * size, size), :], sems.at[i]
        )
        for i in range(parts)
    ]
    for copy in copies:
        copy.start()
    code = code_ref[...]
    shift = (code - lax.axis_index(axis)) & (groups - 1)
    rel = jnp.maximum(jnp.where(2 * shift > groups, 2 * (groups - shift), 2 * shift - 1), 0)
    label = code >> (groups.bit_length() - 1)
    lines = max(8, groups)
    onehot = lax.broadcasted_iota(jnp.int32, (lines, rows), 0) == rel
    before = lax.broadcasted_iota(jnp.int32, (rows, rows), 0) < lax.broadcasted_iota(
        jnp.int32, (rows, rows), 1
    )
    ranks = jnp.dot(
        jnp.where(onehot, 1.0, 0.0).astype(jnp.bfloat16),
        jnp.where(before, 1.0, 0.0).astype(jnp.bfloat16),
        preferred_element_type=jnp.float32,
    )
    rank = jnp.sum(jnp.where(onehot, ranks, 0.0), axis=0, keepdims=True)
    place = rel * capacity + rank.astype(jnp.int32)
    place_ref[...] = place
    move = jnp.where(
        lax.broadcasted_iota(jnp.int32, (slots, rows), 0) == place, 1.0, 0.0
    ).astype(jnp.bfloat16)
    labels = jnp.broadcast_to(label + 1, (TAIL, rows)).astype(jnp.bfloat16)
    sorted_labels = (
        lax.dot_general(
            labels, move, (((1,), (1,)), ((), ())), preferred_element_type=jnp.float32
        )
        - 1.0
    ).astype(jnp.bfloat16)
    for i, copy in enumerate(copies):
        copy.wait()
        feats = near_ref[pl.ds(i * size, size), :].astype(jnp.float32)
        squares = jnp.sum(feats * feats, axis=1, keepdims=True) + 1e-06
        unit_ref[pl.ds(i * size, size), :] = (feats * lax.rsqrt(squares)).astype(jnp.bfloat16)
    for k, block_ref in enumerate(block_refs):
        part = slice(k * capacity, (k + 1) * capacity)
        block = jnp.dot(
            move[part], unit_ref[...], preferred_element_type=jnp.float32
        ).astype(jnp.bfloat16)
        for c in range(chunks):
            block_ref[pl.ds(c * capacity, capacity), :] = block[:, c * LANES : (c + 1) * LANES]
        block_ref[pl.ds(chunks * capacity, TAIL), :] = sorted_labels[:, part]


def stack_kernel(*refs):
    for k, ref in enumerate(refs[:-1]):
        refs[-1][k] = ref[...]


def score_kernel(sources, tasks, groups, done, first, *refs):
    *refs, flat_ref, side_ref = refs
    outs = 2 + len(done)
    inputs, (row_ref, column_ref, *out_refs) = refs[:-outs], refs[-outs:]
    capacity = LANES
    slots = groups * capacity
    low = jnp.float32(LOW)
    if first:
        row_ref[...] = jnp.full(row_ref.shape, low)
        column_ref[...] = jnp.full(column_ref.shape, low)
    else:
        *inputs, old_rows, old_columns = inputs
        row_ref[...] = old_rows[...]
        column_ref[...] = old_columns[...]
    tops = {}
    for (role, k), (index, part) in sources.items():
        ref = inputs[index] if part is None else inputs[index].at[part]
        height = ref.shape[0] - TAIL
        rows = pl.ds(k * capacity, capacity)
        for c in range(height // capacity):
            flat_ref[role, rows, pl.ds(c * LANES, LANES)] = ref[pl.ds(c * capacity, capacity), :]
        tops[role, k] = ref[pl.ds(height, TAIL), :][0:1].astype(jnp.float32)
    for role, k in sorted({(left, k) for left, ks, _, _, _ in tasks for k in ks}):
        side_ref[role, pl.ds(k * capacity, capacity), :] = column_of(tops[role, k])
    for left, left_ks, right, right_ks, want_rows in tasks:
        start, count = left_ks[0] * capacity, len(left_ks) * capacity
        rows = pl.ds(start, count)
        for i in range(0, len(right_ks), 2):
            some = right_ks[i : i + 2]
            width = len(some) * capacity
            columns = pl.ds(some[0] * capacity, width)
            scores = lax.dot_general(
                flat_ref[left, rows, :],
                flat_ref[right, columns, :],
                (((1,), (1,)), ((), ())),
                preferred_element_type=jnp.float32,
            )
            top = jnp.concatenate([tops[right, k] for k in some], axis=1)
            same = jnp.concatenate([side_ref[left, rows, :]] * len(some), axis=1) == top
            if left == right:
                same = same & (
                    lax.broadcasted_iota(jnp.int32, (count, width), 0) + start
                    != lax.broadcasted_iota(jnp.int32, (count, width), 1) + some[0] * capacity
                )
            scores = jnp.where(same, scores, low)
            if want_rows:
                best = row_ref[left, rows, :]
                for c in range(len(some)):
                    best = jnp.maximum(best, scores[:, c * LANES : (c + 1) * LANES])
                row_ref[left, rows, :] = best
            best = jnp.max(scores.reshape(count // 8, 8, width), axis=0)
            column_ref[right, :, columns] = jnp.maximum(column_ref[right, :, columns], best)
    for role, out_ref in zip(done, out_refs):
        best = jnp.max(column_ref[role], axis=0, keepdims=True)
        turned = [
            jnp.max(
                jnp.transpose(row_ref[role, pl.ds(k * capacity, capacity), :]),
                axis=0,
                keepdims=True,
            )
            for k in range(groups)
        ]
        out_ref[...] = jnp.maximum(best, jnp.concatenate(turned, axis=1))


def merge_kernel(roles, *refs):
    best = refs[0][...]
    for r in range(1, roles):
        best = jnp.maximum(best, refs[r][...])
    best = jnp.maximum(best, jnp.float32(-1.0))
    for k, out_ref in enumerate(refs[roles:]):
        out_ref[...] = best[:, k * LANES : (k + 1) * LANES]


def place_kernel(groups, *refs):
    place = refs[groups][...]
    rows = place.shape[1]
    best = jnp.full((1, rows), jnp.float32(LOW))
    for k in range(groups):
        values = jnp.concatenate([column_of(refs[groups - 1 - k][...])] * (rows // LANES), axis=1)
        here = lax.broadcasted_iota(jnp.int32, (LANES, rows), 0) + k * LANES == place
        best = jnp.maximum(
            best, jnp.max(jnp.where(here, values, jnp.float32(LOW)), axis=0, keepdims=True)
        )
    refs[groups + 1][...] = best


def in_vmem(count):
    return [pl.BlockSpec(memory_space=pltpu.VMEM)] * count


def call(
    kernel, out_shape, scratch, args, flops, bytes_accessed, in_specs=None, limit=48 * MIB, aliases=None
):
    return pl.pallas_call(
        kernel,
        out_shape=out_shape,
        in_specs=in_specs or in_vmem(len(args)),
        out_specs=in_vmem(len(out_shape)),
        scratch_shapes=scratch,
        input_output_aliases=aliases or {},
        compiler_params=pltpu.CompilerParams(vmem_limit_bytes=limit),
        cost_estimate=pl.CostEstimate(
            flops=flops, bytes_accessed=bytes_accessed, transcendentals=0
        ),
    )(*args)


def after(x, *earlier):
    return lax.optimization_barrier((x, *earlier))[0]


def stack(parts, wait):
    return call(
        stack_kernel,
        [jax.ShapeDtypeStruct((len(parts), *parts[0].shape), parts[0].dtype)],
        [],
        parts,
        wait,
        4 * len(parts) * parts[0].size,
    )[0]


def score(held, tasks, acc, done, slots, width):
    roles, groups = len(held), len(held[0])
    used = sorted(
        {(left, k) for left, ks, _, _, _ in tasks for k in ks}
        | {(right, k) for _, _, right, ks, _ in tasks for k in ks},
        key=lambda x: (x[0], -x[1]),
    )
    arrays, sources = [], {}
    for role, k in used:
        array, part = held[role][k]
        index = next((i for i, x in enumerate(arrays) if x is array), len(arrays))
        if index == len(arrays):
            arrays.append(array)
        sources[role, k] = (index, part)
    states = [
        jax.ShapeDtypeStruct((roles, slots, LANES), jnp.float32),
        jax.ShapeDtypeStruct((roles, 8, slots), jnp.float32),
    ]
    ends = [jax.ShapeDtypeStruct((1, slots), jnp.float32)] * len(done)
    tiles = sum(len(task[1]) * len(task[3]) for task in tasks)
    count = len(arrays)
    got = call(
        lambda *refs: score_kernel(sources, tasks, groups, done, not acc, *refs),
        states + ends,
        [
            pltpu.VMEM((roles, slots, width), jnp.bfloat16),
            pltpu.VMEM((roles, slots, LANES), jnp.float32),
        ],
        arrays + list(acc),
        2 * tiles * LANES * LANES * width,
        2 * len(used) * LANES * width,
        aliases={count: 0, count + 1: 1} if acc else {},
    )
    return got[:2], got[2:]


def per_device(embeddings, row_group, row_cluster):
    rows, width = embeddings.shape
    groups = lax.axis_size("group")
    shards = lax.axis_size("shard")
    capacity = rows // 4
    slots = groups * capacity
    ring = ring_order(shards)
    offsets, pairs = offset_cover(shards)
    roles = len(offsets)
    height = width * capacity // LANES + TAIL

    def from_offset(x, offset):
        perm = [(ring[(e + offset) % shards], ring[e]) for e in range(shards)]
        return lax.ppermute(x, "shard", perm)

    def exchange(blocks, way, last=()):
        got = list(blocks)
        for k in range(1, groups):
            shift = way * ((k + 1) // 2 if k % 2 else -(k // 2))
            block = after(blocks[k], got[1]) if last and k > 2 else blocks[k]
            got[k] = lax.ppermute(block, "group", [(z, (z + shift) % groups) for z in range(groups)])
        return got

    code = row_cluster * groups + row_group[:, 0]
    *send, place = call(
        lambda *refs: sort_kernel("group", *refs),
        [jax.ShapeDtypeStruct((height, LANES), jnp.bfloat16)] * groups
        + [jax.ShapeDtypeStruct((1, rows), jnp.int32)],
        [
            pltpu.VMEM((rows, width), embeddings.dtype),
            pltpu.VMEM((rows, width), jnp.bfloat16),
            pltpu.SemaphoreType.DMA((4,)),
        ],
        (embeddings, code.reshape(1, rows)),
        2 * rows * slots * width,
        4 * rows * width,
        [pl.BlockSpec(memory_space=pltpu.HBM), pl.BlockSpec(memory_space=pltpu.VMEM)],
        53 * MIB,
    )

    late = [groups - 1] if groups > 1 else []
    early = list(range(groups - len(late)))
    near = [r for r in range(1, roles) if 2 * offsets[r] != shards]
    far = [r for r in range(1, roles) if r not in near]
    first = {r: from_offset(send[0], offsets[r]) for r in near}
    own = exchange(send, 1, True)
    held = [[None] * groups for _ in offsets]
    held[0] = [(x, None) for x in own]
    for r in near:
        held[r][0] = (first[r], None)
    for ks, wait in ((early[1:], WAIT), (late, WAIT)):
        if ks:
            passed = []
            block = stack([after(own[k], *passed) for k in ks], wait)
            for r in near:
                got = from_offset(block, offsets[r])
                for i, k in enumerate(ks):
                    held[r][k] = (got, i)
    got = {r: from_offset(stack(own, 0), offsets[r]) for r in far}
    everything = [(0, 0, False)]
    everything += [(offsets.index(a), offsets.index(b), both) for a, b, both in pairs]
    steps = [[] for _ in range(4)]
    final = [0] * roles
    for left, right, both in everything:
        for left_ks in (early, late):
            for right_ks in (early, late):
                if left_ks and right_ks:
                    step = 0
                    for role, ks in ((left, left_ks), (right, right_ks)):
                        if role in far:
                            step = max(step, 1)
                        elif ks is late:
                            step = max(step, (3 if role == near[0] else 2) if role else 1)
                    steps[step].append((left, left_ks, right, right_ks, both))
                    final[right] = max(final[right], step)
                    if both:
                        final[left] = max(final[left], step)
    acc, partial = [], [None] * roles
    for step, tasks in enumerate(steps):
        if tasks:
            if step == 1:
                for r in far:
                    held[r] = [(got[r], k) for k in range(groups)]
            done = [r for r in range(roles) if final[r] == step]
            acc, ends = score(held, tasks, acc, done, slots, width)
            for r, end in zip(done, ends):
                partial[r] = end

    others = [from_offset(partial[r], -offsets[r]) for r in range(1, roles)]
    best = call(
        lambda *refs: merge_kernel(roles, *refs),
        [jax.ShapeDtypeStruct((1, capacity), jnp.float32)] * groups,
        [],
        [partial[0]] + others,
        roles * slots,
        4 * roles * slots,
    )
    back = exchange(best, -1)
    (result,) = call(
        lambda *refs: place_kernel(groups, *refs),
        [jax.ShapeDtypeStruct((1, rows), jnp.float32)],
        [],
        back[::-1] + [place],
        rows * slots,
        4 * slots,
    )
    return result.reshape(rows)


def solution(mesh):
    placed = (P(("shard", "group"), None), P(("shard", "group"), None), P(("shard", "group")))
    return jax.shard_map(
        per_device, mesh=mesh, in_specs=placed, out_specs=P(("shard", "group")), check_vma=False
    )
```

```python
import jax
import jax.numpy as jnp
from jax import lax
from jax.experimental import pallas as pl
from jax.experimental.pallas import tpu as pltpu
from jax.sharding import PartitionSpec as P

LANES = 128
TAIL = 16
LOW = -2.0
MIB = 1024 * 1024
WAIT = 2 * 10**10


def ring_order(size):
    if size % 2:
        return list(range(size))
    half = size // 2
    chips = [i ^ (i >> 1) for i in range(half)]
    if sorted(chips) != list(range(half)):
        chips = list(range(half))
    return [2 * chip + core for core in range(2) for chip in chips]


def offset_cover(size):
    offsets = list(dict.fromkeys([0, size // 2, 1 % size, (size - 1) % size]))

    def missing(chosen):
        have = {(a - b) % size for a in chosen for b in chosen}
        return [d for d in range(size) if d not in have]

    while missing(offsets):
        offsets.append(min(range(size), key=lambda x: len(missing(offsets + [x]))))
    pairs = []
    for diff in range(1, size // 2 + 1):
        found = [
            (a, b)
            for b in [(size - 1) % size] + offsets
            for a in offsets
            if (a - b) % size in (diff, size - diff)
        ]
        if 2 * diff == size:
            found = [(a, b) for a, b in found if b == 0] + found
        a, b = found[0]
        pairs.append((a, b, b != 0 or 2 * diff != size))
    return offsets, pairs


def column_of(row):
    size = row.shape[1]
    return jnp.transpose(jnp.broadcast_to(row, (size, size)))


def sort_kernel(axis, far_ref, code_ref, *refs):
    *block_refs, place_ref, near_ref, unit_ref, sems = refs
    rows, width = near_ref.shape
    groups = len(block_refs)
    capacity = (block_refs[0].shape[0] - TAIL) * LANES // width
    slots = groups * capacity
    chunks = width // LANES
    parts = sems.shape[0]
    size = rows // parts
    copies = [
        pltpu.make_async_copy(
            far_ref.at[pl.ds(i * size, size), :], near_ref.at[pl.ds(i * size, size), :], sems.at[i]
        )
        for i in range(parts)
    ]
    for copy in copies:
        copy.start()
    code = code_ref[...]
    shift = (code - lax.axis_index(axis)) & (groups - 1)
    rel = jnp.maximum(jnp.where(2 * shift > groups, 2 * (groups - shift), 2 * shift - 1), 0)
    label = code >> (groups.bit_length() - 1)
    lines = max(8, groups)
    onehot = lax.broadcasted_iota(jnp.int32, (lines, rows), 0) == rel
    before = lax.broadcasted_iota(jnp.int32, (rows, rows), 0) < lax.broadcasted_iota(
        jnp.int32, (rows, rows), 1
    )
    ranks = jnp.dot(
        jnp.where(onehot, 1.0, 0.0).astype(jnp.bfloat16),
        jnp.where(before, 1.0, 0.0).astype(jnp.bfloat16),
        preferred_element_type=jnp.float32,
    )
    rank = jnp.sum(jnp.where(onehot, ranks, 0.0), axis=0, keepdims=True)
    place = rel * capacity + rank.astype(jnp.int32)
    place_ref[...] = place
    move = jnp.where(
        lax.broadcasted_iota(jnp.int32, (slots, rows), 0) == place, 1.0, 0.0
    ).astype(jnp.bfloat16)
    labels = jnp.broadcast_to(label + 1, (TAIL, rows)).astype(jnp.bfloat16)
    sorted_labels = (
        lax.dot_general(
            labels, move, (((1,), (1,)), ((), ())), preferred_element_type=jnp.float32
        )
        - 1.0
    ).astype(jnp.bfloat16)
    for i, copy in enumerate(copies):
        copy.wait()
        feats = near_ref[pl.ds(i * size, size), :].astype(jnp.float32)
        squares = jnp.sum(feats * feats, axis=1, keepdims=True) + 1e-06
        unit_ref[pl.ds(i * size, size), :] = (feats * lax.rsqrt(squares)).astype(jnp.bfloat16)
    for k, block_ref in enumerate(block_refs):
        part = slice(k * capacity, (k + 1) * capacity)
        block = jnp.dot(
            move[part], unit_ref[...], preferred_element_type=jnp.float32
        ).astype(jnp.bfloat16)
        for c in range(chunks):
            block_ref[pl.ds(c * capacity, capacity), :] = block[:, c * LANES : (c + 1) * LANES]
        block_ref[pl.ds(chunks * capacity, TAIL), :] = sorted_labels[:, part]


def stack_kernel(*refs):
    for k, ref in enumerate(refs[:-1]):
        refs[-1][k] = ref[...]


def score_kernel(sources, tasks, turns, done, first, *refs):
    *refs, flat_ref, side_ref = refs
    outs = 2 + len(done)
    inputs, (row_ref, column_ref, *out_refs) = refs[:-outs], refs[-outs:]
    capacity = LANES
    low = jnp.float32(LOW)
    if first:
        row_ref[...] = jnp.full(row_ref.shape, low)
        column_ref[...] = jnp.full(column_ref.shape, low)
    else:
        *inputs, old_rows, old_columns = inputs
        row_ref[...] = old_rows[...]
        column_ref[...] = old_columns[...]
    tops = {}
    for (role, k), (index, part) in sources.items():
        ref = inputs[index] if part is None else inputs[index].at[part]
        height = ref.shape[0] - TAIL
        rows = pl.ds(k * capacity, capacity)
        for c in range(height // capacity):
            flat_ref[role, rows, pl.ds(c * LANES, LANES)] = ref[pl.ds(c * capacity, capacity), :]
        tops[role, k] = ref[pl.ds(height, TAIL), :][0:1].astype(jnp.float32)
    for role, k in sorted({(left, k) for left, ks, _, _, _ in tasks for k in ks}):
        side_ref[role, pl.ds(k * capacity, capacity), :] = column_of(tops[role, k])
    for left, left_ks, right, right_ks, want_rows in tasks:
        start, count = left_ks[0] * capacity, len(left_ks) * capacity
        rows = pl.ds(start, count)
        for i in range(0, len(right_ks), 2):
            some = right_ks[i : i + 2]
            width = len(some) * capacity
            columns = pl.ds(some[0] * capacity, width)
            scores = lax.dot_general(
                flat_ref[left, rows, :],
                flat_ref[right, columns, :],
                (((1,), (1,)), ((), ())),
                preferred_element_type=jnp.float32,
            )
            top = jnp.concatenate([tops[right, k] for k in some], axis=1)
            same = jnp.concatenate([side_ref[left, rows, :]] * len(some), axis=1) == top
            if left == right:
                same = same & (
                    lax.broadcasted_iota(jnp.int32, (count, width), 0) + start
                    != lax.broadcasted_iota(jnp.int32, (count, width), 1) + some[0] * capacity
                )
            scores = jnp.where(same, scores, low)
            if want_rows:
                best = row_ref[left, rows, :]
                for c in range(len(some)):
                    best = jnp.maximum(best, scores[:, c * LANES : (c + 1) * LANES])
                row_ref[left, rows, :] = best
            best = jnp.max(scores.reshape(count // 8, 8, width), axis=0)
            column_ref[right, :, columns] = jnp.maximum(column_ref[right, :, columns], best)
    for role, k in turns:
        rows = pl.ds(k * capacity, capacity)
        turned = jnp.transpose(row_ref[role, rows, :]).reshape(capacity // 8, 8, capacity)
        column_ref[role, :, rows] = jnp.maximum(column_ref[role, :, rows], jnp.max(turned, axis=0))
    for role, out_ref in zip(done, out_refs):
        out_ref[...] = jnp.max(column_ref[role], axis=0, keepdims=True)


def merge_kernel(roles, *refs):
    best = refs[0][...]
    for r in range(1, roles):
        best = jnp.maximum(best, refs[r][...])
    best = jnp.maximum(best, jnp.float32(-1.0))
    for k, out_ref in enumerate(refs[roles:]):
        out_ref[...] = best[:, k * LANES : (k + 1) * LANES]


def place_kernel(groups, *refs):
    place = refs[groups][...]
    rows = place.shape[1]
    best = jnp.full((1, rows), jnp.float32(LOW))
    for k in range(groups):
        values = jnp.concatenate([column_of(refs[groups - 1 - k][...])] * (rows // LANES), axis=1)
        here = lax.broadcasted_iota(jnp.int32, (LANES, rows), 0) + k * LANES == place
        best = jnp.maximum(
            best, jnp.max(jnp.where(here, values, jnp.float32(LOW)), axis=0, keepdims=True)
        )
    refs[groups + 1][...] = best


def in_vmem(count):
    return [pl.BlockSpec(memory_space=pltpu.VMEM)] * count


def call(
    kernel, out_shape, scratch, args, flops, bytes_accessed, in_specs=None, limit=48 * MIB, aliases=None
):
    return pl.pallas_call(
        kernel,
        out_shape=out_shape,
        in_specs=in_specs or in_vmem(len(args)),
        out_specs=in_vmem(len(out_shape)),
        scratch_shapes=scratch,
        input_output_aliases=aliases or {},
        compiler_params=pltpu.CompilerParams(vmem_limit_bytes=limit),
        cost_estimate=pl.CostEstimate(
            flops=flops, bytes_accessed=bytes_accessed, transcendentals=0
        ),
    )(*args)


def after(x, *earlier):
    return lax.optimization_barrier((x, *earlier))[0]


def stack(parts, wait):
    return call(
        stack_kernel,
        [jax.ShapeDtypeStruct((len(parts), *parts[0].shape), parts[0].dtype)],
        [],
        parts,
        wait,
        4 * len(parts) * parts[0].size,
    )[0]


def score(held, tasks, turns, acc, done, slots, width):
    roles = len(held)
    used = sorted(
        {(left, k) for left, ks, _, _, _ in tasks for k in ks}
        | {(right, k) for _, _, right, ks, _ in tasks for k in ks},
        key=lambda x: (x[0], -x[1]),
    )
    arrays, sources = [], {}
    for role, k in used:
        array, part = held[role][k]
        index = next((i for i, x in enumerate(arrays) if x is array), len(arrays))
        if index == len(arrays):
            arrays.append(array)
        sources[role, k] = (index, part)
    states = [
        jax.ShapeDtypeStruct((roles, slots, LANES), jnp.float32),
        jax.ShapeDtypeStruct((roles, 8, slots), jnp.float32),
    ]
    ends = [jax.ShapeDtypeStruct((1, slots), jnp.float32)] * len(done)
    tiles = sum(len(task[1]) * len(task[3]) for task in tasks)
    got = call(
        lambda *refs: score_kernel(sources, tasks, turns, done, not acc, *refs),
        states + ends,
        [
            pltpu.VMEM((roles, slots, width), jnp.bfloat16),
            pltpu.VMEM((roles, slots, LANES), jnp.float32),
        ],
        arrays + list(acc),
        2 * tiles * LANES * LANES * width,
        2 * len(used) * LANES * width,
        aliases={len(arrays) + i: i for i in range(len(acc))},
    )
    return got[: len(states)], got[len(states) :]


def per_device(embeddings, row_group, row_cluster):
    rows, width = embeddings.shape
    groups = lax.axis_size("group")
    shards = lax.axis_size("shard")
    capacity = rows // 4
    slots = groups * capacity
    ring = ring_order(shards)
    offsets, pairs = offset_cover(shards)
    roles = len(offsets)
    height = width * capacity // LANES + TAIL

    def from_offset(x, offset):
        perm = [(ring[(e + offset) % shards], ring[e]) for e in range(shards)]
        return lax.ppermute(x, "shard", perm)

    def exchange(blocks, way, stagger=False):
        got = list(blocks)
        for k in range(1, groups):
            shift = way * ((k + 1) // 2 if k % 2 else -(k // 2))
            block = after(blocks[k], got[1]) if stagger and k > 2 else blocks[k]
            got[k] = lax.ppermute(block, "group", [(z, (z + shift) % groups) for z in range(groups)])
        return got

    code = row_cluster * groups + row_group[:, 0]
    *send, place = call(
        lambda *refs: sort_kernel("group", *refs),
        [jax.ShapeDtypeStruct((height, LANES), jnp.bfloat16)] * groups
        + [jax.ShapeDtypeStruct((1, rows), jnp.int32)],
        [
            pltpu.VMEM((rows, width), embeddings.dtype),
            pltpu.VMEM((rows, width), jnp.bfloat16),
            pltpu.SemaphoreType.DMA((4,)),
        ],
        (embeddings, code.reshape(1, rows)),
        2 * rows * slots * width,
        4 * rows * width,
        [pl.BlockSpec(memory_space=pltpu.HBM), pl.BlockSpec(memory_space=pltpu.VMEM)],
        53 * MIB,
    )

    late = [groups - 1] if groups > 1 else []
    early = list(range(groups - len(late)))
    late = [groups - 1] if groups > 1 else []
    early = list(range(groups - len(late)))
    near = [r for r in range(1, roles) if 2 * offsets[r] != shards]
    far = [r for r in range(1, roles) if r not in near]
    first = {r: from_offset(send[0], offsets[r]) for r in near}
    own = exchange(send, 1, True)
    held = [[None] * groups for _ in offsets]
    held[0] = [(x, None) for x in own]
    for r in near:
        held[r][0] = (first[r], None)
    for k in range(1, groups):
        if k == 1:
            block = after(own[k], first[near[0]]) if near else own[k]
        else:
            passed = [held[r][k - 2][0] for r in near]
            block = stack([after(own[k], *passed)], WAIT if k in late else WAIT // 20)
        for r in near:
            held[r][k] = (from_offset(block, offsets[r]), 0 if k > 1 else None)
    got = {r: from_offset(stack(own, 0), offsets[r]) for r in far}
    everything = [(0, 0, False)]
    everything += [(offsets.index(a), offsets.index(b), both) for a, b, both in pairs]
    steps = [[] for _ in range(4)]
    turn, final = {}, [0] * roles
    for left, right, both in everything:
        for left_ks in (early, late):
            for right_ks in (early, late):
                if left_ks and right_ks:
                    step = 0
                    for role, ks in ((left, left_ks), (right, right_ks)):
                        if role in far:
                            step = max(step, 1)
                        elif ks is late:
                            step = max(step, (3 if role == near[0] else 2) if role else 1)
                    steps[step].append((left, left_ks, right, right_ks, both))
                    final[right] = max(final[right], step)
                    if both:
                        final[left] = max(final[left], step)
                        for k in left_ks:
                            turn[left, k] = max(turn.get((left, k), step), step)
    acc, partial = [], [None] * roles
    for step, tasks in enumerate(steps):
        if tasks:
            if step == 1:
                for r in far:
                    held[r] = [(got[r], k) for k in range(groups)]
            done = [r for r in range(roles) if final[r] == step]
            turns = sorted(x for x in turn if turn[x] == step)
            acc, ends = score(held, tasks, turns, acc, done, slots, width)
            for r, end in zip(done, ends):
                partial[r] = end

    others = [from_offset(partial[r], -offsets[r]) for r in range(1, roles)]
    best = call(
        lambda *refs: merge_kernel(roles, *refs),
        [jax.ShapeDtypeStruct((1, capacity), jnp.float32)] * groups,
        [],
        [partial[0]] + others,
        roles * slots,
        4 * roles * slots,
    )
    back = exchange(best, -1)
    (result,) = call(
        lambda *refs: place_kernel(groups, *refs),
        [jax.ShapeDtypeStruct((1, rows), jnp.float32)],
        [],
        back[::-1] + [place],
        rows * slots,
        4 * slots,
    )
    return result.reshape(rows)


def solution(mesh):
    placed = (P(("shard", "group"), None), P(("shard", "group"), None), P(("shard", "group")))
    return jax.shard_map(
        per_device, mesh=mesh, in_specs=placed, out_specs=P(("shard", "group")), check_vma=False
    )
```

```python
import jax
import jax.numpy as jnp
from jax import lax
from jax.experimental import pallas as pl
from jax.experimental.pallas import tpu as pltpu
from jax.sharding import PartitionSpec as P

LANES = 128
TAIL = 16
LOW = -2.0
MIB = 1024 * 1024
WAIT = 2 * 10**10


def ring_order(size):
    if size % 2:
        return list(range(size))
    half = size // 2
    chips = [i ^ (i >> 1) for i in range(half)]
    if sorted(chips) != list(range(half)):
        chips = list(range(half))
    return [2 * chip + core for core in range(2) for chip in chips]


def offset_cover(size):
    offsets = list(dict.fromkeys([0, size // 2, 1 % size, (size - 1) % size]))

    def missing(chosen):
        have = {(a - b) % size for a in chosen for b in chosen}
        return [d for d in range(size) if d not in have]

    while missing(offsets):
        offsets.append(min(range(size), key=lambda x: len(missing(offsets + [x]))))
    pairs = []
    for diff in range(1, size // 2 + 1):
        found = [
            (a, b)
            for b in [(size - 1) % size] + offsets
            for a in offsets
            if (a - b) % size in (diff, size - diff)
        ]
        if 2 * diff == size:
            found = [(a, b) for a, b in found if b == 0] + found
        a, b = found[0]
        pairs.append((a, b, b != 0 or 2 * diff != size))
    return offsets, pairs


def column_of(row):
    size = row.shape[1]
    return jnp.transpose(jnp.broadcast_to(row, (size, size)))


def sort_kernel(axis, far_ref, code_ref, *refs):
    *block_refs, place_ref, near_ref, unit_ref, sems = refs
    rows, width = near_ref.shape
    groups = len(block_refs)
    capacity = (block_refs[0].shape[0] - TAIL) * LANES // width
    slots = groups * capacity
    chunks = width // LANES
    parts = sems.shape[0]
    size = rows // parts
    copies = [
        pltpu.make_async_copy(
            far_ref.at[pl.ds(i * size, size), :], near_ref.at[pl.ds(i * size, size), :], sems.at[i]
        )
        for i in range(parts)
    ]
    for copy in copies:
        copy.start()
    code = code_ref[...]
    shift = (code - lax.axis_index(axis)) & (groups - 1)
    rel = jnp.maximum(jnp.where(2 * shift > groups, 2 * (groups - shift), 2 * shift - 1), 0)
    label = code >> (groups.bit_length() - 1)
    lines = max(8, groups)
    onehot = lax.broadcasted_iota(jnp.int32, (lines, rows), 0) == rel
    before = lax.broadcasted_iota(jnp.int32, (rows, rows), 0) < lax.broadcasted_iota(
        jnp.int32, (rows, rows), 1
    )
    ranks = jnp.dot(
        jnp.where(onehot, 1.0, 0.0).astype(jnp.bfloat16),
        jnp.where(before, 1.0, 0.0).astype(jnp.bfloat16),
        preferred_element_type=jnp.float32,
    )
    rank = jnp.sum(jnp.where(onehot, ranks, 0.0), axis=0, keepdims=True)
    place = rel * capacity + rank.astype(jnp.int32)
    place_ref[...] = (code & (groups - 1)) * capacity + rank.astype(jnp.int32)
    move = jnp.where(
        lax.broadcasted_iota(jnp.int32, (slots, rows), 0) == place, 1.0, 0.0
    ).astype(jnp.bfloat16)
    labels = jnp.broadcast_to(label + 1, (TAIL, rows)).astype(jnp.bfloat16)
    sorted_labels = (
        lax.dot_general(
            labels, move, (((1,), (1,)), ((), ())), preferred_element_type=jnp.float32
        )
        - 1.0
    ).astype(jnp.bfloat16)
    for i, copy in enumerate(copies):
        copy.wait()
        feats = near_ref[pl.ds(i * size, size), :].astype(jnp.float32)
        squares = jnp.sum(feats * feats, axis=1, keepdims=True) + 1e-06
        unit_ref[pl.ds(i * size, size), :] = (feats * lax.rsqrt(squares)).astype(jnp.bfloat16)
    for k, block_ref in enumerate(block_refs):
        part = slice(k * capacity, (k + 1) * capacity)
        block = jnp.dot(
            move[part], unit_ref[...], preferred_element_type=jnp.float32
        ).astype(jnp.bfloat16)
        for c in range(chunks):
            block_ref[pl.ds(c * capacity, capacity), :] = block[:, c * LANES : (c + 1) * LANES]
        block_ref[pl.ds(chunks * capacity, TAIL), :] = sorted_labels[:, part]


def stack_kernel(*refs):
    for k, ref in enumerate(refs[:-1]):
        refs[-1][k] = ref[...]


def score_kernel(sources, tasks, turns, done, first, *refs):
    *refs, flat_ref, side_ref = refs
    outs = 2 + len(done)
    inputs, (row_ref, column_ref, *out_refs) = refs[:-outs], refs[-outs:]
    capacity = LANES
    low = jnp.float32(LOW)
    if first:
        row_ref[...] = jnp.full(row_ref.shape, low)
        column_ref[...] = jnp.full(column_ref.shape, low)
    else:
        *inputs, old_rows, old_columns = inputs
        row_ref[...] = old_rows[...]
        column_ref[...] = old_columns[...]
    tops = {}
    for (role, k), (index, part) in sources.items():
        ref = inputs[index] if part is None else inputs[index].at[part]
        height = ref.shape[0] - TAIL
        rows = pl.ds(k * capacity, capacity)
        for c in range(height // capacity):
            flat_ref[role, rows, pl.ds(c * LANES, LANES)] = ref[pl.ds(c * capacity, capacity), :]
        tops[role, k] = ref[pl.ds(height, TAIL), :][0:1].astype(jnp.float32)
    for role, k in sorted({(left, k) for left, ks, _, _, _ in tasks for k in ks}):
        side_ref[role, pl.ds(k * capacity, capacity), :] = column_of(tops[role, k])
    for left, left_ks, right, right_ks, want_rows in tasks:
        start, count = left_ks[0] * capacity, len(left_ks) * capacity
        rows = pl.ds(start, count)
        for i in range(0, len(right_ks), 2):
            some = right_ks[i : i + 2]
            width = len(some) * capacity
            columns = pl.ds(some[0] * capacity, width)
            scores = lax.dot_general(
                flat_ref[left, rows, :],
                flat_ref[right, columns, :],
                (((1,), (1,)), ((), ())),
                preferred_element_type=jnp.float32,
            )
            top = jnp.concatenate([tops[right, k] for k in some], axis=1)
            same = jnp.concatenate([side_ref[left, rows, :]] * len(some), axis=1) == top
            if left == right:
                same = same & (
                    lax.broadcasted_iota(jnp.int32, (count, width), 0) + start
                    != lax.broadcasted_iota(jnp.int32, (count, width), 1) + some[0] * capacity
                )
            scores = jnp.where(same, scores, low)
            if want_rows:
                best = row_ref[left, rows, :]
                for c in range(len(some)):
                    best = jnp.maximum(best, scores[:, c * LANES : (c + 1) * LANES])
                row_ref[left, rows, :] = best
            best = jnp.max(scores.reshape(count // 8, 8, width), axis=0)
            column_ref[right, :, columns] = jnp.maximum(column_ref[right, :, columns], best)
    for role, k in turns:
        rows = pl.ds(k * capacity, capacity)
        turned = jnp.transpose(row_ref[role, rows, :]).reshape(capacity // 8, 8, capacity)
        column_ref[role, :, rows] = jnp.maximum(column_ref[role, :, rows], jnp.max(turned, axis=0))
    for role, out_ref in zip(done, out_refs):
        out_ref[...] = jnp.max(column_ref[role], axis=0, keepdims=True)


def slot_shift(k):
    return (k + 1) // 2 if k % 2 else -(k // 2)


def spread_kernel(ring, offsets, groups, *refs):
    *partial_refs, out_ref = refs
    shards = len(ring)
    out_ref[...] = jnp.full(out_ref.shape, jnp.float32(LOW))
    shard, group = lax.axis_index("shard"), lax.axis_index("group")
    for offset, ref in zip(offsets, partial_refs):
        target = sum(
            jnp.where(shard == ring[e], ring[(e + offset) % shards], 0) for e in range(shards)
        )
        for k in range(groups):
            row = target * groups + ((group - slot_shift(k)) & (groups - 1))
            out_ref[pl.ds(row, 1)] = ref[:, k * LANES : (k + 1) * LANES].reshape(1, 1, LANES)


def place_kernel(groups, back_ref, place_ref, out_ref):
    place = place_ref[...]
    rows = place.shape[1]
    best = jnp.full((1, rows), jnp.float32(LOW))
    for g in range(groups):
        row = jnp.full((1, LANES), jnp.float32(-1.0))
        for s in range(back_ref.shape[0] // groups):
            row = jnp.maximum(row, back_ref[s * groups + g])
        values = jnp.concatenate([column_of(row)] * (rows // LANES), axis=1)
        here = lax.broadcasted_iota(jnp.int32, (LANES, rows), 0) + g * LANES == place
        best = jnp.maximum(
            best, jnp.max(jnp.where(here, values, jnp.float32(LOW)), axis=0, keepdims=True)
        )
    out_ref[...] = best


def in_vmem(count):
    return [pl.BlockSpec(memory_space=pltpu.VMEM)] * count


def call(
    kernel, out_shape, scratch, args, flops, bytes_accessed, in_specs=None, limit=48 * MIB, aliases=None
):
    return pl.pallas_call(
        kernel,
        out_shape=out_shape,
        in_specs=in_specs or in_vmem(len(args)),
        out_specs=in_vmem(len(out_shape)),
        scratch_shapes=scratch,
        input_output_aliases=aliases or {},
        compiler_params=pltpu.CompilerParams(vmem_limit_bytes=limit),
        cost_estimate=pl.CostEstimate(
            flops=flops, bytes_accessed=bytes_accessed, transcendentals=0
        ),
    )(*args)


def after(x, *earlier):
    return lax.optimization_barrier((x, *earlier))[0]


def stack(parts, wait):
    return call(
        stack_kernel,
        [jax.ShapeDtypeStruct((len(parts), *parts[0].shape), parts[0].dtype)],
        [],
        parts,
        wait,
        4 * len(parts) * parts[0].size,
    )[0]


def score(held, tasks, turns, acc, done, slots, width):
    roles = len(held)
    used = sorted(
        {(left, k) for left, ks, _, _, _ in tasks for k in ks}
        | {(right, k) for _, _, right, ks, _ in tasks for k in ks},
        key=lambda x: (x[0], -x[1]),
    )
    arrays, sources = [], {}
    for role, k in used:
        array, part = held[role][k]
        index = next((i for i, x in enumerate(arrays) if x is array), len(arrays))
        if index == len(arrays):
            arrays.append(array)
        sources[role, k] = (index, part)
    states = [
        jax.ShapeDtypeStruct((roles, slots, LANES), jnp.float32),
        jax.ShapeDtypeStruct((roles, 8, slots), jnp.float32),
    ]
    ends = [jax.ShapeDtypeStruct((1, slots), jnp.float32)] * len(done)
    tiles = sum(len(task[1]) * len(task[3]) for task in tasks)
    got = call(
        lambda *refs: score_kernel(sources, tasks, turns, done, not acc, *refs),
        states + ends,
        [
            pltpu.VMEM((roles, slots, width), jnp.bfloat16),
            pltpu.VMEM((roles, slots, LANES), jnp.float32),
        ],
        arrays + list(acc),
        2 * tiles * LANES * LANES * width,
        2 * len(used) * LANES * width,
        aliases={len(arrays) + i: i for i in range(len(acc))},
    )
    return got[: len(states)], got[len(states) :]


def per_device(embeddings, row_group, row_cluster):
    rows, width = embeddings.shape
    groups = lax.axis_size("group")
    shards = lax.axis_size("shard")
    capacity = rows // 4
    slots = groups * capacity
    ring = ring_order(shards)
    offsets, pairs = offset_cover(shards)
    roles = len(offsets)
    height = width * capacity // LANES + TAIL

    def from_offset(x, offset):
        perm = [(ring[(e + offset) % shards], ring[e]) for e in range(shards)]
        return lax.ppermute(x, "shard", perm)

    def exchange(blocks):
        got = list(blocks)
        for k in range(1, groups):
            shift = slot_shift(k)
            block = after(blocks[k], got[1]) if k > 2 else blocks[k]
            got[k] = lax.ppermute(block, "group", [(z, (z + shift) % groups) for z in range(groups)])
        return got

    code = row_cluster * groups + row_group[:, 0]
    *send, place = call(
        lambda *refs: sort_kernel("group", *refs),
        [jax.ShapeDtypeStruct((height, LANES), jnp.bfloat16)] * groups
        + [jax.ShapeDtypeStruct((1, rows), jnp.int32)],
        [
            pltpu.VMEM((rows, width), embeddings.dtype),
            pltpu.VMEM((rows, width), jnp.bfloat16),
            pltpu.SemaphoreType.DMA((4,)),
        ],
        (embeddings, code.reshape(1, rows)),
        2 * rows * slots * width,
        4 * rows * width,
        [pl.BlockSpec(memory_space=pltpu.HBM), pl.BlockSpec(memory_space=pltpu.VMEM)],
        53 * MIB,
    )

    late = [groups - 1] if groups > 1 else []
    early = list(range(groups - len(late)))
    late = [groups - 1] if groups > 1 else []
    early = list(range(groups - len(late)))
    near = [r for r in range(1, roles) if 2 * offsets[r] != shards]
    far = [r for r in range(1, roles) if r not in near]
    first = {r: from_offset(send[0], offsets[r]) for r in near}
    own = exchange(send)
    held = [[None] * groups for _ in offsets]
    held[0] = [(x, None) for x in own]
    for r in near:
        held[r][0] = (first[r], None)
    for ks, wait in ((early[1:], WAIT), (late, WAIT)):
        if ks:
            block = stack([own[k] for k in ks], wait)
            for r in near:
                moved = from_offset(block, offsets[r])
                for i, k in enumerate(ks):
                    held[r][k] = (moved, i)
    got = {r: from_offset(stack(own, 0), offsets[r]) for r in far}
    everything = [(0, 0, False)]
    everything += [(offsets.index(a), offsets.index(b), both) for a, b, both in pairs]
    steps = [[] for _ in range(4)]
    turn, final = {}, [0] * roles
    for left, right, both in everything:
        for left_ks in (early, late):
            for right_ks in (early, late):
                if left_ks and right_ks:
                    step = 0
                    for role, ks in ((left, left_ks), (right, right_ks)):
                        if role in far:
                            step = max(step, 1)
                        elif ks is late:
                            step = max(step, (3 if role == near[0] else 2) if role else 1)
                    steps[step].append((left, left_ks, right, right_ks, both))
                    final[right] = max(final[right], step)
                    if both:
                        final[left] = max(final[left], step)
                        for k in left_ks:
                            turn[left, k] = max(turn.get((left, k), step), step)
    acc, partial = [], [None] * roles
    for step, tasks in enumerate(steps):
        if tasks:
            if step == 1:
                for r in far:
                    held[r] = [(got[r], k) for k in range(groups)]
            done = [r for r in range(roles) if final[r] == step]
            turns = sorted(x for x in turn if turn[x] == step)
            acc, ends = score(held, tasks, turns, acc, done, slots, width)
            for r, end in zip(done, ends):
                partial[r] = end

    (best,) = call(
        lambda *refs: spread_kernel(ring, offsets, groups, *refs),
        [jax.ShapeDtypeStruct((shards * groups, 1, capacity), jnp.float32)],
        [],
        partial,
        roles * slots,
        4 * roles * slots,
    )
    back = lax.all_to_all(best, ("shard", "group"), split_axis=0, concat_axis=0, tiled=True)
    (result,) = call(
        lambda *refs: place_kernel(groups, *refs),
        [jax.ShapeDtypeStruct((1, rows), jnp.float32)],
        [],
        [back, place],
        rows * slots,
        4 * slots,
    )
    return result.reshape(rows)


def solution(mesh):
    placed = (P(("shard", "group"), None), P(("shard", "group"), None), P(("shard", "group")))
    return jax.shard_map(
        per_device, mesh=mesh, in_specs=placed, out_specs=P(("shard", "group")), check_vma=False
    )
```

```python
import jax
import jax.numpy as jnp
from jax import lax
from jax.experimental import pallas as pl
from jax.experimental.pallas import tpu as pltpu
from jax.sharding import PartitionSpec as P

LANES = 128
TAIL = 16
LOW = -2.0
MIB = 1024 * 1024
WAIT = 2 * 10**10


def ring_order(size):
    if size % 2:
        return list(range(size))
    half = size // 2
    chips = [i ^ (i >> 1) for i in range(half)]
    if sorted(chips) != list(range(half)):
        chips = list(range(half))
    return [2 * chip + core for core in range(2) for chip in chips]


def offset_cover(size):
    offsets = list(dict.fromkeys([0, size // 2, 1 % size, (size - 1) % size]))

    def missing(chosen):
        have = {(a - b) % size for a in chosen for b in chosen}
        return [d for d in range(size) if d not in have]

    while missing(offsets):
        offsets.append(min(range(size), key=lambda x: len(missing(offsets + [x]))))
    pairs = []
    for diff in range(1, size // 2 + 1):
        found = [
            (a, b)
            for b in [(size - 1) % size] + offsets
            for a in offsets
            if (a - b) % size in (diff, size - diff)
        ]
        if 2 * diff == size:
            found = [(a, b) for a, b in found if b == 0] + found
        a, b = found[0]
        pairs.append((a, b, b != 0 or 2 * diff != size))
    return offsets, pairs


def column_of(row):
    size = row.shape[1]
    return jnp.transpose(jnp.broadcast_to(row, (size, size)))


def unit_kernel(far_ref, unit_ref, near_ref, sems):
    parts = sems.shape[0]
    size = far_ref.shape[0] // parts
    copies = [
        pltpu.make_async_copy(
            far_ref.at[pl.ds(i * size, size), :], near_ref.at[pl.ds(i * size, size), :], sems.at[i]
        )
        for i in range(parts)
    ]
    for copy in copies:
        copy.start()
    for i, copy in enumerate(copies):
        copy.wait()
        feats = near_ref[pl.ds(i * size, size), :].astype(jnp.float32)
        squares = jnp.sum(feats * feats, axis=1, keepdims=True) + 1e-06
        unit_ref[pl.ds(i * size, size), :] = (feats * lax.rsqrt(squares)).astype(jnp.bfloat16)


def sort_kernel(axis, unit_ref, group_ref, label_ref, *out_refs):
    *block_refs, place_ref = out_refs
    rows, width = unit_ref.shape
    groups = len(block_refs)
    capacity = (block_refs[0].shape[0] - TAIL) * LANES // width
    slots = groups * capacity
    chunks = width // LANES
    owner = group_ref[...]
    rel = owner ^ lax.axis_index(axis)
    lines = max(8, groups)
    onehot = lax.broadcasted_iota(jnp.int32, (lines, rows), 0) == rel
    before = lax.broadcasted_iota(jnp.int32, (rows, rows), 0) < lax.broadcasted_iota(
        jnp.int32, (rows, rows), 1
    )
    ranks = jnp.dot(
        jnp.where(onehot, 1.0, 0.0).astype(jnp.bfloat16),
        jnp.where(before, 1.0, 0.0).astype(jnp.bfloat16),
        preferred_element_type=jnp.float32,
    )
    rank = jnp.sum(jnp.where(onehot, ranks, 0.0), axis=0, keepdims=True).astype(jnp.int32)
    place_ref[...] = owner * capacity + rank
    move = jnp.where(
        lax.broadcasted_iota(jnp.int32, (slots, rows), 0) == rel * capacity + rank, 1.0, 0.0
    ).astype(jnp.bfloat16)
    labels = jnp.broadcast_to(label_ref[...] + 1, (TAIL, rows)).astype(jnp.bfloat16)
    sorted_labels = (
        lax.dot_general(
            labels, move, (((1,), (1,)), ((), ())), preferred_element_type=jnp.float32
        )
        - 1.0
    ).astype(jnp.bfloat16)
    for k, block_ref in enumerate(block_refs):
        part = slice(k * capacity, (k + 1) * capacity)
        block = jnp.dot(
            move[part], unit_ref[...], preferred_element_type=jnp.float32
        ).astype(jnp.bfloat16)
        for c in range(chunks):
            block_ref[pl.ds(c * capacity, capacity), :] = block[:, c * LANES : (c + 1) * LANES]
        block_ref[pl.ds(chunks * capacity, TAIL), :] = sorted_labels[:, part]


def stack_kernel(*refs):
    for k, ref in enumerate(refs[:-1]):
        refs[-1][k] = ref[...]


def score_kernel(sources, tasks, done, *refs):
    *refs, flat_ref, side_ref, row_ref = refs
    outs = 1 + len(done)
    inputs, (best_ref, *out_refs) = refs[:-outs], refs[-outs:]
    capacity = LANES
    low = jnp.float32(LOW)
    arrays = 1 + max(index for index, _ in sources.values())
    best_ref[...] = inputs[arrays][...] if len(inputs) > arrays else jnp.full(best_ref.shape, low)
    tops = {}
    for (role, k), (index, part) in sources.items():
        ref = inputs[index] if part is None else inputs[index].at[part]
        height = ref.shape[0] - TAIL
        rows = pl.ds(k * capacity, capacity)
        for c in range(height // capacity):
            flat_ref[role, rows, pl.ds(c * LANES, LANES)] = ref[pl.ds(c * capacity, capacity), :]
        tops[role, k] = ref[pl.ds(height, TAIL), :][0:1].astype(jnp.float32)
    for role, k in sorted({(left, k) for left, ks, _, _, _ in tasks for k in ks}):
        side_ref[role, pl.ds(k * capacity, capacity), :] = column_of(tops[role, k])
    turns = sorted({(left, k) for left, ks, _, _, both in tasks if both for k in ks})
    for role, k in turns:
        row_ref[role, pl.ds(k * capacity, capacity), :] = jnp.full((capacity, LANES), low)
    for left, left_ks, right, right_ks, both in tasks:
        start, count = left_ks[0] * capacity, len(left_ks) * capacity
        rows = pl.ds(start, count)
        for i in range(0, len(right_ks), 2):
            some = right_ks[i : i + 2]
            width = len(some) * capacity
            columns = pl.ds(some[0] * capacity, width)
            scores = lax.dot_general(
                flat_ref[left, rows, :],
                flat_ref[right, columns, :],
                (((1,), (1,)), ((), ())),
                preferred_element_type=jnp.float32,
            )
            top = jnp.concatenate([tops[right, k] for k in some], axis=1)
            same = jnp.concatenate([side_ref[left, rows, :]] * len(some), axis=1) == top
            if left == right:
                same = same & (
                    lax.broadcasted_iota(jnp.int32, (count, width), 0) + start
                    != lax.broadcasted_iota(jnp.int32, (count, width), 1) + some[0] * capacity
                )
            scores = jnp.where(same, scores, low)
            if both:
                best = row_ref[left, rows, :]
                for c in range(len(some)):
                    best = jnp.maximum(best, scores[:, c * LANES : (c + 1) * LANES])
                row_ref[left, rows, :] = best
            best = jnp.max(scores.reshape(count // 8, 8, width), axis=0)
            best_ref[right, :, columns] = jnp.maximum(best_ref[right, :, columns], best)
    for role, k in turns:
        rows = pl.ds(k * capacity, capacity)
        turned = jnp.transpose(row_ref[role, rows, :]).reshape(capacity // 8, 8, capacity)
        best_ref[role, :, rows] = jnp.maximum(best_ref[role, :, rows], jnp.max(turned, axis=0))
    for role, out_ref in zip(done, out_refs):
        out_ref[...] = jnp.max(best_ref[role], axis=0, keepdims=True)


def spread_kernel(ring, offsets, groups, *refs):
    *partial_refs, out_ref = refs
    shards = len(ring)
    out_ref[...] = jnp.full(out_ref.shape, jnp.float32(LOW))
    shard, group = lax.axis_index("shard"), lax.axis_index("group")
    for offset, ref in zip(offsets, partial_refs):
        target = sum(
            jnp.where(shard == ring[e], ring[(e + offset) % shards], 0) for e in range(shards)
        )
        for k in range(groups):
            row = target * groups + (group ^ k)
            out_ref[pl.ds(row, 1)] = ref[:, k * LANES : (k + 1) * LANES].reshape(1, 1, LANES)


def place_kernel(groups, back_ref, place_ref, out_ref):
    place = place_ref[...]
    rows = place.shape[1]
    best = jnp.full((1, rows), jnp.float32(LOW))
    for g in range(groups):
        row = jnp.full((1, LANES), jnp.float32(-1.0))
        for s in range(back_ref.shape[0] // groups):
            row = jnp.maximum(row, back_ref[s * groups + g])
        values = jnp.concatenate([column_of(row)] * (rows // LANES), axis=1)
        here = lax.broadcasted_iota(jnp.int32, (LANES, rows), 0) + g * LANES == place
        best = jnp.maximum(
            best, jnp.max(jnp.where(here, values, jnp.float32(LOW)), axis=0, keepdims=True)
        )
    out_ref[...] = best


def in_vmem(count):
    return [pl.BlockSpec(memory_space=pltpu.VMEM)] * count


def call(
    kernel, out_shape, scratch, args, flops, bytes_accessed, in_specs=None, limit=48 * MIB
):
    return pl.pallas_call(
        kernel,
        out_shape=out_shape,
        in_specs=in_specs or in_vmem(len(args)),
        out_specs=in_vmem(len(out_shape)),
        scratch_shapes=scratch,
        compiler_params=pltpu.CompilerParams(vmem_limit_bytes=limit),
        cost_estimate=pl.CostEstimate(
            flops=flops, bytes_accessed=bytes_accessed, transcendentals=0
        ),
    )(*args)


def after(x, *earlier):
    return lax.optimization_barrier((x, *earlier))[0]


def stack(parts, wait):
    return call(
        stack_kernel,
        [jax.ShapeDtypeStruct((len(parts), *parts[0].shape), parts[0].dtype)],
        [],
        parts,
        wait,
        4 * len(parts) * parts[0].size,
    )[0]


def score(held, tasks, acc, done, slots, width):
    roles = len(held)
    used = sorted(
        {(left, k) for left, ks, _, _, _ in tasks for k in ks}
        | {(right, k) for _, _, right, ks, _ in tasks for k in ks},
        key=lambda x: (x[0], -x[1]),
    )
    arrays, sources = [], {}
    for role, k in used:
        array, part = held[role][k]
        index = next((i for i, x in enumerate(arrays) if x is array), len(arrays))
        if index == len(arrays):
            arrays.append(array)
        sources[role, k] = (index, part)
    ends = [jax.ShapeDtypeStruct((1, slots), jnp.float32)] * len(done)
    tiles = sum(len(task[1]) * len(task[3]) for task in tasks)
    best, *ends = call(
        lambda *refs: score_kernel(sources, tasks, done, *refs),
        [jax.ShapeDtypeStruct((roles, 8, slots), jnp.float32)] + ends,
        [
            pltpu.VMEM((roles, slots, width), jnp.bfloat16),
            pltpu.VMEM((roles, slots, LANES), jnp.float32),
            pltpu.VMEM((roles, slots, LANES), jnp.float32),
        ],
        arrays + acc,
        2 * tiles * LANES * LANES * width,
        2 * len(used) * LANES * width,
    )
    return [best], ends


def per_device(embeddings, row_group, row_cluster):
    rows, width = embeddings.shape
    groups = lax.axis_size("group")
    shards = lax.axis_size("shard")
    capacity = rows // 4
    slots = groups * capacity
    ring = ring_order(shards)
    offsets, pairs = offset_cover(shards)
    roles = len(offsets)
    height = width * capacity // LANES + TAIL

    def from_offset(x, offset):
        perm = [(ring[(e + offset) % shards], ring[e]) for e in range(shards)]
        return lax.ppermute(x, "shard", perm)

    def exchange(blocks):
        got = list(blocks)
        for k in range(1, groups):
            block = after(blocks[k], got[1]) if k > 2 else blocks[k]
            got[k] = lax.ppermute(block, "group", [(z, z ^ k) for z in range(groups)])
        return got

    (units,) = call(
        unit_kernel,
        [jax.ShapeDtypeStruct((rows, width), jnp.bfloat16)],
        [pltpu.VMEM((rows, width), embeddings.dtype), pltpu.SemaphoreType.DMA((4,))],
        (embeddings,),
        4 * rows * width,
        4 * rows * width,
        [pl.BlockSpec(memory_space=pltpu.HBM)],
        53 * MIB,
    )
    *send, place = call(
        lambda *refs: sort_kernel("group", *refs),
        [jax.ShapeDtypeStruct((height, LANES), jnp.bfloat16)] * groups
        + [jax.ShapeDtypeStruct((1, rows), jnp.int32)],
        [],
        (units, *lax.optimization_barrier((row_group.reshape(1, rows), row_cluster.reshape(1, rows)))),
        2 * rows * slots * width,
        4 * rows * width,
    )

    late = [groups - 1] if groups > 1 else []
    early = list(range(groups - len(late)))
    late = [groups - 1] if groups > 1 else []
    early = list(range(groups - len(late)))
    near = [r for r in range(1, roles) if 2 * offsets[r] != shards]
    far = [r for r in range(1, roles) if r not in near]
    first = {r: from_offset(send[0], offsets[r]) for r in near}
    own = exchange(send)
    held = [[None] * groups for _ in offsets]
    held[0] = [(x, None) for x in own]
    for r in near:
        held[r][0] = (first[r], None)
    for k in range(1, groups):
        if k == 1:
            block = after(own[k], first[near[0]]) if near else own[k]
        else:
            passed = [held[r][k - 2][0] for r in near]
            block = stack([after(own[k], *passed)], WAIT)
        for r in near:
            held[r][k] = (from_offset(block, offsets[r]), 0 if k > 1 else None)
    got = {r: from_offset(stack(own, 0), offsets[r]) for r in far}
    for r in far:
        held[r] = [(got[r], k) for k in range(groups)]
    everything = [(0, 0, False)]
    everything += [(offsets.index(a), offsets.index(b), both) for a, b, both in pairs]
    steps = [[] for _ in range(4)]
    final = [0] * roles
    for left, right, both in everything:
        for left_ks in (early, late):
            for right_ks in (early, late):
                if left_ks and right_ks:
                    step = 0
                    for role, ks in ((left, left_ks), (right, right_ks)):
                        if role in near:
                            step = max(step, 1 if ks is early else 3 if role == near[0] else 2)
                    task = (left, left_ks, right, right_ks, both)
                    if both and right_ks is late:
                        task = (right, right_ks, left, left_ks, both)
                    steps[step].append(task)
                    final[right] = max(final[right], step)
                    if both:
                        final[left] = max(final[left], step)
    acc, partial = [], [None] * roles
    for step, tasks in enumerate(steps):
        if tasks:
            done = [r for r in range(roles) if final[r] == step]
            acc, ends = score(held, tasks, acc, done, slots, width)
            for r, end in zip(done, ends):
                partial[r] = end
    (best,) = call(
        lambda *refs: spread_kernel(ring, offsets, groups, *refs),
        [jax.ShapeDtypeStruct((shards * groups, 1, capacity), jnp.float32)],
        [],
        partial,
        roles * slots,
        4 * roles * slots,
    )
    back = lax.all_to_all(best, ("shard", "group"), split_axis=0, concat_axis=0, tiled=True)
    (result,) = call(
        lambda *refs: place_kernel(groups, *refs),
        [jax.ShapeDtypeStruct((1, rows), jnp.float32)],
        [],
        [back, place],
        rows * slots,
        4 * slots,
    )
    return result.reshape(rows)


def solution(mesh):
    placed = (P(("shard", "group"), None), P(("shard", "group"), None), P(("shard", "group")))
    return jax.shard_map(
        per_device, mesh=mesh, in_specs=placed, out_specs=P(("shard", "group")), check_vma=False
    )
```

```python
import jax
import jax.numpy as jnp
from jax import lax
from jax.experimental import pallas as pl
from jax.experimental.pallas import tpu as pltpu
from jax.sharding import PartitionSpec as P

LANES = 128
TAIL = 16
LOW = -2.0
MIB = 1024 * 1024
WAIT = 2 * 10**10


def ring_order(size):
    if size % 2:
        return list(range(size))
    half = size // 2
    chips = [i ^ (i >> 1) for i in range(half)]
    if sorted(chips) != list(range(half)):
        chips = list(range(half))
    return [2 * chip + core for core in range(2) for chip in chips]


def offset_cover(size):
    offsets = list(dict.fromkeys([0, size // 2, 1 % size, (size - 1) % size]))

    def missing(chosen):
        have = {(a - b) % size for a in chosen for b in chosen}
        return [d for d in range(size) if d not in have]

    while missing(offsets):
        offsets.append(min(range(size), key=lambda x: len(missing(offsets + [x]))))
    pairs = []
    for diff in range(1, size // 2 + 1):
        found = [
            (a, b)
            for b in [(size - 1) % size] + offsets
            for a in offsets
            if (a - b) % size in (diff, size - diff)
        ]
        if 2 * diff == size:
            found = [(a, b) for a, b in found if b == 0] + found
        a, b = found[0]
        pairs.append((a, b, b != 0 or 2 * diff != size))
    return offsets, pairs


def column_of(row):
    size = row.shape[1]
    return jnp.transpose(jnp.broadcast_to(row, (size, size)))


def unit_kernel(far_ref, unit_ref, near_ref, sems):
    parts = sems.shape[0]
    size = far_ref.shape[0] // parts
    copies = [
        pltpu.make_async_copy(
            far_ref.at[pl.ds(i * size, size), :], near_ref.at[pl.ds(i * size, size), :], sems.at[i]
        )
        for i in range(parts)
    ]
    for copy in copies:
        copy.start()
    for i, copy in enumerate(copies):
        copy.wait()
        feats = near_ref[pl.ds(i * size, size), :].astype(jnp.float32)
        squares = jnp.sum(feats * feats, axis=1, keepdims=True) + 1e-06
        unit_ref[pl.ds(i * size, size), :] = (feats * lax.rsqrt(squares)).astype(jnp.bfloat16)


def sort_kernel(axis, unit_ref, group_ref, label_ref, *out_refs):
    *block_refs, place_ref = out_refs
    rows, width = unit_ref.shape
    groups = len(block_refs)
    capacity = (block_refs[0].shape[0] - TAIL) * LANES // width
    slots = groups * capacity
    chunks = width // LANES
    owner = group_ref[...]
    rel = owner ^ lax.axis_index(axis)
    lines = max(8, groups)
    onehot = lax.broadcasted_iota(jnp.int32, (lines, rows), 0) == rel
    before = lax.broadcasted_iota(jnp.int32, (rows, rows), 0) < lax.broadcasted_iota(
        jnp.int32, (rows, rows), 1
    )
    ranks = jnp.dot(
        jnp.where(onehot, 1.0, 0.0).astype(jnp.bfloat16),
        jnp.where(before, 1.0, 0.0).astype(jnp.bfloat16),
        preferred_element_type=jnp.float32,
    )
    rank = jnp.sum(jnp.where(onehot, ranks, 0.0), axis=0, keepdims=True).astype(jnp.int32)
    place_ref[...] = owner * capacity + rank
    move = jnp.where(
        lax.broadcasted_iota(jnp.int32, (slots, rows), 0) == rel * capacity + rank, 1.0, 0.0
    ).astype(jnp.bfloat16)
    labels = jnp.broadcast_to(label_ref[...] + 1, (TAIL, rows)).astype(jnp.bfloat16)
    sorted_labels = (
        lax.dot_general(
            labels, move, (((1,), (1,)), ((), ())), preferred_element_type=jnp.float32
        )
        - 1.0
    ).astype(jnp.bfloat16)
    for k, block_ref in enumerate(block_refs):
        part = slice(k * capacity, (k + 1) * capacity)
        block = jnp.dot(
            move[part], unit_ref[...], preferred_element_type=jnp.float32
        ).astype(jnp.bfloat16)
        for c in range(chunks):
            block_ref[pl.ds(c * capacity, capacity), :] = block[:, c * LANES : (c + 1) * LANES]
        block_ref[pl.ds(chunks * capacity, TAIL), :] = sorted_labels[:, part]


def stack_kernel(*refs):
    for k, ref in enumerate(refs[:-1]):
        refs[-1][k] = ref[...]


def score_kernel(sources, tasks, done, *refs):
    *refs, flat_ref, side_ref, row_ref = refs
    outs = 1 + len(done)
    inputs, (best_ref, *out_refs) = refs[:-outs], refs[-outs:]
    capacity = LANES
    low = jnp.float32(LOW)
    arrays = 1 + max(index for index, _ in sources.values())
    best_ref[...] = inputs[arrays][...] if len(inputs) > arrays else jnp.full(best_ref.shape, low)
    tops = {}
    for (role, k), (index, part) in sources.items():
        ref = inputs[index] if part is None else inputs[index].at[part]
        height = ref.shape[0] - TAIL
        rows = pl.ds(k * capacity, capacity)
        for c in range(height // capacity):
            flat_ref[role, rows, pl.ds(c * LANES, LANES)] = ref[pl.ds(c * capacity, capacity), :]
        tops[role, k] = ref[pl.ds(height, TAIL), :][0:1].astype(jnp.float32)
    for role, k in sorted({(left, k) for left, ks, _, _, _ in tasks for k in ks}):
        side_ref[role, pl.ds(k * capacity, capacity), :] = column_of(tops[role, k])
    turns = sorted({(left, k) for left, ks, _, _, both in tasks if both for k in ks})
    for role, k in turns:
        row_ref[role, pl.ds(k * capacity, capacity), :] = jnp.full((capacity, LANES), low)
    for left, left_ks, right, right_ks, both in tasks:
        start, count = left_ks[0] * capacity, len(left_ks) * capacity
        rows = pl.ds(start, count)
        for i in range(0, len(right_ks), 2):
            some = right_ks[i : i + 2]
            width = len(some) * capacity
            columns = pl.ds(some[0] * capacity, width)
            scores = lax.dot_general(
                flat_ref[left, rows, :],
                flat_ref[right, columns, :],
                (((1,), (1,)), ((), ())),
                preferred_element_type=jnp.float32,
            )
            top = jnp.concatenate([tops[right, k] for k in some], axis=1)
            same = jnp.concatenate([side_ref[left, rows, :]] * len(some), axis=1) == top
            if left == right:
                same = same & (
                    lax.broadcasted_iota(jnp.int32, (count, width), 0) + start
                    != lax.broadcasted_iota(jnp.int32, (count, width), 1) + some[0] * capacity
                )
            scores = jnp.where(same, scores, low)
            if both:
                best = row_ref[left, rows, :]
                for c in range(len(some)):
                    best = jnp.maximum(best, scores[:, c * LANES : (c + 1) * LANES])
                row_ref[left, rows, :] = best
            best = jnp.max(scores.reshape(count // 8, 8, width), axis=0)
            best_ref[right, :, columns] = jnp.maximum(best_ref[right, :, columns], best)
    for role, k in turns:
        rows = pl.ds(k * capacity, capacity)
        turned = jnp.transpose(row_ref[role, rows, :]).reshape(capacity // 8, 8, capacity)
        best_ref[role, :, rows] = jnp.maximum(best_ref[role, :, rows], jnp.max(turned, axis=0))
    for role, out_ref in zip(done, out_refs):
        out_ref[...] = jnp.max(best_ref[role], axis=0, keepdims=True)


def spread_kernel(ring, offsets, groups, *refs):
    *partial_refs, out_ref = refs
    shards = len(ring)
    out_ref[...] = jnp.full(out_ref.shape, jnp.float32(LOW))
    shard, group = lax.axis_index("shard"), lax.axis_index("group")
    for offset, ref in zip(offsets, partial_refs):
        target = sum(
            jnp.where(shard == ring[e], ring[(e + offset) % shards], 0) for e in range(shards)
        )
        for k in range(groups):
            row = (shards - target) * groups - 1 - (group ^ k)
            out_ref[pl.ds(row, 1)] = ref[:, k * LANES : (k + 1) * LANES].reshape(1, 1, LANES)


def place_kernel(groups, back_ref, place_ref, out_ref):
    place = place_ref[...]
    rows = place.shape[1]
    best = jnp.full((1, rows), jnp.float32(LOW))
    for g in range(groups):
        row = jnp.full((1, LANES), jnp.float32(-1.0))
        for s in range(back_ref.shape[0] // groups):
            row = jnp.maximum(row, back_ref[s * groups + groups - 1 - g])
        values = jnp.concatenate([column_of(row)] * (rows // LANES), axis=1)
        here = lax.broadcasted_iota(jnp.int32, (LANES, rows), 0) + g * LANES == place
        best = jnp.maximum(
            best, jnp.max(jnp.where(here, values, jnp.float32(LOW)), axis=0, keepdims=True)
        )
    out_ref[...] = best


def in_vmem(count):
    return [pl.BlockSpec(memory_space=pltpu.VMEM)] * count


def call(
    kernel, out_shape, scratch, args, flops, bytes_accessed, in_specs=None, limit=48 * MIB
):
    return pl.pallas_call(
        kernel,
        out_shape=out_shape,
        in_specs=in_specs or in_vmem(len(args)),
        out_specs=in_vmem(len(out_shape)),
        scratch_shapes=scratch,
        compiler_params=pltpu.CompilerParams(vmem_limit_bytes=limit),
        cost_estimate=pl.CostEstimate(
            flops=flops, bytes_accessed=bytes_accessed, transcendentals=0
        ),
    )(*args)


def after(x, *earlier):
    return lax.optimization_barrier((x, *earlier))[0]


def stack(parts, wait):
    return call(
        stack_kernel,
        [jax.ShapeDtypeStruct((len(parts), *parts[0].shape), parts[0].dtype)],
        [],
        parts,
        wait,
        4 * len(parts) * parts[0].size,
    )[0]


def score(held, tasks, acc, done, slots, width):
    roles = len(held)
    used = sorted(
        {(left, k) for left, ks, _, _, _ in tasks for k in ks}
        | {(right, k) for _, _, right, ks, _ in tasks for k in ks},
        key=lambda x: (x[0], -x[1]),
    )
    arrays, sources = [], {}
    for role, k in used:
        array, part = held[role][k]
        index = next((i for i, x in enumerate(arrays) if x is array), len(arrays))
        if index == len(arrays):
            arrays.append(array)
        sources[role, k] = (index, part)
    ends = [jax.ShapeDtypeStruct((1, slots), jnp.float32)] * len(done)
    tiles = sum(len(task[1]) * len(task[3]) for task in tasks)
    best, *ends = call(
        lambda *refs: score_kernel(sources, tasks, done, *refs),
        [jax.ShapeDtypeStruct((roles, 8, slots), jnp.float32)] + ends,
        [
            pltpu.VMEM((roles, slots, width), jnp.bfloat16),
            pltpu.VMEM((roles, slots, LANES), jnp.float32),
            pltpu.VMEM((roles, slots, LANES), jnp.float32),
        ],
        arrays + acc,
        2 * tiles * LANES * LANES * width,
        2 * len(used) * LANES * width,
    )
    return [best], ends


def per_device(embeddings, row_group, row_cluster):
    rows, width = embeddings.shape
    groups = lax.axis_size("group")
    shards = lax.axis_size("shard")
    capacity = rows // 4
    slots = groups * capacity
    ring = ring_order(shards)
    offsets, pairs = offset_cover(shards)
    roles = len(offsets)
    height = width * capacity // LANES + TAIL

    def from_offset(x, offset):
        perm = [(ring[(e + offset) % shards], ring[e]) for e in range(shards)]
        return lax.ppermute(x, "shard", perm)

    def exchange(blocks):
        got = list(blocks)
        for k in range(1, groups):
            block = after(blocks[k], got[2]) if k > 2 else blocks[k]
            got[k] = lax.ppermute(block, "group", [(z, z ^ k) for z in range(groups)])
        return got

    (units,) = call(
        unit_kernel,
        [jax.ShapeDtypeStruct((rows, width), jnp.bfloat16)],
        [pltpu.VMEM((rows, width), embeddings.dtype), pltpu.SemaphoreType.DMA((4,))],
        (embeddings,),
        4 * rows * width,
        4 * rows * width,
        [pl.BlockSpec(memory_space=pltpu.HBM)],
        53 * MIB,
    )
    *send, place = call(
        lambda *refs: sort_kernel("group", *refs),
        [jax.ShapeDtypeStruct((height, LANES), jnp.bfloat16)] * groups
        + [jax.ShapeDtypeStruct((1, rows), jnp.int32)],
        [],
        (units, *lax.optimization_barrier((row_group.reshape(1, rows), row_cluster.reshape(1, rows)))),
        2 * rows * slots * width,
        4 * rows * width,
    )

    late = [groups - 1] if groups > 1 else []
    early = list(range(groups - len(late)))
    late = [groups - 1] if groups > 1 else []
    early = list(range(groups - len(late)))
    near = [r for r in range(1, roles) if 2 * offsets[r] != shards]
    far = [r for r in range(1, roles) if r not in near]
    first = {r: from_offset(send[0], offsets[r]) for r in near}
    own = exchange(send)
    held = [[None] * groups for _ in offsets]
    held[0] = [(x, None) for x in own]
    for r in near:
        held[r][0] = (first[r], None)
    for k in range(1, groups):
        if k == 1:
            block = after(own[k], first[near[0]]) if near else own[k]
        else:
            passed = [held[r][k - 2][0] for r in near]
            block = stack([after(own[k], *passed)], WAIT)
        for r in near:
            held[r][k] = (from_offset(block, offsets[r]), 0 if k > 1 else None)
    got = {r: from_offset(stack(own, 0), offsets[r]) for r in far}
    for r in far:
        held[r] = [(got[r], k) for k in range(groups)]
    everything = [(0, 0, False)]
    everything += [(offsets.index(a), offsets.index(b), both) for a, b, both in pairs]
    steps = [[] for _ in range(4)]
    final = [0] * roles
    for left, right, both in everything:
        for left_ks in (early, late):
            for right_ks in (early, late):
                if left_ks and right_ks:
                    step = 0
                    for role, ks in ((left, left_ks), (right, right_ks)):
                        if role in near:
                            step = max(step, 1 if ks is early else 3 if role == near[0] else 2)
                    task = (left, left_ks, right, right_ks, both)
                    if both and right_ks is late and left_ks is early:
                        task = (right, right_ks, left, left_ks, both)
                    steps[step].append(task)
                    final[right] = max(final[right], step)
                    if both:
                        final[left] = max(final[left], step)
    acc, partial = [], [None] * roles
    for step, tasks in enumerate(steps):
        if tasks:
            done = [r for r in range(roles) if final[r] == step]
            acc, ends = score(held, tasks, acc, done, slots, width)
            for r, end in zip(done, ends):
                partial[r] = end
    (best,) = call(
        lambda *refs: spread_kernel(ring, offsets, groups, *refs),
        [jax.ShapeDtypeStruct((shards * groups, 1, capacity), jnp.float32)],
        [],
        partial,
        roles * slots,
        4 * roles * slots,
    )
    back = lax.all_to_all(
        best,
        ("shard", "group"),
        split_axis=0,
        concat_axis=0,
        axis_index_groups=[list(reversed(range(shards * groups)))],
        tiled=True,
    )
    (result,) = call(
        lambda *refs: place_kernel(groups, *refs),
        [jax.ShapeDtypeStruct((1, rows), jnp.float32)],
        [],
        [back, place],
        rows * slots,
        4 * slots,
    )
    return result.reshape(rows)


def solution(mesh):
    placed = (P(("shard", "group"), None), P(("shard", "group"), None), P(("shard", "group")))
    return jax.shard_map(
        per_device, mesh=mesh, in_specs=placed, out_specs=P(("shard", "group")), check_vma=False
    )
```

```python
import jax
import jax.numpy as jnp
from jax import lax
from jax.experimental import pallas as pl
from jax.experimental.pallas import tpu as pltpu
from jax.sharding import PartitionSpec as P

LANES = 128
TAIL = 16
LOW = -2.0
MIB = 1024 * 1024
WAIT = 2 * 10**10


def ring_order(size):
    if size % 2:
        return list(range(size))
    half = size // 2
    chips = [i ^ (i >> 1) for i in range(half)]
    if sorted(chips) != list(range(half)):
        chips = list(range(half))
    return [2 * chip + core for core in range(2) for chip in chips]


def offset_cover(size):
    offsets = list(dict.fromkeys([0, size // 2, 1 % size, (size - 1) % size]))

    def missing(chosen):
        have = {(a - b) % size for a in chosen for b in chosen}
        return [d for d in range(size) if d not in have]

    while missing(offsets):
        offsets.append(min(range(size), key=lambda x: len(missing(offsets + [x]))))
    pairs = []
    for diff in range(1, size // 2 + 1):
        found = [
            (a, b)
            for b in [(size - 1) % size] + offsets
            for a in offsets
            if (a - b) % size in (diff, size - diff)
        ]
        if 2 * diff == size:
            found = [(a, b) for a, b in found if b == 0] + found
        a, b = found[0]
        pairs.append((a, b, b != 0 or 2 * diff != size))
    return offsets, pairs


def column_of(row):
    size = row.shape[1]
    return jnp.transpose(jnp.broadcast_to(row, (size, size)))


def unit_kernel(far_ref, unit_ref, near_ref, sems):
    parts = sems.shape[0]
    size = far_ref.shape[0] // parts
    copies = [
        pltpu.make_async_copy(
            far_ref.at[pl.ds(i * size, size), :], near_ref.at[pl.ds(i * size, size), :], sems.at[i]
        )
        for i in range(parts)
    ]
    for copy in copies:
        copy.start()
    for i, copy in enumerate(copies):
        copy.wait()
        feats = near_ref[pl.ds(i * size, size), :].astype(jnp.float32)
        squares = jnp.sum(feats * feats, axis=1, keepdims=True) + 1e-06
        unit_ref[pl.ds(i * size, size), :] = (feats * lax.rsqrt(squares)).astype(jnp.bfloat16)


def sort_kernel(axis, unit_ref, group_ref, label_ref, *out_refs):
    *block_refs, place_ref = out_refs
    rows, width = unit_ref.shape
    groups = len(block_refs)
    capacity = (block_refs[0].shape[0] - TAIL) * LANES // width
    slots = groups * capacity
    chunks = width // LANES
    owner = group_ref[...]
    rel = owner ^ lax.axis_index(axis)
    lines = max(8, groups)
    onehot = lax.broadcasted_iota(jnp.int32, (lines, rows), 0) == rel
    before = lax.broadcasted_iota(jnp.int32, (rows, rows), 0) < lax.broadcasted_iota(
        jnp.int32, (rows, rows), 1
    )
    ranks = jnp.dot(
        jnp.where(onehot, 1.0, 0.0).astype(jnp.bfloat16),
        jnp.where(before, 1.0, 0.0).astype(jnp.bfloat16),
        preferred_element_type=jnp.float32,
    )
    rank = jnp.sum(jnp.where(onehot, ranks, 0.0), axis=0, keepdims=True).astype(jnp.int32)
    place_ref[...] = owner * capacity + rank
    move = jnp.where(
        lax.broadcasted_iota(jnp.int32, (slots, rows), 0) == rel * capacity + rank, 1.0, 0.0
    ).astype(jnp.bfloat16)
    labels = jnp.broadcast_to(label_ref[...] + 1, (TAIL, rows)).astype(jnp.bfloat16)
    sorted_labels = (
        lax.dot_general(
            labels, move, (((1,), (1,)), ((), ())), preferred_element_type=jnp.float32
        )
        - 1.0
    ).astype(jnp.bfloat16)
    for k, block_ref in enumerate(block_refs):
        part = slice(k * capacity, (k + 1) * capacity)
        block = jnp.dot(
            move[part], unit_ref[...], preferred_element_type=jnp.float32
        ).astype(jnp.bfloat16)
        for c in range(chunks):
            block_ref[pl.ds(c * capacity, capacity), :] = block[:, c * LANES : (c + 1) * LANES]
        block_ref[pl.ds(chunks * capacity, TAIL), :] = sorted_labels[:, part]


def stack_kernel(*refs):
    for k, ref in enumerate(refs[:-1]):
        refs[-1][k] = ref[...]


def score_kernel(sources, tasks, done, last, *refs):
    *refs, flat_ref, side_ref, row_ref = refs
    if last:
        *refs, best_ref = refs
        inputs, out_refs = refs[: -len(done)], refs[-len(done) :]
    else:
        outs = 1 + len(done)
        inputs, (best_ref, *out_refs) = refs[:-outs], refs[-outs:]
    capacity = LANES
    low = jnp.float32(LOW)
    arrays = 1 + max(index for index, _ in sources.values())
    best_ref[...] = inputs[arrays][...] if len(inputs) > arrays else jnp.full(best_ref.shape, low)
    tops = {}
    for (role, k), (index, part) in sources.items():
        ref = inputs[index] if part is None else inputs[index].at[part]
        height = ref.shape[0] - TAIL
        rows = pl.ds(k * capacity, capacity)
        for c in range(height // capacity):
            flat_ref[role, rows, pl.ds(c * LANES, LANES)] = ref[pl.ds(c * capacity, capacity), :]
        tops[role, k] = ref[pl.ds(height, TAIL), :][0:1].astype(jnp.float32)
    for role, k in sorted({(left, k) for left, ks, _, _, _ in tasks for k in ks}):
        side_ref[role, pl.ds(k * capacity, capacity), :] = column_of(tops[role, k])
    turns = sorted({(left, k) for left, ks, _, _, both in tasks if both for k in ks})
    for role, k in turns:
        row_ref[role, pl.ds(k * capacity, capacity), :] = jnp.full((capacity, LANES), low)
    for left, left_ks, right, right_ks, both in tasks:
        start, count = left_ks[0] * capacity, len(left_ks) * capacity
        rows = pl.ds(start, count)
        for i in range(0, len(right_ks), 2):
            some = right_ks[i : i + 2]
            width = len(some) * capacity
            columns = pl.ds(some[0] * capacity, width)
            scores = lax.dot_general(
                flat_ref[left, rows, :],
                flat_ref[right, columns, :],
                (((1,), (1,)), ((), ())),
                preferred_element_type=jnp.float32,
            )
            top = jnp.concatenate([tops[right, k] for k in some], axis=1)
            same = jnp.concatenate([side_ref[left, rows, :]] * len(some), axis=1) == top
            if left == right:
                same = same & (
                    lax.broadcasted_iota(jnp.int32, (count, width), 0) + start
                    != lax.broadcasted_iota(jnp.int32, (count, width), 1) + some[0] * capacity
                )
            scores = jnp.where(same, scores, low)
            if both:
                best = row_ref[left, rows, :]
                for c in range(len(some)):
                    best = jnp.maximum(best, scores[:, c * LANES : (c + 1) * LANES])
                row_ref[left, rows, :] = best
            best = jnp.max(scores.reshape(count // 8, 8, width), axis=0)
            best_ref[right, :, columns] = jnp.maximum(best_ref[right, :, columns], best)
    for role, k in turns:
        rows = pl.ds(k * capacity, capacity)
        turned = jnp.transpose(row_ref[role, rows, :]).reshape(capacity // 8, 8, capacity)
        best_ref[role, :, rows] = jnp.maximum(best_ref[role, :, rows], jnp.max(turned, axis=0))
    for role, out_ref in zip(done, out_refs):
        out_ref[...] = jnp.max(best_ref[role], axis=0, keepdims=True)


def spread_kernel(ring, offsets, groups, *refs):
    *partial_refs, out_ref = refs
    shards = len(ring)
    out_ref[...] = jnp.full(out_ref.shape, jnp.float32(LOW))
    shard, group = lax.axis_index("shard"), lax.axis_index("group")
    for offset, ref in zip(offsets, partial_refs):
        target = sum(
            jnp.where(shard == ring[e], ring[(e + offset) % shards], 0) for e in range(shards)
        )
        for k in range(groups):
            row = target * groups + (group ^ k)
            out_ref[pl.ds(row, 1)] = ref[:, k * LANES : (k + 1) * LANES].reshape(1, 1, LANES)


def place_kernel(groups, back_ref, place_ref, out_ref):
    place = place_ref[...]
    rows = place.shape[1]
    best = jnp.full((1, rows), jnp.float32(LOW))
    for g in range(groups):
        row = jnp.full((1, LANES), jnp.float32(-1.0))
        for s in range(back_ref.shape[0] // groups):
            row = jnp.maximum(row, back_ref[s * groups + g])
        values = jnp.concatenate([column_of(row)] * (rows // LANES), axis=1)
        here = lax.broadcasted_iota(jnp.int32, (LANES, rows), 0) + g * LANES == place
        best = jnp.maximum(
            best, jnp.max(jnp.where(here, values, jnp.float32(LOW)), axis=0, keepdims=True)
        )
    out_ref[...] = best


def in_vmem(count):
    return [pl.BlockSpec(memory_space=pltpu.VMEM)] * count


def call(
    kernel, out_shape, scratch, args, flops, bytes_accessed, in_specs=None, limit=48 * MIB
):
    return pl.pallas_call(
        kernel,
        out_shape=out_shape,
        in_specs=in_specs or in_vmem(len(args)),
        out_specs=in_vmem(len(out_shape)),
        scratch_shapes=scratch,
        compiler_params=pltpu.CompilerParams(vmem_limit_bytes=limit),
        cost_estimate=pl.CostEstimate(
            flops=flops, bytes_accessed=bytes_accessed, transcendentals=0
        ),
    )(*args)


def after(x, *earlier):
    return lax.optimization_barrier((x, *earlier))[0]


def stack(parts, wait):
    return call(
        stack_kernel,
        [jax.ShapeDtypeStruct((len(parts), *parts[0].shape), parts[0].dtype)],
        [],
        parts,
        wait,
        4 * len(parts) * parts[0].size,
    )[0]


def score(held, tasks, acc, done, last, slots, width):
    roles = len(held)
    used = sorted(
        {(left, k) for left, ks, _, _, _ in tasks for k in ks}
        | {(right, k) for _, _, right, ks, _ in tasks for k in ks},
        key=lambda x: (x[0], -x[1]),
    )
    arrays, sources = [], {}
    for role, k in used:
        array, part = held[role][k]
        index = next((i for i, x in enumerate(arrays) if x is array), len(arrays))
        if index == len(arrays):
            arrays.append(array)
        sources[role, k] = (index, part)
    ends = [jax.ShapeDtypeStruct((1, slots), jnp.float32)] * len(done)
    tiles = sum(len(task[1]) * len(task[3]) for task in tasks)
    best = [] if last else [jax.ShapeDtypeStruct((roles, 8, slots), jnp.float32)]
    got = call(
        lambda *refs: score_kernel(sources, tasks, done, last, *refs),
        best + ends,
        ([pltpu.VMEM((roles, 8, slots), jnp.float32)] if last else [])
        + [
            pltpu.VMEM((roles, slots, width), jnp.bfloat16),
            pltpu.VMEM((roles, slots, LANES), jnp.float32),
            pltpu.VMEM((roles, slots, LANES), jnp.float32),
        ],
        arrays + list(acc),
        2 * tiles * LANES * LANES * width,
        2 * len(used) * LANES * width,
    )
    return got[: len(best)], got[len(best) :]


def per_device(embeddings, row_group, row_cluster):
    rows, width = embeddings.shape
    groups = lax.axis_size("group")
    shards = lax.axis_size("shard")
    capacity = rows // 4
    slots = groups * capacity
    ring = ring_order(shards)
    offsets, pairs = offset_cover(shards)
    roles = len(offsets)
    height = width * capacity // LANES + TAIL

    def from_offset(x, offset):
        perm = [(ring[(e + offset) % shards], ring[e]) for e in range(shards)]
        return lax.ppermute(x, "shard", perm)

    def exchange(blocks):
        got = list(blocks)
        for k in range(1, groups):
            block = after(blocks[k], got[1]) if k > 2 else blocks[k]
            got[k] = lax.ppermute(block, "group", [(z, z ^ k) for z in range(groups)])
        return got

    (units,) = call(
        unit_kernel,
        [jax.ShapeDtypeStruct((rows, width), jnp.bfloat16)],
        [pltpu.VMEM((rows, width), embeddings.dtype), pltpu.SemaphoreType.DMA((4,))],
        (embeddings,),
        4 * rows * width,
        4 * rows * width,
        [pl.BlockSpec(memory_space=pltpu.HBM)],
        53 * MIB,
    )
    *send, place = call(
        lambda *refs: sort_kernel("group", *refs),
        [jax.ShapeDtypeStruct((height, LANES), jnp.bfloat16)] * groups
        + [jax.ShapeDtypeStruct((1, rows), jnp.int32)],
        [],
        (units, *lax.optimization_barrier((row_group.reshape(1, rows), row_cluster.reshape(1, rows)))),
        2 * rows * slots * width,
        4 * rows * width,
    )

    late = [groups - 1] if groups > 1 else []
    early = list(range(groups - len(late)))
    late = [groups - 1] if groups > 1 else []
    early = list(range(groups - len(late)))
    near = [r for r in range(1, roles) if 2 * offsets[r] != shards]
    far = [r for r in range(1, roles) if r not in near]
    first = {r: from_offset(send[0], offsets[r]) for r in near}
    own = exchange(send)
    held = [[None] * groups for _ in offsets]
    held[0] = [(x, None) for x in own]
    for r in near:
        held[r][0] = (first[r], None)
    for k in range(1, groups):
        if k == 1:
            block = after(own[k], first[near[0]]) if near else own[k]
        else:
            passed = [held[r][k - 2][0] for r in near]
            block = stack([after(own[k], *passed)], WAIT)
        for r in near:
            held[r][k] = (from_offset(block, offsets[r]), 0 if k > 1 else None)
    got = {r: from_offset(stack(own, 0), offsets[r]) for r in far}
    for r in far:
        held[r] = [(got[r], k) for k in range(groups)]
    everything = [(0, 0, False)]
    everything += [(offsets.index(a), offsets.index(b), both) for a, b, both in pairs]
    steps = [[] for _ in range(4)]
    final = [0] * roles
    for left, right, both in everything:
        for left_ks in (early, late):
            for right_ks in (early, late):
                if left_ks and right_ks:
                    step = 0
                    for role, ks in ((left, left_ks), (right, right_ks)):
                        if role in near:
                            step = max(step, 1 if ks is early else 3 if role == near[0] else 2)
                    task = (left, left_ks, right, right_ks, both)
                    if both and right_ks is late and left_ks is early:
                        task = (right, right_ks, left, left_ks, both)
                    steps[step].append(task)
                    final[right] = max(final[right], step)
                    if both:
                        final[left] = max(final[left], step)
    acc, partial = [], [None] * roles
    for step, tasks in enumerate(steps):
        if tasks:
            done = [r for r in range(roles) if final[r] == step]
            last = not any(steps[step + 1 :])
            acc, ends = score(held, tasks, acc, done, last, slots, width)
            for r, end in zip(done, ends):
                partial[r] = end
    (best,) = call(
        lambda *refs: spread_kernel(ring, offsets, groups, *refs),
        [jax.ShapeDtypeStruct((shards * groups, 1, capacity), jnp.float32)],
        [],
        partial,
        roles * slots,
        4 * roles * slots,
    )
    back = lax.all_to_all(best, ("shard", "group"), split_axis=0, concat_axis=0, tiled=True)
    (result,) = call(
        lambda *refs: place_kernel(groups, *refs),
        [jax.ShapeDtypeStruct((1, rows), jnp.float32)],
        [],
        [back, place],
        rows * slots,
        4 * slots,
    )
    return result.reshape(rows)


def solution(mesh):
    placed = (P(("shard", "group"), None), P(("shard", "group"), None), P(("shard", "group")))
    return jax.shard_map(
        per_device, mesh=mesh, in_specs=placed, out_specs=P(("shard", "group")), check_vma=False
    )
```

```python
import jax
import jax.numpy as jnp
from jax import lax
from jax.experimental import pallas as pl
from jax.experimental.pallas import tpu as pltpu
from jax.sharding import PartitionSpec as P

LANES = 128
TAIL = 16
LOW = -2.0
MIB = 1024 * 1024
WAIT = 2 * 10**10


def ring_order(size):
    if size % 2:
        return list(range(size))
    half = size // 2
    chips = [i ^ (i >> 1) for i in range(half)]
    if sorted(chips) != list(range(half)):
        chips = list(range(half))
    return [2 * chip + core for core in range(2) for chip in chips]


def offset_cover(size):
    offsets = list(dict.fromkeys([0, size // 2, 1 % size, (size - 1) % size]))

    def missing(chosen):
        have = {(a - b) % size for a in chosen for b in chosen}
        return [d for d in range(size) if d not in have]

    while missing(offsets):
        offsets.append(min(range(size), key=lambda x: len(missing(offsets + [x]))))
    pairs = []
    for diff in range(1, size // 2 + 1):
        found = [
            (a, b)
            for b in [(size - 1) % size] + offsets
            for a in offsets
            if (a - b) % size in (diff, size - diff)
        ]
        if 2 * diff == size:
            found = [(a, b) for a, b in found if b == 0] + found
        a, b = found[0]
        pairs.append((a, b, b != 0 or 2 * diff != size))
    return offsets, pairs


def column_of(row):
    size = row.shape[1]
    return jnp.transpose(jnp.broadcast_to(row, (size, size)))


def unit_kernel(far_ref, unit_ref, near_ref, sems):
    parts = sems.shape[0]
    size = far_ref.shape[0] // parts
    copies = [
        pltpu.make_async_copy(
            far_ref.at[pl.ds(i * size, size), :], near_ref.at[pl.ds(i * size, size), :], sems.at[i]
        )
        for i in range(parts)
    ]
    for copy in copies:
        copy.start()
    for i, copy in enumerate(copies):
        copy.wait()
        feats = near_ref[pl.ds(i * size, size), :].astype(jnp.float32)
        squares = jnp.sum(feats * feats, axis=1, keepdims=True) + 1e-06
        unit_ref[pl.ds(i * size, size), :] = (feats * lax.rsqrt(squares)).astype(jnp.bfloat16)


def sort_kernel(axis, unit_ref, group_ref, label_ref, *out_refs):
    *block_refs, place_ref = out_refs
    rows, width = unit_ref.shape
    groups = len(block_refs)
    capacity = (block_refs[0].shape[0] - TAIL) * LANES // width
    slots = groups * capacity
    chunks = width // LANES
    owner = group_ref[...]
    rel = owner ^ lax.axis_index(axis)
    lines = max(8, groups)
    onehot = lax.broadcasted_iota(jnp.int32, (lines, rows), 0) == rel
    before = lax.broadcasted_iota(jnp.int32, (rows, rows), 0) < lax.broadcasted_iota(
        jnp.int32, (rows, rows), 1
    )
    ranks = jnp.dot(
        jnp.where(onehot, 1.0, 0.0).astype(jnp.bfloat16),
        jnp.where(before, 1.0, 0.0).astype(jnp.bfloat16),
        preferred_element_type=jnp.float32,
    )
    rank = jnp.sum(jnp.where(onehot, ranks, 0.0), axis=0, keepdims=True).astype(jnp.int32)
    place_ref[...] = owner * capacity + rank
    move = jnp.where(
        lax.broadcasted_iota(jnp.int32, (slots, rows), 0) == rel * capacity + rank, 1.0, 0.0
    ).astype(jnp.bfloat16)
    labels = jnp.broadcast_to(label_ref[...] + 1, (TAIL, rows)).astype(jnp.bfloat16)
    sorted_labels = (
        lax.dot_general(
            labels, move, (((1,), (1,)), ((), ())), preferred_element_type=jnp.float32
        )
        - 1.0
    ).astype(jnp.bfloat16)
    for k, block_ref in enumerate(block_refs):
        part = slice(k * capacity, (k + 1) * capacity)
        block = jnp.dot(
            move[part], unit_ref[...], preferred_element_type=jnp.float32
        ).astype(jnp.bfloat16)
        for c in range(chunks):
            block_ref[pl.ds(c * capacity, capacity), :] = block[:, c * LANES : (c + 1) * LANES]
        block_ref[pl.ds(chunks * capacity, TAIL), :] = sorted_labels[:, part]


def stack_kernel(*refs):
    for k, ref in enumerate(refs[:-1]):
        refs[-1][k] = ref[...]


def score_kernel(sources, tasks, done, last, *refs):
    *refs, flat_ref, side_ref, row_ref = refs
    if last:
        *refs, best_ref = refs
        inputs, out_refs = refs[: -len(done)], refs[-len(done) :]
    else:
        outs = 1 + len(done)
        inputs, (best_ref, *out_refs) = refs[:-outs], refs[-outs:]
    capacity = LANES
    low = jnp.float32(LOW)
    arrays = 1 + max(index for index, _ in sources.values())
    best_ref[...] = inputs[arrays][...] if len(inputs) > arrays else jnp.full(best_ref.shape, low)
    tops = {}
    for (role, k), (index, part) in sources.items():
        ref = inputs[index] if part is None else inputs[index].at[part]
        height = ref.shape[0] - TAIL
        rows = pl.ds(k * capacity, capacity)
        for c in range(height // capacity):
            flat_ref[role, rows, pl.ds(c * LANES, LANES)] = ref[pl.ds(c * capacity, capacity), :]
        tops[role, k] = ref[pl.ds(height, TAIL), :][0:1].astype(jnp.float32)
    for role, k in sorted({(left, k) for left, ks, _, _, _ in tasks for k in ks}):
        side_ref[role, pl.ds(k * capacity, capacity), :] = column_of(tops[role, k])
    turns = sorted({(left, k) for left, ks, _, _, both in tasks if both for k in ks})
    for role, k in turns:
        row_ref[role, pl.ds(k * capacity, capacity), :] = jnp.full((capacity, LANES), low)
    for left, left_ks, right, right_ks, both in tasks:
        start, count = left_ks[0] * capacity, len(left_ks) * capacity
        rows = pl.ds(start, count)
        for i in range(0, len(right_ks), 2):
            some = right_ks[i : i + 2]
            width = len(some) * capacity
            columns = pl.ds(some[0] * capacity, width)
            scores = lax.dot_general(
                flat_ref[left, rows, :],
                flat_ref[right, columns, :],
                (((1,), (1,)), ((), ())),
                preferred_element_type=jnp.float32,
            )
            top = jnp.concatenate([tops[right, k] for k in some], axis=1)
            same = jnp.concatenate([side_ref[left, rows, :]] * len(some), axis=1) == top
            if left == right:
                same = same & (
                    lax.broadcasted_iota(jnp.int32, (count, width), 0) + start
                    != lax.broadcasted_iota(jnp.int32, (count, width), 1) + some[0] * capacity
                )
            scores = jnp.where(same, scores, low)
            if both:
                best = row_ref[left, rows, :]
                for c in range(len(some)):
                    best = jnp.maximum(best, scores[:, c * LANES : (c + 1) * LANES])
                row_ref[left, rows, :] = best
            best = jnp.max(scores.reshape(count // 8, 8, width), axis=0)
            best_ref[right, :, columns] = jnp.maximum(best_ref[right, :, columns], best)
    for role, k in turns:
        rows = pl.ds(k * capacity, capacity)
        turned = jnp.transpose(row_ref[role, rows, :]).reshape(capacity // 8, 8, capacity)
        best_ref[role, :, rows] = jnp.maximum(best_ref[role, :, rows], jnp.max(turned, axis=0))
    for role, out_ref in zip(done, out_refs):
        out_ref[...] = jnp.max(best_ref[role], axis=0, keepdims=True)


def spread_kernel(ring, offsets, groups, *refs):
    *partial_refs, out_ref = refs
    shards = len(ring)
    out_ref[...] = jnp.full(out_ref.shape, jnp.float32(LOW))
    shard, group = lax.axis_index("shard"), lax.axis_index("group")
    for offset, ref in zip(offsets, partial_refs):
        target = sum(
            jnp.where(shard == ring[e], ring[(e + offset) % shards], 0) for e in range(shards)
        )
        for k in range(groups):
            row = target * groups + (group ^ k)
            out_ref[pl.ds(row, 1)] = ref[:, k * LANES : (k + 1) * LANES].reshape(1, 1, LANES)


def place_kernel(groups, back_ref, place_ref, out_ref):
    place = place_ref[...]
    rows = place.shape[1]
    best = jnp.full((1, rows), jnp.float32(LOW))
    for g in range(groups):
        row = jnp.full((1, LANES), jnp.float32(-1.0))
        for s in range(back_ref.shape[0] // groups):
            row = jnp.maximum(row, back_ref[s * groups + g])
        values = jnp.concatenate([column_of(row)] * (rows // LANES), axis=1)
        here = lax.broadcasted_iota(jnp.int32, (LANES, rows), 0) + g * LANES == place
        best = jnp.maximum(
            best, jnp.max(jnp.where(here, values, jnp.float32(LOW)), axis=0, keepdims=True)
        )
    out_ref[...] = best


def in_vmem(count):
    return [pl.BlockSpec(memory_space=pltpu.VMEM)] * count


def call(
    kernel, out_shape, scratch, args, flops, bytes_accessed, in_specs=None, limit=48 * MIB
):
    return pl.pallas_call(
        kernel,
        out_shape=out_shape,
        in_specs=in_specs or in_vmem(len(args)),
        out_specs=in_vmem(len(out_shape)),
        scratch_shapes=scratch,
        compiler_params=pltpu.CompilerParams(vmem_limit_bytes=limit),
        cost_estimate=pl.CostEstimate(
            flops=flops, bytes_accessed=bytes_accessed, transcendentals=0
        ),
    )(*args)


def after(x, *earlier):
    return lax.optimization_barrier((x, *earlier))[0]


def stack(parts, wait):
    return call(
        stack_kernel,
        [jax.ShapeDtypeStruct((len(parts), *parts[0].shape), parts[0].dtype)],
        [],
        parts,
        wait,
        4 * len(parts) * parts[0].size,
    )[0]


def score(held, tasks, acc, done, last, slots, width):
    roles = len(held)
    used = sorted(
        {(left, k) for left, ks, _, _, _ in tasks for k in ks}
        | {(right, k) for _, _, right, ks, _ in tasks for k in ks},
        key=lambda x: (x[0], -x[1]),
    )
    arrays, sources = [], {}
    for role, k in used:
        array, part = held[role][k]
        index = next((i for i, x in enumerate(arrays) if x is array), len(arrays))
        if index == len(arrays):
            arrays.append(array)
        sources[role, k] = (index, part)
    ends = [jax.ShapeDtypeStruct((1, slots), jnp.float32)] * len(done)
    tiles = sum(len(task[1]) * len(task[3]) for task in tasks)
    best = [] if last else [jax.ShapeDtypeStruct((roles, 8, slots), jnp.float32)]
    got = call(
        lambda *refs: score_kernel(sources, tasks, done, last, *refs),
        best + ends,
        ([pltpu.VMEM((roles, 8, slots), jnp.float32)] if last else [])
        + [
            pltpu.VMEM((roles, slots, width), jnp.bfloat16),
            pltpu.VMEM((roles, slots, LANES), jnp.float32),
            pltpu.VMEM((roles, slots, LANES), jnp.float32),
        ],
        arrays + list(acc),
        2 * tiles * LANES * LANES * width,
        2 * len(used) * LANES * width,
    )
    return got[: len(best)], got[len(best) :]


def per_device(embeddings, row_group, row_cluster):
    rows, width = embeddings.shape
    groups = lax.axis_size("group")
    shards = lax.axis_size("shard")
    capacity = rows // 4
    slots = groups * capacity
    ring = ring_order(shards)
    offsets, pairs = offset_cover(shards)
    roles = len(offsets)
    height = width * capacity // LANES + TAIL

    def from_offset(x, offset):
        perm = [(ring[(e + offset) % shards], ring[e]) for e in range(shards)]
        return lax.ppermute(x, "shard", perm)

    def exchange(blocks):
        got = list(blocks)
        for k in range(1, groups):
            block = after(blocks[k], got[2]) if k > 2 else blocks[k]
            got[k] = lax.ppermute(block, "group", [(z, z ^ k) for z in range(groups)])
        return got

    (units,) = call(
        unit_kernel,
        [jax.ShapeDtypeStruct((rows, width), jnp.bfloat16)],
        [pltpu.VMEM((rows, width), embeddings.dtype), pltpu.SemaphoreType.DMA((4,))],
        (embeddings,),
        4 * rows * width,
        4 * rows * width,
        [pl.BlockSpec(memory_space=pltpu.HBM)],
        53 * MIB,
    )
    *send, place = call(
        lambda *refs: sort_kernel("group", *refs),
        [jax.ShapeDtypeStruct((height, LANES), jnp.bfloat16)] * groups
        + [jax.ShapeDtypeStruct((1, rows), jnp.int32)],
        [],
        (units, *lax.optimization_barrier((row_group.reshape(1, rows), row_cluster.reshape(1, rows)))),
        2 * rows * slots * width,
        4 * rows * width,
    )

    late = [groups - 1] if groups > 1 else []
    early = list(range(groups - len(late)))
    late = [groups - 1] if groups > 1 else []
    early = list(range(groups - len(late)))
    near = [r for r in range(1, roles) if 2 * offsets[r] != shards]
    far = [r for r in range(1, roles) if r not in near]
    first = {r: from_offset(send[0], offsets[r]) for r in near}
    own = exchange(send)
    held = [[None] * groups for _ in offsets]
    held[0] = [(x, None) for x in own]
    for r in near:
        held[r][0] = (first[r], None)
    for k in range(1, groups):
        if k == 1:
            block = after(own[k], first[near[0]]) if near else own[k]
        else:
            passed = [held[r][k - 2][0] for r in near]
            block = stack([after(own[k], *passed)], WAIT if k in late else WAIT // 20)
        for r in near:
            held[r][k] = (from_offset(block, offsets[r]), 0 if k > 1 else None)
    got = {r: from_offset(stack(own, 0), offsets[r]) for r in far}
    for r in far:
        held[r] = [(got[r], k) for k in range(groups)]
    everything = [(0, 0, False)]
    everything += [(offsets.index(a), offsets.index(b), both) for a, b, both in pairs]
    steps = [[] for _ in range(4)]
    final = [0] * roles
    for left, right, both in everything:
        for left_ks in (early, late):
            for right_ks in (early, late):
                if left_ks and right_ks:
                    step = 0
                    for role, ks in ((left, left_ks), (right, right_ks)):
                        if role in near:
                            step = max(step, 1 if ks is early else 3 if role == near[0] else 2)
                    task = (left, left_ks, right, right_ks, both)
                    if both and right_ks is late and left_ks is early:
                        task = (right, right_ks, left, left_ks, both)
                    steps[step].append(task)
                    final[right] = max(final[right], step)
                    if both:
                        final[left] = max(final[left], step)
    acc, partial = [], [None] * roles
    for step, tasks in enumerate(steps):
        if tasks:
            done = [r for r in range(roles) if final[r] == step]
            last = not any(steps[step + 1 :])
            acc, ends = score(held, tasks, acc, done, last, slots, width)
            for r, end in zip(done, ends):
                partial[r] = end
    (best,) = call(
        lambda *refs: spread_kernel(ring, offsets, groups, *refs),
        [jax.ShapeDtypeStruct((shards * groups, 1, capacity), jnp.float32)],
        [],
        partial,
        roles * slots,
        4 * roles * slots,
    )
    back = lax.all_to_all(best, ("shard", "group"), split_axis=0, concat_axis=0, tiled=True)
    (result,) = call(
        lambda *refs: place_kernel(groups, *refs),
        [jax.ShapeDtypeStruct((1, rows), jnp.float32)],
        [],
        [back, place],
        rows * slots,
        4 * slots,
    )
    return result.reshape(rows)


def solution(mesh):
    placed = (P(("shard", "group"), None), P(("shard", "group"), None), P(("shard", "group")))
    return jax.shard_map(
        per_device, mesh=mesh, in_specs=placed, out_specs=P(("shard", "group")), check_vma=False
    )
```

```python
import jax
import jax.numpy as jnp
from jax import lax
from jax.experimental import pallas as pl
from jax.experimental.pallas import tpu as pltpu
from jax.sharding import PartitionSpec as P

LANES = 128
TAIL = 16
LOW = -2.0
MIB = 1024 * 1024
WAIT = 2 * 10**10


def ring_order(size):
    if size % 2:
        return list(range(size))
    half = size // 2
    chips = [i ^ (i >> 1) for i in range(half)]
    if sorted(chips) != list(range(half)):
        chips = list(range(half))
    return [2 * chip + core for core in range(2) for chip in chips]


def offset_cover(size):
    offsets = list(dict.fromkeys([0, size // 2, 1 % size, (size - 1) % size]))

    def missing(chosen):
        have = {(a - b) % size for a in chosen for b in chosen}
        return [d for d in range(size) if d not in have]

    while missing(offsets):
        offsets.append(min(range(size), key=lambda x: len(missing(offsets + [x]))))
    pairs = []
    for diff in range(1, size // 2 + 1):
        found = [
            (a, b)
            for b in [(size - 1) % size] + offsets
            for a in offsets
            if (a - b) % size in (diff, size - diff)
        ]
        if 2 * diff == size:
            found = [(a, b) for a, b in found if b == 0] + found
        a, b = found[0]
        pairs.append((a, b, b != 0 or 2 * diff != size))
    return offsets, pairs


def column_of(row):
    size = row.shape[1]
    return jnp.transpose(jnp.broadcast_to(row, (size, size)))


def unit_kernel(far_ref, unit_ref, near_ref, sems):
    parts = sems.shape[0]
    size = far_ref.shape[0] // parts
    copies = [
        pltpu.make_async_copy(
            far_ref.at[pl.ds(i * size, size), :], near_ref.at[pl.ds(i * size, size), :], sems.at[i]
        )
        for i in range(parts)
    ]
    for copy in copies:
        copy.start()
    for i, copy in enumerate(copies):
        copy.wait()
        feats = near_ref[pl.ds(i * size, size), :].astype(jnp.float32)
        squares = jnp.sum(feats * feats, axis=1, keepdims=True) + 1e-06
        unit_ref[pl.ds(i * size, size), :] = (feats * lax.rsqrt(squares)).astype(jnp.bfloat16)


def sort_kernel(axis, unit_ref, group_ref, label_ref, *out_refs):
    *block_refs, place_ref = out_refs
    rows, width = unit_ref.shape
    groups = len(block_refs)
    capacity = (block_refs[0].shape[0] - TAIL) * LANES // width
    slots = groups * capacity
    chunks = width // LANES
    owner = group_ref[...]
    rel = owner ^ lax.axis_index(axis)
    lines = max(8, groups)
    onehot = lax.broadcasted_iota(jnp.int32, (lines, rows), 0) == rel
    before = lax.broadcasted_iota(jnp.int32, (rows, rows), 0) < lax.broadcasted_iota(
        jnp.int32, (rows, rows), 1
    )
    ranks = jnp.dot(
        jnp.where(onehot, 1.0, 0.0).astype(jnp.bfloat16),
        jnp.where(before, 1.0, 0.0).astype(jnp.bfloat16),
        preferred_element_type=jnp.float32,
    )
    rank = jnp.sum(jnp.where(onehot, ranks, 0.0), axis=0, keepdims=True).astype(jnp.int32)
    place_ref[...] = owner * capacity + rank
    move = jnp.where(
        lax.broadcasted_iota(jnp.int32, (slots, rows), 0) == rel * capacity + rank, 1.0, 0.0
    ).astype(jnp.bfloat16)
    labels = jnp.broadcast_to(label_ref[...] + 1, (TAIL, rows)).astype(jnp.bfloat16)
    sorted_labels = (
        lax.dot_general(
            labels, move, (((1,), (1,)), ((), ())), preferred_element_type=jnp.float32
        )
        - 1.0
    ).astype(jnp.bfloat16)
    for k, block_ref in enumerate(block_refs):
        part = slice(k * capacity, (k + 1) * capacity)
        block = jnp.dot(
            move[part], unit_ref[...], preferred_element_type=jnp.float32
        ).astype(jnp.bfloat16)
        for c in range(chunks):
            block_ref[pl.ds(c * capacity, capacity), :] = block[:, c * LANES : (c + 1) * LANES]
        block_ref[pl.ds(chunks * capacity, TAIL), :] = sorted_labels[:, part]


def stack_kernel(*refs):
    for k, ref in enumerate(refs[:-1]):
        refs[-1][k] = ref[...]


def score_kernel(sources, tasks, done, last, *refs):
    *refs, flat_ref, side_ref, row_ref = refs
    if last:
        *refs, best_ref = refs
        inputs, out_refs = refs[: -len(done)], refs[-len(done) :]
    else:
        outs = 1 + len(done)
        inputs, (best_ref, *out_refs) = refs[:-outs], refs[-outs:]
    capacity = LANES
    low = jnp.float32(LOW)
    arrays = 1 + max(index for index, _ in sources.values())
    best_ref[...] = inputs[arrays][...] if len(inputs) > arrays else jnp.full(best_ref.shape, low)
    tops = {}
    for (role, k), (index, part) in sources.items():
        ref = inputs[index] if part is None else inputs[index].at[part]
        height = ref.shape[0] - TAIL
        rows = pl.ds(k * capacity, capacity)
        for c in range(height // capacity):
            flat_ref[role, rows, pl.ds(c * LANES, LANES)] = ref[pl.ds(c * capacity, capacity), :]
        tops[role, k] = ref[pl.ds(height, TAIL), :][0:1].astype(jnp.float32)
    for role, k in sorted({(left, k) for left, ks, _, _, _ in tasks for k in ks}):
        side_ref[role, pl.ds(k * capacity, capacity), :] = column_of(tops[role, k])
    turns = sorted({(left, k) for left, ks, _, _, both in tasks if both for k in ks})
    for role, k in turns:
        row_ref[role, pl.ds(k * capacity, capacity), :] = jnp.full((capacity, LANES), low)
    for left, left_ks, right, right_ks, both in tasks:
        start, count = left_ks[0] * capacity, len(left_ks) * capacity
        rows = pl.ds(start, count)
        for i in range(0, len(right_ks), 2):
            some = right_ks[i : i + 2]
            width = len(some) * capacity
            columns = pl.ds(some[0] * capacity, width)
            scores = lax.dot_general(
                flat_ref[left, rows, :],
                flat_ref[right, columns, :],
                (((1,), (1,)), ((), ())),
                preferred_element_type=jnp.float32,
            )
            top = jnp.concatenate([tops[right, k] for k in some], axis=1)
            same = jnp.concatenate([side_ref[left, rows, :]] * len(some), axis=1) == top
            if left == right:
                same = same & (
                    lax.broadcasted_iota(jnp.int32, (count, width), 0) + start
                    != lax.broadcasted_iota(jnp.int32, (count, width), 1) + some[0] * capacity
                )
            scores = jnp.where(same, scores, low)
            if both:
                best = row_ref[left, rows, :]
                for c in range(len(some)):
                    best = jnp.maximum(best, scores[:, c * LANES : (c + 1) * LANES])
                row_ref[left, rows, :] = best
            best = jnp.max(scores.reshape(count // 8, 8, width), axis=0)
            best_ref[right, :, columns] = jnp.maximum(best_ref[right, :, columns], best)
    for role, k in turns:
        rows = pl.ds(k * capacity, capacity)
        turned = jnp.transpose(row_ref[role, rows, :]).reshape(capacity // 8, 8, capacity)
        best_ref[role, :, rows] = jnp.maximum(best_ref[role, :, rows], jnp.max(turned, axis=0))
    for role, out_ref in zip(done, out_refs):
        out_ref[...] = jnp.max(best_ref[role], axis=0, keepdims=True)


def spread_kernel(ring, offsets, groups, *refs):
    *partial_refs, out_ref = refs
    shards = len(ring)
    out_ref[...] = jnp.full(out_ref.shape, jnp.float32(LOW))
    shard, group = lax.axis_index("shard"), lax.axis_index("group")
    for offset, ref in zip(offsets, partial_refs):
        target = sum(
            jnp.where(shard == ring[e], ring[(e + offset) % shards], 0) for e in range(shards)
        )
        for k in range(groups):
            row = target * groups + (group ^ k)
            out_ref[pl.ds(row, 1)] = ref[:, k * LANES : (k + 1) * LANES].reshape(1, 1, LANES)


def place_kernel(groups, back_ref, place_ref, out_ref):
    place = place_ref[...]
    rows = place.shape[1]
    best = jnp.full((1, rows), jnp.float32(LOW))
    for g in range(groups):
        row = jnp.full((1, LANES), jnp.float32(-1.0))
        for s in range(back_ref.shape[0] // groups):
            row = jnp.maximum(row, back_ref[s * groups + g])
        values = jnp.concatenate([column_of(row)] * (rows // LANES), axis=1)
        here = lax.broadcasted_iota(jnp.int32, (LANES, rows), 0) + g * LANES == place
        best = jnp.maximum(
            best, jnp.max(jnp.where(here, values, jnp.float32(LOW)), axis=0, keepdims=True)
        )
    out_ref[...] = best


def in_vmem(count):
    return [pl.BlockSpec(memory_space=pltpu.VMEM)] * count


def call(
    kernel, out_shape, scratch, args, flops, bytes_accessed, in_specs=None, limit=48 * MIB
):
    return pl.pallas_call(
        kernel,
        out_shape=out_shape,
        in_specs=in_specs or in_vmem(len(args)),
        out_specs=in_vmem(len(out_shape)),
        scratch_shapes=scratch,
        compiler_params=pltpu.CompilerParams(vmem_limit_bytes=limit),
        cost_estimate=pl.CostEstimate(
            flops=flops, bytes_accessed=bytes_accessed, transcendentals=0
        ),
    )(*args)


def after(x, *earlier):
    return lax.optimization_barrier((x, *earlier))[0]


def stack(parts, wait):
    return call(
        stack_kernel,
        [jax.ShapeDtypeStruct((len(parts), *parts[0].shape), parts[0].dtype)],
        [],
        parts,
        wait,
        4 * len(parts) * parts[0].size,
    )[0]


def score(held, tasks, acc, done, last, slots, width):
    roles = len(held)
    used = sorted(
        {(left, k) for left, ks, _, _, _ in tasks for k in ks}
        | {(right, k) for _, _, right, ks, _ in tasks for k in ks},
        key=lambda x: (x[0], -x[1]),
    )
    arrays, sources = [], {}
    for role, k in used:
        array, part = held[role][k]
        index = next((i for i, x in enumerate(arrays) if x is array), len(arrays))
        if index == len(arrays):
            arrays.append(array)
        sources[role, k] = (index, part)
    ends = [jax.ShapeDtypeStruct((1, slots), jnp.float32)] * len(done)
    tiles = sum(len(task[1]) * len(task[3]) for task in tasks)
    best = [] if last else [jax.ShapeDtypeStruct((roles, 8, slots), jnp.float32)]
    got = call(
        lambda *refs: score_kernel(sources, tasks, done, last, *refs),
        best + ends,
        ([pltpu.VMEM((roles, 8, slots), jnp.float32)] if last else [])
        + [
            pltpu.VMEM((roles, slots, width), jnp.bfloat16),
            pltpu.VMEM((roles, slots, LANES), jnp.float32),
            pltpu.VMEM((roles, slots, LANES), jnp.float32),
        ],
        arrays + list(acc),
        2 * tiles * LANES * LANES * width,
        2 * len(used) * LANES * width,
    )
    return got[: len(best)], got[len(best) :]


def per_device(embeddings, row_group, row_cluster):
    rows, width = embeddings.shape
    groups = lax.axis_size("group")
    shards = lax.axis_size("shard")
    capacity = rows // 4
    slots = groups * capacity
    ring = ring_order(shards)
    offsets, pairs = offset_cover(shards)
    roles = len(offsets)
    height = width * capacity // LANES + TAIL

    def from_offset(x, offset):
        perm = [(ring[(e + offset) % shards], ring[e]) for e in range(shards)]
        return lax.ppermute(x, "shard", perm)

    def exchange(blocks):
        got = list(blocks)
        for k in range(1, groups):
            block = after(blocks[k], got[1]) if k > 2 else blocks[k]
            got[k] = lax.ppermute(block, "group", [(z, z ^ k) for z in range(groups)])
        return got

    (units,) = call(
        unit_kernel,
        [jax.ShapeDtypeStruct((rows, width), jnp.bfloat16)],
        [pltpu.VMEM((rows, width), embeddings.dtype), pltpu.SemaphoreType.DMA((4,))],
        (embeddings,),
        4 * rows * width,
        4 * rows * width,
        [pl.BlockSpec(memory_space=pltpu.HBM)],
        53 * MIB,
    )
    *send, place = call(
        lambda *refs: sort_kernel("group", *refs),
        [jax.ShapeDtypeStruct((height, LANES), jnp.bfloat16)] * groups
        + [jax.ShapeDtypeStruct((1, rows), jnp.int32)],
        [],
        (units, *lax.optimization_barrier((row_group.reshape(1, rows), row_cluster.reshape(1, rows)))),
        2 * rows * slots * width,
        4 * rows * width,
    )

    late = [groups - 1] if groups > 1 else []
    early = list(range(groups - len(late)))
    late = [groups - 1] if groups > 1 else []
    early = list(range(groups - len(late)))
    near = [r for r in range(1, roles) if 2 * offsets[r] != shards]
    far = [r for r in range(1, roles) if r not in near]
    first = {r: from_offset(send[0], offsets[r]) for r in near}
    own = exchange(send)
    held = [[None] * groups for _ in offsets]
    held[0] = [(x, None) for x in own]
    for r in near:
        held[r][0] = (first[r], None)
    for k in range(1, groups):
        if k == 1:
            block = after(own[k], *first.values())
        else:
            passed = [held[r][k - 2][0] for r in near]
            block = stack([after(own[k], *passed)], WAIT)
        for r in near:
            held[r][k] = (from_offset(block, offsets[r]), 0 if k > 1 else None)
    got = {r: from_offset(stack(own, 0), offsets[r]) for r in far}
    for r in far:
        held[r] = [(got[r], k) for k in range(groups)]
    everything = [(0, 0, False)]
    everything += [(offsets.index(a), offsets.index(b), both) for a, b, both in pairs]
    steps = [[] for _ in range(4)]
    final = [0] * roles
    for left, right, both in everything:
        for left_ks in (early, late):
            for right_ks in (early, late):
                if left_ks and right_ks:
                    step = 0
                    for role, ks in ((left, left_ks), (right, right_ks)):
                        if role in near:
                            step = max(step, 1 if ks is early else 3 if role == near[0] else 2)
                    task = (left, left_ks, right, right_ks, both)
                    if both and right_ks is late and left_ks is early:
                        task = (right, right_ks, left, left_ks, both)
                    steps[step].append(task)
                    final[right] = max(final[right], step)
                    if both:
                        final[left] = max(final[left], step)
    acc, partial = [], [None] * roles
    for step, tasks in enumerate(steps):
        if tasks:
            done = [r for r in range(roles) if final[r] == step]
            last = not any(steps[step + 1 :])
            acc, ends = score(held, tasks, acc, done, last, slots, width)
            for r, end in zip(done, ends):
                partial[r] = end
    (best,) = call(
        lambda *refs: spread_kernel(ring, offsets, groups, *refs),
        [jax.ShapeDtypeStruct((shards * groups, 1, capacity), jnp.float32)],
        [],
        partial,
        roles * slots,
        4 * roles * slots,
    )
    back = lax.all_to_all(best, ("shard", "group"), split_axis=0, concat_axis=0, tiled=True)
    (result,) = call(
        lambda *refs: place_kernel(groups, *refs),
        [jax.ShapeDtypeStruct((1, rows), jnp.float32)],
        [],
        [back, place],
        rows * slots,
        4 * slots,
    )
    return result.reshape(rows)


def solution(mesh):
    placed = (P(("shard", "group"), None), P(("shard", "group"), None), P(("shard", "group")))
    return jax.shard_map(
        per_device, mesh=mesh, in_specs=placed, out_specs=P(("shard", "group")), check_vma=False
    )
```

```python
import jax
import jax.numpy as jnp
from jax import lax
from jax.experimental import pallas as pl
from jax.experimental.pallas import tpu as pltpu
from jax.sharding import PartitionSpec as P

LANES = 128
TAIL = 16
LOW = -2.0
MIB = 1024 * 1024
WAIT = 2 * 10**10


def ring_order(size):
    if size % 2:
        return list(range(size))
    half = size // 2
    chips = [i ^ (i >> 1) for i in range(half)]
    if sorted(chips) != list(range(half)):
        chips = list(range(half))
    return [2 * chip + core for core in range(2) for chip in chips]


def offset_cover(size):
    offsets = list(dict.fromkeys([0, size // 2, 1 % size, (size - 1) % size]))

    def missing(chosen):
        have = {(a - b) % size for a in chosen for b in chosen}
        return [d for d in range(size) if d not in have]

    while missing(offsets):
        offsets.append(min(range(size), key=lambda x: len(missing(offsets + [x]))))
    pairs = []
    for diff in range(1, size // 2 + 1):
        found = [
            (a, b)
            for b in [(size - 1) % size] + offsets
            for a in offsets
            if (a - b) % size in (diff, size - diff)
        ]
        if 2 * diff == size:
            found = [(a, b) for a, b in found if b == 0] + found
        a, b = found[0]
        pairs.append((a, b, b != 0 or 2 * diff != size))
    return offsets, pairs


def column_of(row):
    size = row.shape[1]
    return jnp.transpose(jnp.broadcast_to(row, (size, size)))


def unit_kernel(far_ref, unit_ref, near_ref, sems):
    parts = sems.shape[0]
    size = far_ref.shape[0] // parts
    copies = [
        pltpu.make_async_copy(
            far_ref.at[pl.ds(i * size, size), :], near_ref.at[pl.ds(i * size, size), :], sems.at[i]
        )
        for i in range(parts)
    ]
    for copy in copies:
        copy.start()
    for i, copy in enumerate(copies):
        copy.wait()
        feats = near_ref[pl.ds(i * size, size), :].astype(jnp.float32)
        squares = jnp.sum(feats * feats, axis=1, keepdims=True) + 1e-06
        unit_ref[pl.ds(i * size, size), :] = (feats * lax.rsqrt(squares)).astype(jnp.bfloat16)


def sort_kernel(axis, unit_ref, group_ref, label_ref, *out_refs):
    *block_refs, place_ref = out_refs
    rows, width = unit_ref.shape
    groups = len(block_refs)
    capacity = (block_refs[0].shape[0] - TAIL) * LANES // width
    slots = groups * capacity
    chunks = width // LANES
    owner = group_ref[...]
    rel = owner ^ lax.axis_index(axis)
    lines = max(8, groups)
    onehot = lax.broadcasted_iota(jnp.int32, (lines, rows), 0) == rel
    before = lax.broadcasted_iota(jnp.int32, (rows, rows), 0) < lax.broadcasted_iota(
        jnp.int32, (rows, rows), 1
    )
    ranks = jnp.dot(
        jnp.where(onehot, 1.0, 0.0).astype(jnp.bfloat16),
        jnp.where(before, 1.0, 0.0).astype(jnp.bfloat16),
        preferred_element_type=jnp.float32,
    )
    rank = jnp.sum(jnp.where(onehot, ranks, 0.0), axis=0, keepdims=True).astype(jnp.int32)
    place_ref[...] = owner * capacity + rank
    move = jnp.where(
        lax.broadcasted_iota(jnp.int32, (slots, rows), 0) == rel * capacity + rank, 1.0, 0.0
    ).astype(jnp.bfloat16)
    labels = jnp.broadcast_to(label_ref[...] + 1, (TAIL, rows)).astype(jnp.bfloat16)
    sorted_labels = (
        lax.dot_general(
            labels, move, (((1,), (1,)), ((), ())), preferred_element_type=jnp.float32
        )
        - 1.0
    ).astype(jnp.bfloat16)
    for k, block_ref in enumerate(block_refs):
        part = slice(k * capacity, (k + 1) * capacity)
        block = jnp.dot(
            move[part], unit_ref[...], preferred_element_type=jnp.float32
        ).astype(jnp.bfloat16)
        for c in range(chunks):
            block_ref[pl.ds(c * capacity, capacity), :] = block[:, c * LANES : (c + 1) * LANES]
        block_ref[pl.ds(chunks * capacity, TAIL), :] = sorted_labels[:, part]


def stack_kernel(*refs):
    for k, ref in enumerate(refs[:-1]):
        refs[-1][k] = ref[...]


def score_kernel(sources, flats, layout, tasks, done, last, *refs):
    *refs, side_ref, row_ref = refs
    if last:
        *refs, best_ref, flat_ref = refs
        inputs, out_refs = refs[: -len(done)], refs[-len(done) :]
    else:
        outs = 2 + len(done)
        inputs, (best_ref, flat_ref, *out_refs) = refs[:-outs], refs[-outs:]
    capacity = LANES
    low = jnp.float32(LOW)
    arrays = 1 + max(index for index, _ in sources.values())
    best_ref[...] = inputs[arrays][...] if len(inputs) > arrays else jnp.full(best_ref.shape, low)

    def units(role, ks):
        rows = pl.ds(ks[0] * capacity, len(ks) * capacity)
        if (role, ks[0]) in flats:
            index, place = flats[role, ks[0]]
            return inputs[arrays + 1 + index][place, rows, :]
        return flat_ref[layout.index(role), rows, :]

    tops = {}
    for (role, k), (index, part) in sources.items():
        ref = inputs[index] if part is None else inputs[index].at[part]
        height = ref.shape[0] - TAIL
        rows = pl.ds(k * capacity, capacity)
        if (role, k) not in flats:
            for c in range(height // capacity):
                flat_ref[layout.index(role), rows, pl.ds(c * LANES, LANES)] = ref[
                    pl.ds(c * capacity, capacity), :
                ]
        tops[role, k] = ref[pl.ds(height, TAIL), :][0:1].astype(jnp.float32)
    for role, k in sorted({(left, k) for left, ks, _, _, _ in tasks for k in ks}):
        side_ref[role, pl.ds(k * capacity, capacity), :] = column_of(tops[role, k])
    turns = sorted({(left, k) for left, ks, _, _, both in tasks if both for k in ks})
    for role, k in turns:
        row_ref[role, pl.ds(k * capacity, capacity), :] = jnp.full((capacity, LANES), low)
    for left, left_ks, right, right_ks, both in tasks:
        start, count = left_ks[0] * capacity, len(left_ks) * capacity
        rows = pl.ds(start, count)
        for i in range(0, len(right_ks), 2):
            some = right_ks[i : i + 2]
            width = len(some) * capacity
            columns = pl.ds(some[0] * capacity, width)
            scores = lax.dot_general(
                units(left, left_ks),
                units(right, some),
                (((1,), (1,)), ((), ())),
                preferred_element_type=jnp.float32,
            )
            top = jnp.concatenate([tops[right, k] for k in some], axis=1)
            same = jnp.concatenate([side_ref[left, rows, :]] * len(some), axis=1) == top
            if left == right:
                same = same & (
                    lax.broadcasted_iota(jnp.int32, (count, width), 0) + start
                    != lax.broadcasted_iota(jnp.int32, (count, width), 1) + some[0] * capacity
                )
            scores = jnp.where(same, scores, low)
            if both:
                best = row_ref[left, rows, :]
                for c in range(len(some)):
                    best = jnp.maximum(best, scores[:, c * LANES : (c + 1) * LANES])
                row_ref[left, rows, :] = best
            best = jnp.max(scores.reshape(count // 8, 8, width), axis=0)
            best_ref[right, :, columns] = jnp.maximum(best_ref[right, :, columns], best)
    for role, k in turns:
        rows = pl.ds(k * capacity, capacity)
        turned = jnp.transpose(row_ref[role, rows, :]).reshape(capacity // 8, 8, capacity)
        best_ref[role, :, rows] = jnp.maximum(best_ref[role, :, rows], jnp.max(turned, axis=0))
    for role, out_ref in zip(done, out_refs):
        out_ref[...] = jnp.max(best_ref[role], axis=0, keepdims=True)


def spread_kernel(ring, offsets, groups, *refs):
    *partial_refs, out_ref = refs
    shards = len(ring)
    out_ref[...] = jnp.full(out_ref.shape, jnp.float32(LOW))
    shard, group = lax.axis_index("shard"), lax.axis_index("group")
    for offset, ref in zip(offsets, partial_refs):
        target = sum(
            jnp.where(shard == ring[e], ring[(e + offset) % shards], 0) for e in range(shards)
        )
        for k in range(groups):
            row = target * groups + (group ^ k)
            out_ref[pl.ds(row, 1)] = ref[:, k * LANES : (k + 1) * LANES].reshape(1, 1, LANES)


def place_kernel(groups, back_ref, place_ref, out_ref):
    place = place_ref[...]
    rows = place.shape[1]
    best = jnp.full((1, rows), jnp.float32(LOW))
    for g in range(groups):
        row = jnp.full((1, LANES), jnp.float32(-1.0))
        for s in range(back_ref.shape[0] // groups):
            row = jnp.maximum(row, back_ref[s * groups + g])
        values = jnp.concatenate([column_of(row)] * (rows // LANES), axis=1)
        here = lax.broadcasted_iota(jnp.int32, (LANES, rows), 0) + g * LANES == place
        best = jnp.maximum(
            best, jnp.max(jnp.where(here, values, jnp.float32(LOW)), axis=0, keepdims=True)
        )
    out_ref[...] = best


def in_vmem(count):
    return [pl.BlockSpec(memory_space=pltpu.VMEM)] * count


def call(
    kernel, out_shape, scratch, args, flops, bytes_accessed, in_specs=None, limit=24 * MIB
):
    return pl.pallas_call(
        kernel,
        out_shape=out_shape,
        in_specs=in_specs or in_vmem(len(args)),
        out_specs=in_vmem(len(out_shape)),
        scratch_shapes=scratch,
        compiler_params=pltpu.CompilerParams(vmem_limit_bytes=limit),
        cost_estimate=pl.CostEstimate(
            flops=flops, bytes_accessed=bytes_accessed, transcendentals=0
        ),
    )(*args)


def after(x, *earlier):
    return lax.optimization_barrier((x, *earlier))[0]


def stack(parts, wait):
    return call(
        stack_kernel,
        [jax.ShapeDtypeStruct((len(parts), *parts[0].shape), parts[0].dtype)],
        [],
        parts,
        wait,
        4 * len(parts) * parts[0].size,
    )[0]


def score(held, tasks, acc, flats, done, last, slots, width):
    roles = len(held)
    used = sorted(
        {(left, k) for left, ks, _, _, _ in tasks for k in ks}
        | {(right, k) for _, _, right, ks, _ in tasks for k in ks},
        key=lambda x: (x[0], -x[1]),
    )
    arrays, sources = [], {}
    for role, k in used:
        array, part = held[role][k]
        index = next((i for i, x in enumerate(arrays) if x is array), len(arrays))
        if index == len(arrays):
            arrays.append(array)
        sources[role, k] = (index, part)
    layout = sorted({role for role, k in used if (role, k) not in flats})
    tiles = sum(len(task[1]) * len(task[3]) for task in tasks)
    kept = [
        jax.ShapeDtypeStruct((roles, 8, slots), jnp.float32),
        jax.ShapeDtypeStruct((len(layout), slots, width), jnp.bfloat16),
    ]
    scratch = [pltpu.VMEM((roles, slots, LANES), jnp.float32)] * 2
    if last:
        scratch = [pltpu.VMEM(x.shape, x.dtype) for x in kept] + scratch
        kept = []
    known = dict(flats)
    got = call(
        lambda *refs: score_kernel(sources, known, layout, tasks, done, last, *refs),
        kept + [jax.ShapeDtypeStruct((1, slots), jnp.float32)] * len(done),
        scratch,
        arrays + list(acc),
        2 * tiles * LANES * LANES * width,
        2 * len(used) * LANES * width,
    )
    if last:
        return acc, got
    for role, k in used:
        if (role, k) not in flats:
            flats[role, k] = (max(len(acc) - 1, 0), layout.index(role))
    return [got[0], *acc[1:], got[1]], got[2:]


def per_device(embeddings, row_group, row_cluster):
    rows, width = embeddings.shape
    groups = lax.axis_size("group")
    shards = lax.axis_size("shard")
    capacity = rows // 4
    slots = groups * capacity
    ring = ring_order(shards)
    offsets, pairs = offset_cover(shards)
    roles = len(offsets)
    height = width * capacity // LANES + TAIL

    def from_offset(x, offset):
        perm = [(ring[(e + offset) % shards], ring[e]) for e in range(shards)]
        return lax.ppermute(x, "shard", perm)

    def exchange(blocks):
        got = list(blocks)
        for k in range(1, groups):
            block = after(blocks[k], got[1]) if k > 2 else blocks[k]
            got[k] = lax.ppermute(block, "group", [(z, z ^ k) for z in range(groups)])
        return got

    (units,) = call(
        unit_kernel,
        [jax.ShapeDtypeStruct((rows, width), jnp.bfloat16)],
        [pltpu.VMEM((rows, width), embeddings.dtype), pltpu.SemaphoreType.DMA((4,))],
        (embeddings,),
        4 * rows * width,
        4 * rows * width,
        [pl.BlockSpec(memory_space=pltpu.HBM)],
        53 * MIB,
    )
    *send, place = call(
        lambda *refs: sort_kernel("group", *refs),
        [jax.ShapeDtypeStruct((height, LANES), jnp.bfloat16)] * groups
        + [jax.ShapeDtypeStruct((1, rows), jnp.int32)],
        [],
        (units, *lax.optimization_barrier((row_group.reshape(1, rows), row_cluster.reshape(1, rows)))),
        2 * rows * slots * width,
        4 * rows * width,
    )

    late = [groups - 1] if groups > 1 else []
    early = list(range(groups - len(late)))
    late = [groups - 1] if groups > 1 else []
    early = list(range(groups - len(late)))
    near = [r for r in range(1, roles) if 2 * offsets[r] != shards]
    far = [r for r in range(1, roles) if r not in near]
    first = {r: from_offset(send[0], offsets[r]) for r in near}
    own = exchange(send)
    held = [[None] * groups for _ in offsets]
    held[0] = [(x, None) for x in own]
    for r in near:
        held[r][0] = (first[r], None)
    for k in range(1, groups):
        if k == 1:
            block = after(own[k], first[near[0]]) if near else own[k]
        else:
            passed = [held[r][k - 2][0] for r in near]
            block = stack([after(own[k], *passed)], WAIT)
        for r in near:
            held[r][k] = (from_offset(block, offsets[r]), 0 if k > 1 else None)
    got = {r: from_offset(stack(own, 0), offsets[r]) for r in far}
    for r in far:
        held[r] = [(got[r], k) for k in range(groups)]
    everything = [(0, 0, False)]
    everything += [(offsets.index(a), offsets.index(b), both) for a, b, both in pairs]
    steps = [[] for _ in range(3)]
    final = [0] * roles
    for left, right, both in everything:
        for left_ks in (early, late):
            for right_ks in (early, late):
                if left_ks and right_ks:
                    step = 0
                    for role, ks in ((left, left_ks), (right, right_ks)):
                        if role in near:
                            step = max(step, 1 if ks is early else 2)
                    task = (left, left_ks, right, right_ks, both)
                    if both and right_ks is late and left_ks is early:
                        task = (right, right_ks, left, left_ks, both)
                    steps[step].append(task)
                    final[right] = max(final[right], step)
                    if both:
                        final[left] = max(final[left], step)
    acc, flats, partial = [], {}, [None] * roles
    for step, tasks in enumerate(steps):
        if tasks:
            done = [r for r in range(roles) if final[r] == step]
            last = not any(steps[step + 1 :])
            acc, ends = score(held, tasks, acc, flats, done, last, slots, width)
            for r, end in zip(done, ends):
                partial[r] = end
    (best,) = call(
        lambda *refs: spread_kernel(ring, offsets, groups, *refs),
        [jax.ShapeDtypeStruct((shards * groups, 1, capacity), jnp.float32)],
        [],
        partial,
        roles * slots,
        4 * roles * slots,
    )
    back = lax.all_to_all(best, ("shard", "group"), split_axis=0, concat_axis=0, tiled=True)
    (result,) = call(
        lambda *refs: place_kernel(groups, *refs),
        [jax.ShapeDtypeStruct((1, rows), jnp.float32)],
        [],
        [back, place],
        rows * slots,
        4 * slots,
    )
    return result.reshape(rows)


def solution(mesh):
    placed = (P(("shard", "group"), None), P(("shard", "group"), None), P(("shard", "group")))
    return jax.shard_map(
        per_device, mesh=mesh, in_specs=placed, out_specs=P(("shard", "group")), check_vma=False
    )
```

```python
import jax
import jax.numpy as jnp
from jax import lax
from jax.experimental import pallas as pl
from jax.experimental.pallas import tpu as pltpu
from jax.sharding import PartitionSpec as P

LANES = 128
TAIL = 16
LOW = -2.0
MIB = 1024 * 1024
WAIT = 2 * 10**10


def ring_order(size):
    if size % 2:
        return list(range(size))
    half = size // 2
    chips = [i ^ (i >> 1) for i in range(half)]
    if sorted(chips) != list(range(half)):
        chips = list(range(half))
    return [2 * chip + core for core in range(2) for chip in chips]


def offset_cover(size):
    offsets = list(dict.fromkeys([0, size // 2, 1 % size, (size - 1) % size]))

    def missing(chosen):
        have = {(a - b) % size for a in chosen for b in chosen}
        return [d for d in range(size) if d not in have]

    while missing(offsets):
        offsets.append(min(range(size), key=lambda x: len(missing(offsets + [x]))))
    pairs = []
    for diff in range(1, size // 2 + 1):
        found = [
            (a, b)
            for b in [(size - 1) % size] + offsets
            for a in offsets
            if (a - b) % size in (diff, size - diff)
        ]
        if 2 * diff == size:
            found = [(a, b) for a, b in found if b == 0] + found
        a, b = found[0]
        pairs.append((a, b, b != 0 or 2 * diff != size))
    return offsets, pairs


def column_of(row):
    size = row.shape[1]
    return jnp.transpose(jnp.broadcast_to(row, (size, size)))


def unit_kernel(far_ref, unit_ref, near_ref, sems):
    parts = sems.shape[0]
    size = far_ref.shape[0] // parts
    copies = [
        pltpu.make_async_copy(
            far_ref.at[pl.ds(i * size, size), :], near_ref.at[pl.ds(i * size, size), :], sems.at[i]
        )
        for i in range(parts)
    ]
    for copy in copies:
        copy.start()
    for i, copy in enumerate(copies):
        copy.wait()
        feats = near_ref[pl.ds(i * size, size), :].astype(jnp.float32)
        squares = jnp.sum(feats * feats, axis=1, keepdims=True) + 1e-06
        unit_ref[pl.ds(i * size, size), :] = (feats * lax.rsqrt(squares)).astype(jnp.bfloat16)


def sort_kernel(axis, unit_ref, group_ref, label_ref, *out_refs):
    *block_refs, place_ref = out_refs
    rows, width = unit_ref.shape
    groups = len(block_refs)
    capacity = (block_refs[0].shape[0] - TAIL) * LANES // width
    slots = groups * capacity
    chunks = width // LANES
    owner = group_ref[...]
    rel = owner ^ lax.axis_index(axis)
    lines = max(8, groups)
    onehot = lax.broadcasted_iota(jnp.int32, (lines, rows), 0) == rel
    before = lax.broadcasted_iota(jnp.int32, (rows, rows), 0) < lax.broadcasted_iota(
        jnp.int32, (rows, rows), 1
    )
    ranks = jnp.dot(
        jnp.where(onehot, 1.0, 0.0).astype(jnp.bfloat16),
        jnp.where(before, 1.0, 0.0).astype(jnp.bfloat16),
        preferred_element_type=jnp.float32,
    )
    rank = jnp.sum(jnp.where(onehot, ranks, 0.0), axis=0, keepdims=True).astype(jnp.int32)
    place_ref[...] = owner * capacity + rank
    move = jnp.where(
        lax.broadcasted_iota(jnp.int32, (slots, rows), 0) == rel * capacity + rank, 1.0, 0.0
    ).astype(jnp.bfloat16)
    labels = jnp.broadcast_to(label_ref[...] + 1, (TAIL, rows)).astype(jnp.bfloat16)
    sorted_labels = (
        lax.dot_general(
            labels, move, (((1,), (1,)), ((), ())), preferred_element_type=jnp.float32
        )
        - 1.0
    ).astype(jnp.bfloat16)
    for k, block_ref in enumerate(block_refs):
        part = slice(k * capacity, (k + 1) * capacity)
        block = jnp.dot(
            move[part], unit_ref[...], preferred_element_type=jnp.float32
        ).astype(jnp.bfloat16)
        for c in range(chunks):
            block_ref[pl.ds(c * capacity, capacity), :] = block[:, c * LANES : (c + 1) * LANES]
        block_ref[pl.ds(chunks * capacity, TAIL), :] = sorted_labels[:, part]


def stack_kernel(*refs):
    for k, ref in enumerate(refs[:-1]):
        refs[-1][k] = ref[...]


def score_kernel(sources, flats, layout, tasks, done, last, *refs):
    *refs, side_ref, row_ref = refs
    if last:
        *refs, best_ref, flat_ref = refs
        inputs, out_refs = refs[: -len(done)], refs[-len(done) :]
    else:
        outs = 2 + len(done)
        inputs, (best_ref, flat_ref, *out_refs) = refs[:-outs], refs[-outs:]
    capacity = LANES
    low = jnp.float32(LOW)
    arrays = 1 + max(index for index, _ in sources.values())
    best_ref[...] = inputs[arrays][...] if len(inputs) > arrays else jnp.full(best_ref.shape, low)

    def units(role, ks):
        rows = pl.ds(ks[0] * capacity, len(ks) * capacity)
        if (role, ks[0]) in flats:
            index, place = flats[role, ks[0]]
            return inputs[arrays + 1 + index][place, rows, :]
        return flat_ref[layout.index(role), rows, :]

    tops = {}
    for (role, k), (index, part) in sources.items():
        ref = inputs[index] if part is None else inputs[index].at[part]
        height = ref.shape[0] - TAIL
        rows = pl.ds(k * capacity, capacity)
        if (role, k) not in flats:
            for c in range(height // capacity):
                flat_ref[layout.index(role), rows, pl.ds(c * LANES, LANES)] = ref[
                    pl.ds(c * capacity, capacity), :
                ]
        tops[role, k] = ref[pl.ds(height, TAIL), :][0:1].astype(jnp.float32)
    for role, k in sorted({(left, k) for left, ks, _, _, _ in tasks for k in ks}):
        side_ref[role, pl.ds(k * capacity, capacity), :] = column_of(tops[role, k])
    turns = sorted({(left, k) for left, ks, _, _, both in tasks if both for k in ks})
    for role, k in turns:
        row_ref[role, pl.ds(k * capacity, capacity), :] = jnp.full((capacity, LANES), low)
    for left, left_ks, right, right_ks, both in tasks:
        start, count = left_ks[0] * capacity, len(left_ks) * capacity
        rows = pl.ds(start, count)
        for i in range(0, len(right_ks), 2):
            some = right_ks[i : i + 2]
            width = len(some) * capacity
            columns = pl.ds(some[0] * capacity, width)
            scores = lax.dot_general(
                units(left, left_ks),
                units(right, some),
                (((1,), (1,)), ((), ())),
                preferred_element_type=jnp.float32,
            )
            top = jnp.concatenate([tops[right, k] for k in some], axis=1)
            same = jnp.concatenate([side_ref[left, rows, :]] * len(some), axis=1) == top
            if left == right:
                same = same & (
                    lax.broadcasted_iota(jnp.int32, (count, width), 0) + start
                    != lax.broadcasted_iota(jnp.int32, (count, width), 1) + some[0] * capacity
                )
            scores = jnp.where(same, scores, low)
            if both:
                best = row_ref[left, rows, :]
                for c in range(len(some)):
                    best = jnp.maximum(best, scores[:, c * LANES : (c + 1) * LANES])
                row_ref[left, rows, :] = best
            best = jnp.max(scores.reshape(count // 8, 8, width), axis=0)
            best_ref[right, :, columns] = jnp.maximum(best_ref[right, :, columns], best)
    for role, k in turns:
        rows = pl.ds(k * capacity, capacity)
        turned = jnp.transpose(row_ref[role, rows, :]).reshape(capacity // 8, 8, capacity)
        best_ref[role, :, rows] = jnp.maximum(best_ref[role, :, rows], jnp.max(turned, axis=0))
    for role, out_ref in zip(done, out_refs):
        out_ref[...] = jnp.max(best_ref[role], axis=0, keepdims=True)


def spread_kernel(ring, offsets, groups, *refs):
    *partial_refs, out_ref = refs
    shards = len(ring)
    out_ref[...] = jnp.full(out_ref.shape, jnp.float32(LOW))
    shard, group = lax.axis_index("shard"), lax.axis_index("group")
    for offset, ref in zip(offsets, partial_refs):
        target = sum(
            jnp.where(shard == ring[e], ring[(e + offset) % shards], 0) for e in range(shards)
        )
        for k in range(groups):
            row = target * groups + (group ^ k)
            out_ref[pl.ds(row, 1)] = ref[:, k * LANES : (k + 1) * LANES].reshape(1, 1, LANES)


def place_kernel(groups, back_ref, place_ref, out_ref):
    place = place_ref[...]
    rows = place.shape[1]
    best = jnp.full((1, rows), jnp.float32(LOW))
    for g in range(groups):
        row = jnp.full((1, LANES), jnp.float32(-1.0))
        for s in range(back_ref.shape[0] // groups):
            row = jnp.maximum(row, back_ref[s * groups + g])
        values = jnp.concatenate([column_of(row)] * (rows // LANES), axis=1)
        here = lax.broadcasted_iota(jnp.int32, (LANES, rows), 0) + g * LANES == place
        best = jnp.maximum(
            best, jnp.max(jnp.where(here, values, jnp.float32(LOW)), axis=0, keepdims=True)
        )
    out_ref[...] = best


def in_vmem(count):
    return [pl.BlockSpec(memory_space=pltpu.VMEM)] * count


def call(
    kernel, out_shape, scratch, args, flops, bytes_accessed, in_specs=None, limit=24 * MIB
):
    return pl.pallas_call(
        kernel,
        out_shape=out_shape,
        in_specs=in_specs or in_vmem(len(args)),
        out_specs=in_vmem(len(out_shape)),
        scratch_shapes=scratch,
        compiler_params=pltpu.CompilerParams(vmem_limit_bytes=limit),
        cost_estimate=pl.CostEstimate(
            flops=flops, bytes_accessed=bytes_accessed, transcendentals=0
        ),
    )(*args)


def after(x, *earlier):
    return lax.optimization_barrier((x, *earlier))[0]


def stack(parts, wait):
    return call(
        stack_kernel,
        [jax.ShapeDtypeStruct((len(parts), *parts[0].shape), parts[0].dtype)],
        [],
        parts,
        wait,
        4 * len(parts) * parts[0].size,
    )[0]


def score(held, tasks, acc, flats, done, last, slots, width):
    roles = len(held)
    used = sorted(
        {(left, k) for left, ks, _, _, _ in tasks for k in ks}
        | {(right, k) for _, _, right, ks, _ in tasks for k in ks},
        key=lambda x: (x[0], -x[1]),
    )
    arrays, sources = [], {}
    for role, k in used:
        array, part = held[role][k]
        index = next((i for i, x in enumerate(arrays) if x is array), len(arrays))
        if index == len(arrays):
            arrays.append(array)
        sources[role, k] = (index, part)
    layout = sorted({role for role, k in used if (role, k) not in flats})
    tiles = sum(len(task[1]) * len(task[3]) for task in tasks)
    kept = [
        jax.ShapeDtypeStruct((roles, 8, slots), jnp.float32),
        jax.ShapeDtypeStruct((len(layout), slots, width), jnp.bfloat16),
    ]
    scratch = [pltpu.VMEM((roles, slots, LANES), jnp.float32)] * 2
    if last:
        scratch = [pltpu.VMEM(x.shape, x.dtype) for x in kept] + scratch
        kept = []
    known = dict(flats)
    got = call(
        lambda *refs: score_kernel(sources, known, layout, tasks, done, last, *refs),
        kept + [jax.ShapeDtypeStruct((1, slots), jnp.float32)] * len(done),
        scratch,
        arrays + list(acc),
        2 * tiles * LANES * LANES * width,
        2 * len(used) * LANES * width,
    )
    if last:
        return acc, got
    for role, k in used:
        if (role, k) not in flats:
            flats[role, k] = (max(len(acc) - 1, 0), layout.index(role))
    return [got[0], *acc[1:], got[1]], got[2:]


def per_device(embeddings, row_group, row_cluster):
    rows, width = embeddings.shape
    groups = lax.axis_size("group")
    shards = lax.axis_size("shard")
    capacity = rows // 4
    slots = groups * capacity
    ring = ring_order(shards)
    offsets, pairs = offset_cover(shards)
    roles = len(offsets)
    height = width * capacity // LANES + TAIL

    def from_offset(x, offset):
        perm = [(ring[(e + offset) % shards], ring[e]) for e in range(shards)]
        return lax.ppermute(x, "shard", perm)

    def exchange(blocks):
        got = list(blocks)
        for k in range(1, groups):
            block = after(blocks[k], got[1]) if k > 2 else blocks[k]
            got[k] = lax.ppermute(block, "group", [(z, z ^ k) for z in range(groups)])
        return got

    (units,) = call(
        unit_kernel,
        [jax.ShapeDtypeStruct((rows, width), jnp.bfloat16)],
        [pltpu.VMEM((rows, width), embeddings.dtype), pltpu.SemaphoreType.DMA((4,))],
        (embeddings,),
        4 * rows * width,
        4 * rows * width,
        [pl.BlockSpec(memory_space=pltpu.HBM)],
        53 * MIB,
    )
    *send, place = call(
        lambda *refs: sort_kernel("group", *refs),
        [jax.ShapeDtypeStruct((height, LANES), jnp.bfloat16)] * groups
        + [jax.ShapeDtypeStruct((1, rows), jnp.int32)],
        [],
        (units, *lax.optimization_barrier((row_group.reshape(1, rows), row_cluster.reshape(1, rows)))),
        2 * rows * slots * width,
        4 * rows * width,
    )

    late = [groups - 1] if groups > 1 else []
    early = list(range(groups - len(late)))
    late = [groups - 1] if groups > 1 else []
    early = list(range(groups - len(late)))
    near = [r for r in range(1, roles) if 2 * offsets[r] != shards]
    far = [r for r in range(1, roles) if r not in near]
    first = {r: from_offset(send[0], offsets[r]) for r in near}
    own = exchange(send)
    held = [[None] * groups for _ in offsets]
    held[0] = [(x, None) for x in own]
    for r in near:
        held[r][0] = (first[r], None)
    for k in range(1, groups):
        if k == 1:
            block = after(own[k], first[near[0]]) if near else own[k]
        else:
            passed = [held[r][k - 2][0] for r in near]
            block = stack([after(own[k], *passed)], WAIT)
        for r in near:
            held[r][k] = (from_offset(block, offsets[r]), 0 if k > 1 else None)
    got = {r: from_offset(stack(own, 0), offsets[r]) for r in far}
    for r in far:
        held[r] = [(got[r], k) for k in range(groups)]
    everything = [(0, 0, False)]
    everything += [(offsets.index(a), offsets.index(b), both) for a, b, both in pairs]
    steps = [[] for _ in range(4)]
    final = [0] * roles
    for left, right, both in everything:
        for left_ks in (early, late):
            for right_ks in (early, late):
                if left_ks and right_ks:
                    step = 0
                    for role, ks in ((left, left_ks), (right, right_ks)):
                        if role in near:
                            step = max(step, 1 if ks is early else 3 if role == near[0] else 2)
                    task = (left, left_ks, right, right_ks, both)
                    if both and right_ks is late and left_ks is early:
                        task = (right, right_ks, left, left_ks, both)
                    steps[step].append(task)
                    final[right] = max(final[right], step)
                    if both:
                        final[left] = max(final[left], step)
    acc, flats, partial = [], {}, [None] * roles
    for step, tasks in enumerate(steps):
        if tasks:
            done = [r for r in range(roles) if final[r] == step]
            last = not any(steps[step + 1 :])
            acc, ends = score(held, tasks, acc, flats, done, last, slots, width)
            for r, end in zip(done, ends):
                partial[r] = end
    (best,) = call(
        lambda *refs: spread_kernel(ring, offsets, groups, *refs),
        [jax.ShapeDtypeStruct((shards * groups, 1, capacity), jnp.float32)],
        [],
        partial,
        roles * slots,
        4 * roles * slots,
    )
    back = lax.all_to_all(best, ("shard", "group"), split_axis=0, concat_axis=0, tiled=True)
    (result,) = call(
        lambda *refs: place_kernel(groups, *refs),
        [jax.ShapeDtypeStruct((1, rows), jnp.float32)],
        [],
        [back, place],
        rows * slots,
        4 * slots,
    )
    return result.reshape(rows)


def solution(mesh):
    placed = (P(("shard", "group"), None), P(("shard", "group"), None), P(("shard", "group")))
    return jax.shard_map(
        per_device, mesh=mesh, in_specs=placed, out_specs=P(("shard", "group")), check_vma=False
    )
```

```python
import jax
import jax.numpy as jnp
from jax import lax
from jax.experimental import pallas as pl
from jax.experimental.pallas import tpu as pltpu
from jax.sharding import PartitionSpec as P

LANES = 128
TAIL = 16
LOW = -2.0
MIB = 1024 * 1024
WAIT = 2 * 10**10


def ring_order(size):
    if size % 2:
        return list(range(size))
    half = size // 2
    chips = [i ^ (i >> 1) for i in range(half)]
    if sorted(chips) != list(range(half)):
        chips = list(range(half))
    return [2 * chip + core for core in range(2) for chip in chips]


def offset_cover(size):
    offsets = list(dict.fromkeys([0, size // 2, 1 % size, (size - 1) % size]))

    def missing(chosen):
        have = {(a - b) % size for a in chosen for b in chosen}
        return [d for d in range(size) if d not in have]

    while missing(offsets):
        offsets.append(min(range(size), key=lambda x: len(missing(offsets + [x]))))
    pairs = []
    for diff in range(1, size // 2 + 1):
        found = [
            (a, b)
            for b in [(size - 1) % size] + offsets
            for a in offsets
            if (a - b) % size in (diff, size - diff)
        ]
        if 2 * diff == size:
            found = [(a, b) for a, b in found if b == 0] + found
        a, b = found[0]
        pairs.append((a, b, b != 0 or 2 * diff != size))
    return offsets, pairs


def column_of(row):
    size = row.shape[1]
    return jnp.transpose(jnp.broadcast_to(row, (size, size)))


def unit_kernel(far_ref, unit_ref, near_ref, sems):
    parts = sems.shape[0]
    size = far_ref.shape[0] // parts
    copies = [
        pltpu.make_async_copy(
            far_ref.at[pl.ds(i * size, size), :], near_ref.at[pl.ds(i * size, size), :], sems.at[i]
        )
        for i in range(parts)
    ]
    for copy in copies:
        copy.start()
    for i, copy in enumerate(copies):
        copy.wait()
        feats = near_ref[pl.ds(i * size, size), :].astype(jnp.float32)
        squares = jnp.sum(feats * feats, axis=1, keepdims=True) + 1e-06
        unit_ref[pl.ds(i * size, size), :] = (feats * lax.rsqrt(squares)).astype(jnp.bfloat16)


def sort_kernel(axis, unit_ref, group_ref, label_ref, *out_refs):
    *block_refs, place_ref = out_refs
    rows, width = unit_ref.shape
    groups = len(block_refs)
    capacity = (block_refs[0].shape[0] - TAIL) * LANES // width
    slots = groups * capacity
    chunks = width // LANES
    owner = group_ref[...]
    rel = owner ^ lax.axis_index(axis)
    lines = max(8, groups)
    onehot = lax.broadcasted_iota(jnp.int32, (lines, rows), 0) == rel
    before = lax.broadcasted_iota(jnp.int32, (rows, rows), 0) < lax.broadcasted_iota(
        jnp.int32, (rows, rows), 1
    )
    ranks = jnp.dot(
        jnp.where(onehot, 1.0, 0.0).astype(jnp.bfloat16),
        jnp.where(before, 1.0, 0.0).astype(jnp.bfloat16),
        preferred_element_type=jnp.float32,
    )
    rank = jnp.sum(jnp.where(onehot, ranks, 0.0), axis=0, keepdims=True).astype(jnp.int32)
    place_ref[...] = owner * capacity + rank
    move = jnp.where(
        lax.broadcasted_iota(jnp.int32, (slots, rows), 0) == rel * capacity + rank, 1.0, 0.0
    ).astype(jnp.bfloat16)
    labels = jnp.broadcast_to(label_ref[...] + 1, (TAIL, rows)).astype(jnp.bfloat16)
    sorted_labels = (
        lax.dot_general(
            labels, move, (((1,), (1,)), ((), ())), preferred_element_type=jnp.float32
        )
        - 1.0
    ).astype(jnp.bfloat16)
    for k, block_ref in enumerate(block_refs):
        part = slice(k * capacity, (k + 1) * capacity)
        block = jnp.dot(
            move[part], unit_ref[...], preferred_element_type=jnp.float32
        ).astype(jnp.bfloat16)
        for c in range(chunks):
            block_ref[pl.ds(c * capacity, capacity), :] = block[:, c * LANES : (c + 1) * LANES]
        block_ref[pl.ds(chunks * capacity, TAIL), :] = sorted_labels[:, part]


def stack_kernel(*refs):
    for k, ref in enumerate(refs[:-1]):
        refs[-1][k] = ref[...]


def score_kernel(sources, flats, layout, tasks, done, last, *refs):
    *refs, side_ref, row_ref = refs
    if last:
        *refs, best_ref, flat_ref = refs
        inputs, out_refs = refs[: -len(done)], refs[-len(done) :]
    else:
        outs = 2 + len(done)
        inputs, (best_ref, flat_ref, *out_refs) = refs[:-outs], refs[-outs:]
    capacity = LANES
    low = jnp.float32(LOW)
    arrays = 1 + max(index for index, _ in sources.values())
    best_ref[...] = inputs[arrays][...] if len(inputs) > arrays else jnp.full(best_ref.shape, low)

    def units(role, ks):
        rows = pl.ds(ks[0] * capacity, len(ks) * capacity)
        if (role, ks[0]) in flats:
            index, place = flats[role, ks[0]]
            return inputs[arrays + 1 + index][place, rows, :]
        return flat_ref[layout.index(role), rows, :]

    tops = {}
    for (role, k), (index, part) in sources.items():
        ref = inputs[index] if part is None else inputs[index].at[part]
        height = ref.shape[0] - TAIL
        rows = pl.ds(k * capacity, capacity)
        if (role, k) not in flats:
            for c in range(height // capacity):
                flat_ref[layout.index(role), rows, pl.ds(c * LANES, LANES)] = ref[
                    pl.ds(c * capacity, capacity), :
                ]
        tops[role, k] = ref[pl.ds(height, TAIL), :][0:1].astype(jnp.float32)
    for role, k in sorted({(left, k) for left, ks, _, _, _ in tasks for k in ks}):
        side_ref[role, pl.ds(k * capacity, capacity), :] = column_of(tops[role, k])
    turns = sorted({(left, k) for left, ks, _, _, both in tasks if both for k in ks})
    for role, k in turns:
        row_ref[role, pl.ds(k * capacity, capacity), :] = jnp.full((capacity, LANES), low)
    for left, left_ks, right, right_ks, both in tasks:
        start, count = left_ks[0] * capacity, len(left_ks) * capacity
        rows = pl.ds(start, count)
        for i in range(0, len(right_ks), 2):
            some = right_ks[i : i + 2]
            width = len(some) * capacity
            columns = pl.ds(some[0] * capacity, width)
            scores = lax.dot_general(
                units(left, left_ks),
                units(right, some),
                (((1,), (1,)), ((), ())),
                preferred_element_type=jnp.float32,
            )
            top = jnp.concatenate([tops[right, k] for k in some], axis=1)
            same = jnp.concatenate([side_ref[left, rows, :]] * len(some), axis=1) == top
            if left == right:
                same = same & (
                    lax.broadcasted_iota(jnp.int32, (count, width), 0) + start
                    != lax.broadcasted_iota(jnp.int32, (count, width), 1) + some[0] * capacity
                )
            scores = jnp.where(same, scores, low)
            if both:
                best = row_ref[left, rows, :]
                for c in range(len(some)):
                    best = jnp.maximum(best, scores[:, c * LANES : (c + 1) * LANES])
                row_ref[left, rows, :] = best
            best = jnp.max(scores.reshape(count // 8, 8, width), axis=0)
            best_ref[right, :, columns] = jnp.maximum(best_ref[right, :, columns], best)
    for role, k in turns:
        rows = pl.ds(k * capacity, capacity)
        turned = jnp.transpose(row_ref[role, rows, :]).reshape(capacity // 8, 8, capacity)
        best_ref[role, :, rows] = jnp.maximum(best_ref[role, :, rows], jnp.max(turned, axis=0))
    for role, out_ref in zip(done, out_refs):
        out_ref[...] = jnp.max(best_ref[role], axis=0, keepdims=True)


def spread_kernel(ring, offsets, groups, *refs):
    *partial_refs, out_ref = refs
    shards = len(ring)
    out_ref[...] = jnp.full(out_ref.shape, jnp.float32(LOW))
    shard, group = lax.axis_index("shard"), lax.axis_index("group")
    for offset, ref in zip(offsets, partial_refs):
        target = sum(
            jnp.where(shard == ring[e], ring[(e + offset) % shards], 0) for e in range(shards)
        )
        for k in range(groups):
            row = target * groups + (group ^ k)
            out_ref[pl.ds(row, 1)] = ref[:, k * LANES : (k + 1) * LANES].reshape(1, 1, LANES)


def place_kernel(groups, back_ref, place_ref, out_ref):
    place = place_ref[...]
    rows = place.shape[1]
    best = jnp.full((1, rows), jnp.float32(LOW))
    for g in range(groups):
        row = jnp.full((1, LANES), jnp.float32(-1.0))
        for s in range(back_ref.shape[0] // groups):
            row = jnp.maximum(row, back_ref[s * groups + g])
        values = jnp.concatenate([column_of(row)] * (rows // LANES), axis=1)
        here = lax.broadcasted_iota(jnp.int32, (LANES, rows), 0) + g * LANES == place
        best = jnp.maximum(
            best, jnp.max(jnp.where(here, values, jnp.float32(LOW)), axis=0, keepdims=True)
        )
    out_ref[...] = best


def in_vmem(count):
    return [pl.BlockSpec(memory_space=pltpu.VMEM)] * count


def call(
    kernel, out_shape, scratch, args, flops, bytes_accessed, in_specs=None, limit=24 * MIB
):
    return pl.pallas_call(
        kernel,
        out_shape=out_shape,
        in_specs=in_specs or in_vmem(len(args)),
        out_specs=in_vmem(len(out_shape)),
        scratch_shapes=scratch,
        compiler_params=pltpu.CompilerParams(vmem_limit_bytes=limit),
        cost_estimate=pl.CostEstimate(
            flops=flops, bytes_accessed=bytes_accessed, transcendentals=0
        ),
    )(*args)


def after(x, *earlier):
    return lax.optimization_barrier((x, *earlier))[0]


def stack(parts, wait):
    return call(
        stack_kernel,
        [jax.ShapeDtypeStruct((len(parts), *parts[0].shape), parts[0].dtype)],
        [],
        parts,
        wait,
        4 * len(parts) * parts[0].size,
    )[0]


def score(held, tasks, acc, flats, done, last, slots, width):
    roles = len(held)
    used = sorted(
        {(left, k) for left, ks, _, _, _ in tasks for k in ks}
        | {(right, k) for _, _, right, ks, _ in tasks for k in ks},
        key=lambda x: (x[0], -x[1]),
    )
    arrays, sources = [], {}
    for role, k in used:
        array, part = held[role][k]
        index = next((i for i, x in enumerate(arrays) if x is array), len(arrays))
        if index == len(arrays):
            arrays.append(array)
        sources[role, k] = (index, part)
    layout = sorted({role for role, k in used if (role, k) not in flats})
    tiles = sum(len(task[1]) * len(task[3]) for task in tasks)
    kept = [
        jax.ShapeDtypeStruct((roles, 8, slots), jnp.float32),
        jax.ShapeDtypeStruct((len(layout), slots, width), jnp.bfloat16),
    ]
    scratch = [pltpu.VMEM((roles, slots, LANES), jnp.float32)] * 2
    if last:
        scratch = [pltpu.VMEM(x.shape, x.dtype) for x in kept] + scratch
        kept = []
    known = dict(flats)
    got = call(
        lambda *refs: score_kernel(sources, known, layout, tasks, done, last, *refs),
        kept + [jax.ShapeDtypeStruct((1, slots), jnp.float32)] * len(done),
        scratch,
        arrays + list(acc),
        2 * tiles * LANES * LANES * width,
        2 * len(used) * LANES * width,
    )
    if last:
        return acc, got
    for role, k in used:
        if (role, k) not in flats:
            flats[role, k] = (max(len(acc) - 1, 0), layout.index(role))
    return [got[0], *acc[1:], got[1]], got[2:]


def per_device(embeddings, row_group, row_cluster):
    rows, width = embeddings.shape
    groups = lax.axis_size("group")
    shards = lax.axis_size("shard")
    capacity = rows // 4
    slots = groups * capacity
    ring = ring_order(shards)
    offsets, pairs = offset_cover(shards)
    roles = len(offsets)
    height = width * capacity // LANES + TAIL

    def from_offset(x, offset):
        perm = [(ring[(e + offset) % shards], ring[e]) for e in range(shards)]
        return lax.ppermute(x, "shard", perm)

    def exchange(blocks):
        got = list(blocks)
        for k in range(1, groups):
            got[k] = lax.ppermute(blocks[k], "group", [(z, z ^ k) for z in range(groups)])
        return got

    (units,) = call(
        unit_kernel,
        [jax.ShapeDtypeStruct((rows, width), jnp.bfloat16)],
        [pltpu.VMEM((rows, width), embeddings.dtype), pltpu.SemaphoreType.DMA((8,))],
        (embeddings,),
        4 * rows * width,
        4 * rows * width,
        [pl.BlockSpec(memory_space=pltpu.HBM)],
        53 * MIB,
    )
    *send, place = call(
        lambda *refs: sort_kernel("group", *refs),
        [jax.ShapeDtypeStruct((height, LANES), jnp.bfloat16)] * groups
        + [jax.ShapeDtypeStruct((1, rows), jnp.int32)],
        [],
        (units, *lax.optimization_barrier((row_group.reshape(1, rows), row_cluster.reshape(1, rows)))),
        2 * rows * slots * width,
        4 * rows * width,
    )

    late = [groups - 1] if groups > 1 else []
    early = list(range(groups - len(late)))
    late = [groups - 1] if groups > 1 else []
    early = list(range(groups - len(late)))
    near = [r for r in range(1, roles) if 2 * offsets[r] != shards]
    far = [r for r in range(1, roles) if r not in near]
    first = {r: from_offset(send[0], offsets[r]) for r in near}
    own = exchange(send)
    held = [[None] * groups for _ in offsets]
    held[0] = [(x, None) for x in own]
    for r in near:
        held[r][0] = (first[r], None)
    for k in range(1, groups):
        if k == 1:
            block = after(own[k], first[near[0]]) if near else own[k]
        else:
            passed = [held[r][k - 2][0] for r in near]
            block = stack([after(own[k], *passed)], WAIT)
        for r in near:
            held[r][k] = (from_offset(block, offsets[r]), 0 if k > 1 else None)
    got = {r: from_offset(stack(own, 0), offsets[r]) for r in far}
    for r in far:
        held[r] = [(got[r], k) for k in range(groups)]
    everything = [(0, 0, False)]
    everything += [(offsets.index(a), offsets.index(b), both) for a, b, both in pairs]
    steps = [[] for _ in range(4)]
    final = [0] * roles
    for left, right, both in everything:
        for left_ks in (early, late):
            for right_ks in (early, late):
                if left_ks and right_ks:
                    step = 0
                    for role, ks in ((left, left_ks), (right, right_ks)):
                        if role in near:
                            step = max(step, 1 if ks is early else 3 if role == near[0] else 2)
                    task = (left, left_ks, right, right_ks, both)
                    if both and right_ks is late and left_ks is early:
                        task = (right, right_ks, left, left_ks, both)
                    steps[step].append(task)
                    final[right] = max(final[right], step)
                    if both:
                        final[left] = max(final[left], step)
    acc, flats, partial = [], {}, [None] * roles
    for step, tasks in enumerate(steps):
        if tasks:
            done = [r for r in range(roles) if final[r] == step]
            last = not any(steps[step + 1 :])
            acc, ends = score(held, tasks, acc, flats, done, last, slots, width)
            for r, end in zip(done, ends):
                partial[r] = end
    (best,) = call(
        lambda *refs: spread_kernel(ring, offsets, groups, *refs),
        [jax.ShapeDtypeStruct((shards * groups, 1, capacity), jnp.float32)],
        [],
        partial,
        roles * slots,
        4 * roles * slots,
    )
    back = lax.all_to_all(best, ("shard", "group"), split_axis=0, concat_axis=0, tiled=True)
    (result,) = call(
        lambda *refs: place_kernel(groups, *refs),
        [jax.ShapeDtypeStruct((1, rows), jnp.float32)],
        [],
        [back, place],
        rows * slots,
        4 * slots,
    )
    return result.reshape(rows)


def solution(mesh):
    placed = (P(("shard", "group"), None), P(("shard", "group"), None), P(("shard", "group")))
    return jax.shard_map(
        per_device, mesh=mesh, in_specs=placed, out_specs=P(("shard", "group")), check_vma=False
    )
```

```python
import jax
import jax.numpy as jnp
from jax import lax
from jax.experimental import pallas as pl
from jax.experimental.pallas import tpu as pltpu
from jax.sharding import PartitionSpec as P

LANES = 128
TAIL = 16
LOW = -2.0
MIB = 1024 * 1024
WAIT = 2 * 10**10


def ring_order(size):
    if size % 2:
        return list(range(size))
    half = size // 2
    chips = [i ^ (i >> 1) for i in range(half)]
    if sorted(chips) != list(range(half)):
        chips = list(range(half))
    return [2 * chip + core for core in range(2) for chip in chips]


def offset_cover(size):
    offsets = list(dict.fromkeys([0, size // 2, 1 % size, (size - 1) % size]))

    def missing(chosen):
        have = {(a - b) % size for a in chosen for b in chosen}
        return [d for d in range(size) if d not in have]

    while missing(offsets):
        offsets.append(min(range(size), key=lambda x: len(missing(offsets + [x]))))
    pairs = []
    for diff in range(1, size // 2 + 1):
        found = [
            (a, b)
            for b in [(size - 1) % size] + offsets
            for a in offsets
            if (a - b) % size in (diff, size - diff)
        ]
        if 2 * diff == size:
            found = [(a, b) for a, b in found if b == 0] + found
        a, b = found[0]
        pairs.append((a, b, b != 0 or 2 * diff != size))
    return offsets, pairs


def column_of(row):
    size = row.shape[1]
    return jnp.transpose(jnp.broadcast_to(row, (size, size)))


def unit_kernel(far_ref, unit_ref, near_ref, sems):
    parts = sems.shape[0]
    size = far_ref.shape[0] // parts
    copies = [
        pltpu.make_async_copy(
            far_ref.at[pl.ds(i * size, size), :], near_ref.at[pl.ds(i * size, size), :], sems.at[i]
        )
        for i in range(parts)
    ]
    for copy in copies:
        copy.start()
    for i, copy in enumerate(copies):
        copy.wait()
        feats = near_ref[pl.ds(i * size, size), :].astype(jnp.float32)
        squares = jnp.sum(feats * feats, axis=1, keepdims=True) + 1e-06
        unit_ref[pl.ds(i * size, size), :] = (feats * lax.rsqrt(squares)).astype(jnp.bfloat16)


def sort_kernel(axis, unit_ref, group_ref, label_ref, *out_refs):
    *block_refs, place_ref = out_refs
    rows, width = unit_ref.shape
    groups = len(block_refs)
    capacity = (block_refs[0].shape[0] - TAIL) * LANES // width
    slots = groups * capacity
    chunks = width // LANES
    owner = group_ref[...]
    rel = owner ^ lax.axis_index(axis)
    lines = max(8, groups)
    onehot = lax.broadcasted_iota(jnp.int32, (lines, rows), 0) == rel
    before = lax.broadcasted_iota(jnp.int32, (rows, rows), 0) < lax.broadcasted_iota(
        jnp.int32, (rows, rows), 1
    )
    ranks = jnp.dot(
        jnp.where(onehot, 1.0, 0.0).astype(jnp.bfloat16),
        jnp.where(before, 1.0, 0.0).astype(jnp.bfloat16),
        preferred_element_type=jnp.float32,
    )
    rank = jnp.sum(jnp.where(onehot, ranks, 0.0), axis=0, keepdims=True).astype(jnp.int32)
    place_ref[...] = owner * capacity + rank
    move = jnp.where(
        lax.broadcasted_iota(jnp.int32, (slots, rows), 0) == rel * capacity + rank, 1.0, 0.0
    ).astype(jnp.bfloat16)
    labels = jnp.broadcast_to(label_ref[...] + 1, (TAIL, rows)).astype(jnp.bfloat16)
    sorted_labels = (
        lax.dot_general(
            labels, move, (((1,), (1,)), ((), ())), preferred_element_type=jnp.float32
        )
        - 1.0
    ).astype(jnp.bfloat16)
    for k, block_ref in enumerate(block_refs):
        part = slice(k * capacity, (k + 1) * capacity)
        block = jnp.dot(
            move[part], unit_ref[...], preferred_element_type=jnp.float32
        ).astype(jnp.bfloat16)
        for c in range(chunks):
            block_ref[pl.ds(c * capacity, capacity), :] = block[:, c * LANES : (c + 1) * LANES]
        block_ref[pl.ds(chunks * capacity, TAIL), :] = sorted_labels[:, part]


def stack_kernel(*refs):
    for k, ref in enumerate(refs[:-1]):
        refs[-1][k] = ref[...]


def score_kernel(sources, flats, layout, tasks, done, last, *refs):
    *refs, side_ref, row_ref = refs
    if last:
        *refs, best_ref, flat_ref = refs
        inputs, out_refs = refs[: -len(done)], refs[-len(done) :]
    else:
        outs = 2 + len(done)
        inputs, (best_ref, flat_ref, *out_refs) = refs[:-outs], refs[-outs:]
    capacity = LANES
    low = jnp.float32(LOW)
    arrays = 1 + max(index for index, _ in sources.values())
    best_ref[...] = inputs[arrays][...] if len(inputs) > arrays else jnp.full(best_ref.shape, low)

    def units(role, ks):
        rows = pl.ds(ks[0] * capacity, len(ks) * capacity)
        if (role, ks[0]) in flats:
            index, place = flats[role, ks[0]]
            return inputs[arrays + 1 + index][place, rows, :]
        return flat_ref[layout.index(role), rows, :]

    tops = {}
    for (role, k), (index, part) in sources.items():
        ref = inputs[index] if part is None else inputs[index].at[part]
        height = ref.shape[0] - TAIL
        rows = pl.ds(k * capacity, capacity)
        if (role, k) not in flats:
            for c in range(height // capacity):
                flat_ref[layout.index(role), rows, pl.ds(c * LANES, LANES)] = ref[
                    pl.ds(c * capacity, capacity), :
                ]
        tops[role, k] = ref[pl.ds(height, TAIL), :][0:1].astype(jnp.float32)
    for role, k in sorted({(left, k) for left, ks, _, _, _ in tasks for k in ks}):
        side_ref[role, pl.ds(k * capacity, capacity), :] = column_of(tops[role, k])
    turns = sorted({(left, k) for left, ks, _, _, both in tasks if both for k in ks})
    for role, k in turns:
        row_ref[role, pl.ds(k * capacity, capacity), :] = jnp.full((capacity, LANES), low)
    for left, left_ks, right, right_ks, both in tasks:
        start, count = left_ks[0] * capacity, len(left_ks) * capacity
        rows = pl.ds(start, count)
        for i in range(0, len(right_ks), 2):
            some = right_ks[i : i + 2]
            width = len(some) * capacity
            columns = pl.ds(some[0] * capacity, width)
            scores = lax.dot_general(
                units(left, left_ks),
                units(right, some),
                (((1,), (1,)), ((), ())),
                preferred_element_type=jnp.float32,
            )
            top = jnp.concatenate([tops[right, k] for k in some], axis=1)
            same = jnp.concatenate([side_ref[left, rows, :]] * len(some), axis=1) == top
            if left == right:
                same = same & (
                    lax.broadcasted_iota(jnp.int32, (count, width), 0) + start
                    != lax.broadcasted_iota(jnp.int32, (count, width), 1) + some[0] * capacity
                )
            scores = jnp.where(same, scores, low)
            if both:
                best = row_ref[left, rows, :]
                for c in range(len(some)):
                    best = jnp.maximum(best, scores[:, c * LANES : (c + 1) * LANES])
                row_ref[left, rows, :] = best
            best = jnp.max(scores.reshape(count // 8, 8, width), axis=0)
            best_ref[right, :, columns] = jnp.maximum(best_ref[right, :, columns], best)
    for role, k in turns:
        rows = pl.ds(k * capacity, capacity)
        turned = jnp.transpose(row_ref[role, rows, :]).reshape(capacity // 8, 8, capacity)
        best_ref[role, :, rows] = jnp.maximum(best_ref[role, :, rows], jnp.max(turned, axis=0))
    for role, out_ref in zip(done, out_refs):
        out_ref[...] = jnp.max(best_ref[role], axis=0, keepdims=True)


def spread_kernel(ring, offsets, groups, *refs):
    *partial_refs, out_ref = refs
    shards = len(ring)
    out_ref[...] = jnp.full(out_ref.shape, jnp.float32(LOW))
    shard, group = lax.axis_index("shard"), lax.axis_index("group")
    for offset, ref in zip(offsets, partial_refs):
        target = sum(
            jnp.where(shard == ring[e], ring[(e + offset) % shards], 0) for e in range(shards)
        )
        for k in range(groups):
            row = target * groups + (group ^ k)
            out_ref[pl.ds(row, 1)] = ref[:, k * LANES : (k + 1) * LANES].reshape(1, 1, LANES)


def place_kernel(groups, back_ref, place_ref, out_ref):
    place = place_ref[...]
    rows = place.shape[1]
    best = jnp.full((1, rows), jnp.float32(LOW))
    for g in range(groups):
        row = jnp.full((1, LANES), jnp.float32(-1.0))
        for s in range(back_ref.shape[0] // groups):
            row = jnp.maximum(row, back_ref[s * groups + g])
        values = jnp.concatenate([column_of(row)] * (rows // LANES), axis=1)
        here = lax.broadcasted_iota(jnp.int32, (LANES, rows), 0) + g * LANES == place
        best = jnp.maximum(
            best, jnp.max(jnp.where(here, values, jnp.float32(LOW)), axis=0, keepdims=True)
        )
    out_ref[...] = best


def in_vmem(count):
    return [pl.BlockSpec(memory_space=pltpu.VMEM)] * count


def call(
    kernel, out_shape, scratch, args, flops, bytes_accessed, in_specs=None, limit=24 * MIB
):
    return pl.pallas_call(
        kernel,
        out_shape=out_shape,
        in_specs=in_specs or in_vmem(len(args)),
        out_specs=in_vmem(len(out_shape)),
        scratch_shapes=scratch,
        compiler_params=pltpu.CompilerParams(vmem_limit_bytes=limit),
        cost_estimate=pl.CostEstimate(
            flops=flops, bytes_accessed=bytes_accessed, transcendentals=0
        ),
    )(*args)


def after(x, *earlier):
    return lax.optimization_barrier((x, *earlier))[0]


def stack(parts, wait):
    return call(
        stack_kernel,
        [jax.ShapeDtypeStruct((len(parts), *parts[0].shape), parts[0].dtype)],
        [],
        parts,
        wait,
        4 * len(parts) * parts[0].size,
    )[0]


def score(held, tasks, acc, flats, done, last, slots, width):
    roles = len(held)
    used = sorted(
        {(left, k) for left, ks, _, _, _ in tasks for k in ks}
        | {(right, k) for _, _, right, ks, _ in tasks for k in ks},
        key=lambda x: (x[0], -x[1]),
    )
    arrays, sources = [], {}
    for role, k in used:
        array, part = held[role][k]
        index = next((i for i, x in enumerate(arrays) if x is array), len(arrays))
        if index == len(arrays):
            arrays.append(array)
        sources[role, k] = (index, part)
    layout = sorted({role for role, k in used if (role, k) not in flats})
    tiles = sum(len(task[1]) * len(task[3]) for task in tasks)
    kept = [
        jax.ShapeDtypeStruct((roles, 8, slots), jnp.float32),
        jax.ShapeDtypeStruct((len(layout), slots, width), jnp.bfloat16),
    ]
    scratch = [pltpu.VMEM((roles, slots, LANES), jnp.float32)] * 2
    if last:
        scratch = [pltpu.VMEM(x.shape, x.dtype) for x in kept] + scratch
        kept = []
    known = dict(flats)
    got = call(
        lambda *refs: score_kernel(sources, known, layout, tasks, done, last, *refs),
        kept + [jax.ShapeDtypeStruct((1, slots), jnp.float32)] * len(done),
        scratch,
        arrays + list(acc),
        2 * tiles * LANES * LANES * width,
        2 * len(used) * LANES * width,
    )
    if last:
        return acc, got
    for role, k in used:
        if (role, k) not in flats:
            flats[role, k] = (max(len(acc) - 1, 0), layout.index(role))
    return [got[0], *acc[1:], got[1]], got[2:]


def per_device(embeddings, row_group, row_cluster):
    rows, width = embeddings.shape
    groups = lax.axis_size("group")
    shards = lax.axis_size("shard")
    capacity = rows // 4
    slots = groups * capacity
    ring = ring_order(shards)
    offsets, pairs = offset_cover(shards)
    roles = len(offsets)
    height = width * capacity // LANES + TAIL

    def from_offset(x, offset):
        perm = [(ring[(e + offset) % shards], ring[e]) for e in range(shards)]
        return lax.ppermute(x, "shard", perm)

    def exchange(blocks):
        got = list(blocks)
        for k in range(1, groups):
            block = after(blocks[k], got[1]) if k > 2 else blocks[k]
            got[k] = lax.ppermute(block, "group", [(z, z ^ k) for z in range(groups)])
        return got

    (units,) = call(
        unit_kernel,
        [jax.ShapeDtypeStruct((rows, width), jnp.bfloat16)],
        [pltpu.VMEM((rows, width), embeddings.dtype), pltpu.SemaphoreType.DMA((2,))],
        (embeddings,),
        4 * rows * width,
        4 * rows * width,
        [pl.BlockSpec(memory_space=pltpu.HBM)],
        53 * MIB,
    )
    *send, place = call(
        lambda *refs: sort_kernel("group", *refs),
        [jax.ShapeDtypeStruct((height, LANES), jnp.bfloat16)] * groups
        + [jax.ShapeDtypeStruct((1, rows), jnp.int32)],
        [],
        (units, *lax.optimization_barrier((row_group.reshape(1, rows), row_cluster.reshape(1, rows)))),
        2 * rows * slots * width,
        4 * rows * width,
    )

    late = [groups - 1] if groups > 1 else []
    early = list(range(groups - len(late)))
    late = [groups - 1] if groups > 1 else []
    early = list(range(groups - len(late)))
    near = [r for r in range(1, roles) if 2 * offsets[r] != shards]
    far = [r for r in range(1, roles) if r not in near]
    first = {r: from_offset(send[0], offsets[r]) for r in near}
    own = exchange(send)
    held = [[None] * groups for _ in offsets]
    held[0] = [(x, None) for x in own]
    for r in near:
        held[r][0] = (first[r], None)
    for k in range(1, groups):
        if k == 1:
            block = after(own[k], first[near[-1]]) if near else own[k]
        else:
            passed = [held[r][k - 2][0] for r in near]
            block = stack([after(own[k], *passed)], WAIT)
        for r in near:
            held[r][k] = (from_offset(block, offsets[r]), 0 if k > 1 else None)
    got = {r: from_offset(stack(own, 0), offsets[r]) for r in far}
    for r in far:
        held[r] = [(got[r], k) for k in range(groups)]
    everything = [(0, 0, False)]
    everything += [(offsets.index(a), offsets.index(b), both) for a, b, both in pairs]
    steps = [[] for _ in range(4)]
    final = [0] * roles
    for left, right, both in everything:
        for left_ks in (early, late):
            for right_ks in (early, late):
                if left_ks and right_ks:
                    step = 0
                    for role, ks in ((left, left_ks), (right, right_ks)):
                        if role in near:
                            step = max(step, 1 if ks is early else 3 if role == near[0] else 2)
                    task = (left, left_ks, right, right_ks, both)
                    if both and right_ks is late and left_ks is early:
                        task = (right, right_ks, left, left_ks, both)
                    steps[step].append(task)
                    final[right] = max(final[right], step)
                    if both:
                        final[left] = max(final[left], step)
    acc, flats, partial = [], {}, [None] * roles
    for step, tasks in enumerate(steps):
        if tasks:
            done = [r for r in range(roles) if final[r] == step]
            last = not any(steps[step + 1 :])
            acc, ends = score(held, tasks, acc, flats, done, last, slots, width)
            for r, end in zip(done, ends):
                partial[r] = end
    (best,) = call(
        lambda *refs: spread_kernel(ring, offsets, groups, *refs),
        [jax.ShapeDtypeStruct((shards * groups, 1, capacity), jnp.float32)],
        [],
        partial,
        roles * slots,
        4 * roles * slots,
    )
    back = lax.all_to_all(best, ("shard", "group"), split_axis=0, concat_axis=0, tiled=True)
    (result,) = call(
        lambda *refs: place_kernel(groups, *refs),
        [jax.ShapeDtypeStruct((1, rows), jnp.float32)],
        [],
        [back, place],
        rows * slots,
        4 * slots,
    )
    return result.reshape(rows)


def solution(mesh):
    placed = (P(("shard", "group"), None), P(("shard", "group"), None), P(("shard", "group")))
    return jax.shard_map(
        per_device, mesh=mesh, in_specs=placed, out_specs=P(("shard", "group")), check_vma=False
    )
```

```python
import jax
import jax.numpy as jnp
from jax import lax
from jax.experimental import pallas as pl
from jax.experimental.pallas import tpu as pltpu
from jax.sharding import PartitionSpec as P

LANES = 128
TAIL = 16
LOW = -2.0
MIB = 1024 * 1024
WAIT = 2 * 10**10


def ring_order(size):
    if size % 2:
        return list(range(size))
    half = size // 2
    chips = [i ^ (i >> 1) for i in range(half)]
    if sorted(chips) != list(range(half)):
        chips = list(range(half))
    return [2 * chip + core for core in range(2) for chip in chips]


def offset_cover(size):
    offsets = list(dict.fromkeys([0, size // 2, 1 % size, (size - 1) % size]))

    def missing(chosen):
        have = {(a - b) % size for a in chosen for b in chosen}
        return [d for d in range(size) if d not in have]

    while missing(offsets):
        offsets.append(min(range(size), key=lambda x: len(missing(offsets + [x]))))
    pairs = []
    for diff in range(1, size // 2 + 1):
        found = [
            (a, b)
            for b in [(size - 1) % size] + offsets
            for a in offsets
            if (a - b) % size in (diff, size - diff)
        ]
        if 2 * diff == size:
            found = [(a, b) for a, b in found if b == 0] + found
        a, b = found[0]
        pairs.append((a, b, b != 0 or 2 * diff != size))
    return offsets, pairs


def column_of(row):
    size = row.shape[1]
    return jnp.transpose(jnp.broadcast_to(row, (size, size)))


def unit_kernel(far_ref, unit_ref, near_ref, sems):
    parts = sems.shape[0]
    size = far_ref.shape[0] // parts
    copies = [
        pltpu.make_async_copy(
            far_ref.at[pl.ds(i * size, size), :], near_ref.at[pl.ds(i * size, size), :], sems.at[i]
        )
        for i in range(parts)
    ]
    for copy in copies:
        copy.start()
    for i, copy in enumerate(copies):
        copy.wait()
        feats = near_ref[pl.ds(i * size, size), :].astype(jnp.float32)
        squares = jnp.sum(feats * feats, axis=1, keepdims=True) + 1e-06
        unit_ref[pl.ds(i * size, size), :] = (feats * lax.rsqrt(squares)).astype(jnp.bfloat16)


def sort_kernel(axis, pieces, capacity, unit_ref, group_ref, label_ref, *out_refs):
    *block_refs, place_ref = out_refs
    rows, width = unit_ref.shape
    groups = len(pieces)
    slots = groups * capacity
    chunks = width // LANES
    owner = group_ref[...]
    rel = owner ^ lax.axis_index(axis)
    lines = max(8, groups)
    onehot = lax.broadcasted_iota(jnp.int32, (lines, rows), 0) == rel
    before = lax.broadcasted_iota(jnp.int32, (rows, rows), 0) < lax.broadcasted_iota(
        jnp.int32, (rows, rows), 1
    )
    ranks = jnp.dot(
        jnp.where(onehot, 1.0, 0.0).astype(jnp.bfloat16),
        jnp.where(before, 1.0, 0.0).astype(jnp.bfloat16),
        preferred_element_type=jnp.float32,
    )
    rank = jnp.sum(jnp.where(onehot, ranks, 0.0), axis=0, keepdims=True).astype(jnp.int32)
    place_ref[...] = owner * capacity + rank
    move = jnp.where(
        lax.broadcasted_iota(jnp.int32, (slots, rows), 0) == rel * capacity + rank, 1.0, 0.0
    ).astype(jnp.bfloat16)
    labels = jnp.broadcast_to(label_ref[...] + 1, (TAIL, rows)).astype(jnp.bfloat16)
    sorted_labels = (
        lax.dot_general(
            labels, move, (((1,), (1,)), ((), ())), preferred_element_type=jnp.float32
        )
        - 1.0
    ).astype(jnp.bfloat16)
    for k in range(groups):
        part = slice(k * capacity, (k + 1) * capacity)
        block = jnp.dot(
            move[part], unit_ref[...], preferred_element_type=jnp.float32
        ).astype(jnp.bfloat16)
        size = capacity // pieces[k]
        for i in range(pieces[k]):
            block_ref = block_refs[sum(pieces[:k]) + i]
            for c in range(chunks):
                block_ref[pl.ds(c * size, size), :] = block[
                    i * size : (i + 1) * size, c * LANES : (c + 1) * LANES
                ]
            block_ref[pl.ds(chunks * size, TAIL), :] = sorted_labels[:, part]


def stack_kernel(*refs):
    start = 0
    for ref in refs[:-1]:
        refs[-1][pl.ds(start, ref.shape[0]), :] = ref[...]
        start += ref.shape[0]


def score_kernel(sources, flats, layout, tasks, done, last, *refs):
    *refs, side_ref, row_ref = refs
    if last:
        *refs, best_ref, flat_ref = refs
        inputs, out_refs = refs[: -len(done)], refs[-len(done) :]
    else:
        outs = 2 + len(done)
        inputs, (best_ref, flat_ref, *out_refs) = refs[:-outs], refs[-outs:]
    capacity = LANES
    low = jnp.float32(LOW)
    arrays = 1 + max(index for found in sources.values() for index, _, _ in found)
    chunks = flat_ref.shape[-1] // LANES
    best_ref[...] = inputs[arrays][...] if len(inputs) > arrays else jnp.full(best_ref.shape, low)

    def units(role, ks):
        rows = pl.ds(ks[0] * capacity, len(ks) * capacity)
        if (role, ks[0]) in flats:
            index, place = flats[role, ks[0]]
            return inputs[arrays + 1 + index][place, rows, :]
        return flat_ref[layout.index(role), rows, :]

    tops = {}
    for (role, k), found in sources.items():
        at = k * capacity
        for index, start, size in found:
            if (role, k) not in flats:
                for c in range(chunks):
                    flat_ref[
                        layout.index(role), pl.ds(at, size), pl.ds(c * LANES, LANES)
                    ] = inputs[index][pl.ds(start + c * size, size), :]
            at += size
        tops[role, k] = inputs[index][pl.ds(start + chunks * size, TAIL), :][0:1].astype(
            jnp.float32
        )
    for role, k in sorted({(left, k) for left, ks, _, _, _ in tasks for k in ks}):
        side_ref[role, pl.ds(k * capacity, capacity), :] = column_of(tops[role, k])
    turns = sorted({(left, k) for left, ks, _, _, both in tasks if both for k in ks})
    for role, k in turns:
        row_ref[role, pl.ds(k * capacity, capacity), :] = jnp.full((capacity, LANES), low)
    for left, left_ks, right, right_ks, both in tasks:
        start, count = left_ks[0] * capacity, len(left_ks) * capacity
        rows = pl.ds(start, count)
        for i in range(0, len(right_ks), 2):
            some = right_ks[i : i + 2]
            width = len(some) * capacity
            columns = pl.ds(some[0] * capacity, width)
            scores = lax.dot_general(
                units(left, left_ks),
                units(right, some),
                (((1,), (1,)), ((), ())),
                preferred_element_type=jnp.float32,
            )
            top = jnp.concatenate([tops[right, k] for k in some], axis=1)
            same = jnp.concatenate([side_ref[left, rows, :]] * len(some), axis=1) == top
            if left == right:
                same = same & (
                    lax.broadcasted_iota(jnp.int32, (count, width), 0) + start
                    != lax.broadcasted_iota(jnp.int32, (count, width), 1) + some[0] * capacity
                )
            scores = jnp.where(same, scores, low)
            if both:
                best = row_ref[left, rows, :]
                for c in range(len(some)):
                    best = jnp.maximum(best, scores[:, c * LANES : (c + 1) * LANES])
                row_ref[left, rows, :] = best
            best = jnp.max(scores.reshape(count // 8, 8, width), axis=0)
            best_ref[right, :, columns] = jnp.maximum(best_ref[right, :, columns], best)
    for role, k in turns:
        rows = pl.ds(k * capacity, capacity)
        turned = jnp.transpose(row_ref[role, rows, :]).reshape(capacity // 8, 8, capacity)
        best_ref[role, :, rows] = jnp.maximum(best_ref[role, :, rows], jnp.max(turned, axis=0))
    for role, out_ref in zip(done, out_refs):
        out_ref[...] = jnp.max(best_ref[role], axis=0, keepdims=True)


def spread_kernel(ring, offsets, groups, *refs):
    *partial_refs, out_ref = refs
    shards = len(ring)
    out_ref[...] = jnp.full(out_ref.shape, jnp.float32(LOW))
    shard, group = lax.axis_index("shard"), lax.axis_index("group")
    for offset, ref in zip(offsets, partial_refs):
        target = sum(
            jnp.where(shard == ring[e], ring[(e + offset) % shards], 0) for e in range(shards)
        )
        for k in range(groups):
            row = target * groups + (group ^ k)
            out_ref[pl.ds(row, 1)] = ref[:, k * LANES : (k + 1) * LANES].reshape(1, 1, LANES)


def place_kernel(groups, back_ref, place_ref, out_ref):
    place = place_ref[...]
    rows = place.shape[1]
    best = jnp.full((1, rows), jnp.float32(LOW))
    for g in range(groups):
        row = jnp.full((1, LANES), jnp.float32(-1.0))
        for s in range(back_ref.shape[0] // groups):
            row = jnp.maximum(row, back_ref[s * groups + g])
        values = jnp.concatenate([column_of(row)] * (rows // LANES), axis=1)
        here = lax.broadcasted_iota(jnp.int32, (LANES, rows), 0) + g * LANES == place
        best = jnp.maximum(
            best, jnp.max(jnp.where(here, values, jnp.float32(LOW)), axis=0, keepdims=True)
        )
    out_ref[...] = best


def in_vmem(count):
    return [pl.BlockSpec(memory_space=pltpu.VMEM)] * count


def call(
    kernel, out_shape, scratch, args, flops, bytes_accessed, in_specs=None, limit=24 * MIB
):
    return pl.pallas_call(
        kernel,
        out_shape=out_shape,
        in_specs=in_specs or in_vmem(len(args)),
        out_specs=in_vmem(len(out_shape)),
        scratch_shapes=scratch,
        compiler_params=pltpu.CompilerParams(vmem_limit_bytes=limit),
        cost_estimate=pl.CostEstimate(
            flops=flops, bytes_accessed=bytes_accessed, transcendentals=0
        ),
    )(*args)


def after(x, *earlier):
    return lax.optimization_barrier((x, *earlier))[0]


def stack(parts, wait):
    starts = [sum(x.shape[0] for x in parts[:i]) for i in range(len(parts) + 1)]
    (pack,) = call(
        stack_kernel,
        [jax.ShapeDtypeStruct((starts[-1], LANES), parts[0].dtype)],
        [],
        parts,
        wait,
        4 * starts[-1] * LANES,
    )
    return pack, starts[:-1]


def score(held, tasks, acc, flats, done, last, slots, width):
    roles = len(held)
    used = sorted(
        {(left, k) for left, ks, _, _, _ in tasks for k in ks}
        | {(right, k) for _, _, right, ks, _ in tasks for k in ks},
        key=lambda x: (x[0], -x[1]),
    )
    arrays, sources = [], {}
    for role, k in used:
        sources[role, k] = []
        for array, start, size in held[role][k]:
            index = next((i for i, x in enumerate(arrays) if x is array), len(arrays))
            if index == len(arrays):
                arrays.append(array)
            sources[role, k].append((index, start, size))
    layout = sorted({role for role, k in used if (role, k) not in flats})
    tiles = sum(len(task[1]) * len(task[3]) for task in tasks)
    kept = [
        jax.ShapeDtypeStruct((roles, 8, slots), jnp.float32),
        jax.ShapeDtypeStruct((len(layout), slots, width), jnp.bfloat16),
    ]
    scratch = [pltpu.VMEM((roles, slots, LANES), jnp.float32)] * 2
    if last:
        scratch = [pltpu.VMEM(x.shape, x.dtype) for x in kept] + scratch
        kept = []
    known = dict(flats)
    got = call(
        lambda *refs: score_kernel(sources, known, layout, tasks, done, last, *refs),
        kept + [jax.ShapeDtypeStruct((1, slots), jnp.float32)] * len(done),
        scratch,
        arrays + list(acc),
        2 * tiles * LANES * LANES * width,
        2 * len(used) * LANES * width,
    )
    if last:
        return acc, got
    for role, k in used:
        if (role, k) not in flats:
            flats[role, k] = (max(len(acc) - 1, 0), layout.index(role))
    return [got[0], *acc[1:], got[1]], got[2:]


def per_device(embeddings, row_group, row_cluster):
    rows, width = embeddings.shape
    groups = lax.axis_size("group")
    shards = lax.axis_size("shard")
    capacity = rows // 4
    slots = groups * capacity
    ring = ring_order(shards)
    offsets, pairs = offset_cover(shards)
    roles = len(offsets)
    pieces = [1] * (groups - 1) + [2 if groups > 2 else 1]
    sizes = [capacity // n for n in pieces for _ in range(n)]

    def from_offset(x, offset):
        perm = [(ring[(e + offset) % shards], ring[e]) for e in range(shards)]
        return lax.ppermute(x, "shard", perm)

    def across(x, k):
        return lax.ppermute(x, "group", [(z, z ^ k) for z in range(groups)])

    (units,) = call(
        unit_kernel,
        [jax.ShapeDtypeStruct((rows, width), jnp.bfloat16)],
        [pltpu.VMEM((rows, width), embeddings.dtype), pltpu.SemaphoreType.DMA((2,))],
        (embeddings,),
        4 * rows * width,
        4 * rows * width,
        [pl.BlockSpec(memory_space=pltpu.HBM)],
        53 * MIB,
    )
    *send, place = call(
        lambda *refs: sort_kernel("group", pieces, capacity, *refs),
        [
            jax.ShapeDtypeStruct((width * size // LANES + TAIL, LANES), jnp.bfloat16)
            for size in sizes
        ]
        + [jax.ShapeDtypeStruct((1, rows), jnp.int32)],
        [],
        (units, *lax.optimization_barrier((row_group.reshape(1, rows), row_cluster.reshape(1, rows)))),
        2 * rows * slots * width,
        4 * rows * width,
    )

    late = [groups - 1] if groups > 1 else []
    early = list(range(groups - len(late)))
    near = [r for r in range(1, roles) if 2 * offsets[r] != shards]
    far = [r for r in range(1, roles) if r not in near]
    first = {r: from_offset(send[0], offsets[r]) for r in near}
    own = []
    for k in range(groups):
        own.append([])
        for i in range(pieces[k]):
            piece = send[sum(pieces[:k]) + i]
            if k > 2 and i == pieces[k] - 1:
                piece = after(piece, own[1][0])
            own[k].append(across(piece, k) if k else piece)
    held = [[[] for _ in range(groups)] for _ in offsets]
    held[0] = [[(x, 0, capacity // pieces[k]) for x in own[k]] for k in range(groups)]
    for r in near:
        held[r][0] = [(first[r], 0, capacity)]
    for k in range(1, groups):
        if k == 1:
            block, starts = own[k][0], [0]
            if near:
                block = after(block, first[near[-1]])
            parts = [k]
        else:
            passed = [held[r][k - 2][0][0] for r in near]
            parts = [k]
            some = [own[k][-1]]
            if k == groups - 2 and pieces[-1] == 2:
                parts.append(k + 1)
                some.append(own[k + 1][0])
            block, starts = stack([after(x, *passed) for x in some], WAIT)
        for r in near:
            moved = from_offset(block, offsets[r])
            for j, start in zip(parts, starts):
                held[r][j].append((moved, start, capacity // pieces[j]))
    pack, starts = stack([x for found in own for x in found], 0)
    for r in far:
        got = from_offset(pack, offsets[r])
        place_of = iter(zip(starts, sizes))
        for k in range(groups):
            held[r][k] = [(got, *next(place_of)) for _ in range(pieces[k])]
    everything = [(0, 0, False)]
    everything += [(offsets.index(a), offsets.index(b), both) for a, b, both in pairs]
    steps = [[] for _ in range(4)]
    final = [0] * roles
    for left, right, both in everything:
        for left_ks in (early, late):
            for right_ks in (early, late):
                if left_ks and right_ks:
                    step = 0
                    for role, ks in ((left, left_ks), (right, right_ks)):
                        if role in near:
                            step = max(step, 1 if ks is early else 3 if role == near[0] else 2)
                    task = (left, left_ks, right, right_ks, both)
                    if both and right_ks is late and left_ks is early:
                        task = (right, right_ks, left, left_ks, both)
                    steps[step].append(task)
                    final[right] = max(final[right], step)
                    if both:
                        final[left] = max(final[left], step)
    acc, flats, partial = [], {}, [None] * roles
    for step, tasks in enumerate(steps):
        if tasks:
            done = [r for r in range(roles) if final[r] == step]
            last = not any(steps[step + 1 :])
            acc, ends = score(held, tasks, acc, flats, done, last, slots, width)
            for r, end in zip(done, ends):
                partial[r] = end
    (best,) = call(
        lambda *refs: spread_kernel(ring, offsets, groups, *refs),
        [jax.ShapeDtypeStruct((shards * groups, 1, capacity), jnp.float32)],
        [],
        partial,
        roles * slots,
        4 * roles * slots,
    )
    back = lax.all_to_all(best, ("shard", "group"), split_axis=0, concat_axis=0, tiled=True)
    (result,) = call(
        lambda *refs: place_kernel(groups, *refs),
        [jax.ShapeDtypeStruct((1, rows), jnp.float32)],
        [],
        [back, place],
        rows * slots,
        4 * slots,
    )
    return result.reshape(rows)


def solution(mesh):
    placed = (P(("shard", "group"), None), P(("shard", "group"), None), P(("shard", "group")))
    return jax.shard_map(
        per_device, mesh=mesh, in_specs=placed, out_specs=P(("shard", "group")), check_vma=False
    )
```

```python
import jax
import jax.numpy as jnp
from jax import lax
from jax.experimental import pallas as pl
from jax.experimental.pallas import tpu as pltpu
from jax.sharding import PartitionSpec as P

LANES = 128
TAIL = 16
LOW = -2.0
MIB = 1024 * 1024
WAIT = 2 * 10**10


def ring_order(size):
    if size % 2:
        return list(range(size))
    half = size // 2
    chips = [i ^ (i >> 1) for i in range(half)]
    if sorted(chips) != list(range(half)):
        chips = list(range(half))
    return [2 * chip + core for core in range(2) for chip in chips]


def offset_cover(size):
    offsets = list(dict.fromkeys([0, size // 2, 1 % size, (size - 1) % size]))

    def missing(chosen):
        have = {(a - b) % size for a in chosen for b in chosen}
        return [d for d in range(size) if d not in have]

    while missing(offsets):
        offsets.append(min(range(size), key=lambda x: len(missing(offsets + [x]))))
    pairs = []
    for diff in range(1, size // 2 + 1):
        found = [
            (a, b)
            for b in [(size - 1) % size] + offsets
            for a in offsets
            if (a - b) % size in (diff, size - diff)
        ]
        if 2 * diff == size:
            found = [(a, b) for a, b in found if b == 0] + found
        a, b = found[0]
        pairs.append((a, b, b != 0 or 2 * diff != size))
    return offsets, pairs


def column_of(row):
    size = row.shape[1]
    return jnp.transpose(jnp.broadcast_to(row, (size, size)))


def unit_kernel(far_ref, unit_ref, near_ref, sems):
    parts = sems.shape[0]
    size = far_ref.shape[0] // parts
    copies = [
        pltpu.make_async_copy(
            far_ref.at[pl.ds(i * size, size), :], near_ref.at[pl.ds(i * size, size), :], sems.at[i]
        )
        for i in range(parts)
    ]
    for copy in copies:
        copy.start()
    for i, copy in enumerate(copies):
        copy.wait()
        feats = near_ref[pl.ds(i * size, size), :].astype(jnp.float32)
        squares = jnp.sum(feats * feats, axis=1, keepdims=True) + 1e-06
        unit_ref[pl.ds(i * size, size), :] = (feats * lax.rsqrt(squares)).astype(jnp.bfloat16)


def sort_kernel(axis, unit_ref, group_ref, label_ref, *out_refs):
    *block_refs, place_ref = out_refs
    rows, width = unit_ref.shape
    groups = len(block_refs)
    capacity = (block_refs[0].shape[0] - TAIL) * LANES // width
    slots = groups * capacity
    chunks = width // LANES
    owner = group_ref[...]
    shift = (owner - lax.axis_index(axis)) & (groups - 1)
    rel = jnp.maximum(jnp.where(2 * shift > groups, 2 * (groups - shift), 2 * shift - 1), 0)
    lines = max(8, groups)
    onehot = lax.broadcasted_iota(jnp.int32, (lines, rows), 0) == rel
    before = lax.broadcasted_iota(jnp.int32, (rows, rows), 0) < lax.broadcasted_iota(
        jnp.int32, (rows, rows), 1
    )
    ranks = jnp.dot(
        jnp.where(onehot, 1.0, 0.0).astype(jnp.bfloat16),
        jnp.where(before, 1.0, 0.0).astype(jnp.bfloat16),
        preferred_element_type=jnp.float32,
    )
    rank = jnp.sum(jnp.where(onehot, ranks, 0.0), axis=0, keepdims=True).astype(jnp.int32)
    place_ref[...] = owner * capacity + rank
    move = jnp.where(
        lax.broadcasted_iota(jnp.int32, (slots, rows), 0) == rel * capacity + rank, 1.0, 0.0
    ).astype(jnp.bfloat16)
    labels = jnp.broadcast_to(label_ref[...] + 1, (TAIL, rows)).astype(jnp.bfloat16)
    sorted_labels = (
        lax.dot_general(
            labels, move, (((1,), (1,)), ((), ())), preferred_element_type=jnp.float32
        )
        - 1.0
    ).astype(jnp.bfloat16)
    for k, block_ref in enumerate(block_refs):
        part = slice(k * capacity, (k + 1) * capacity)
        block = jnp.dot(
            move[part], unit_ref[...], preferred_element_type=jnp.float32
        ).astype(jnp.bfloat16)
        for c in range(chunks):
            block_ref[pl.ds(c * capacity, capacity), :] = block[:, c * LANES : (c + 1) * LANES]
        block_ref[pl.ds(chunks * capacity, TAIL), :] = sorted_labels[:, part]


def stack_kernel(*refs):
    for k, ref in enumerate(refs[:-1]):
        refs[-1][k] = ref[...]


def score_kernel(sources, flats, layout, tasks, done, last, *refs):
    *refs, side_ref, row_ref = refs
    if last:
        *refs, best_ref, flat_ref = refs
        inputs, out_refs = refs[: -len(done)], refs[-len(done) :]
    else:
        outs = 2 + len(done)
        inputs, (best_ref, flat_ref, *out_refs) = refs[:-outs], refs[-outs:]
    capacity = LANES
    low = jnp.float32(LOW)
    arrays = 1 + max(index for index, _ in sources.values())
    best_ref[...] = inputs[arrays][...] if len(inputs) > arrays else jnp.full(best_ref.shape, low)

    def units(role, ks):
        rows = pl.ds(ks[0] * capacity, len(ks) * capacity)
        if (role, ks[0]) in flats:
            index, place = flats[role, ks[0]]
            return inputs[arrays + 1 + index][place, rows, :]
        return flat_ref[layout.index(role), rows, :]

    tops = {}
    for (role, k), (index, part) in sources.items():
        ref = inputs[index] if part is None else inputs[index].at[part]
        height = ref.shape[0] - TAIL
        rows = pl.ds(k * capacity, capacity)
        if (role, k) not in flats:
            for c in range(height // capacity):
                flat_ref[layout.index(role), rows, pl.ds(c * LANES, LANES)] = ref[
                    pl.ds(c * capacity, capacity), :
                ]
        tops[role, k] = ref[pl.ds(height, TAIL), :][0:1].astype(jnp.float32)
    for role, k in sorted({(left, k) for left, ks, _, _, _ in tasks for k in ks}):
        side_ref[role, pl.ds(k * capacity, capacity), :] = column_of(tops[role, k])
    turns = sorted({(left, k) for left, ks, _, _, both in tasks if both for k in ks})
    for role, k in turns:
        row_ref[role, pl.ds(k * capacity, capacity), :] = jnp.full((capacity, LANES), low)
    for left, left_ks, right, right_ks, both in tasks:
        start, count = left_ks[0] * capacity, len(left_ks) * capacity
        rows = pl.ds(start, count)
        for i in range(0, len(right_ks), 2):
            some = right_ks[i : i + 2]
            width = len(some) * capacity
            columns = pl.ds(some[0] * capacity, width)
            scores = lax.dot_general(
                units(left, left_ks),
                units(right, some),
                (((1,), (1,)), ((), ())),
                preferred_element_type=jnp.float32,
            )
            top = jnp.concatenate([tops[right, k] for k in some], axis=1)
            same = jnp.concatenate([side_ref[left, rows, :]] * len(some), axis=1) == top
            if left == right:
                same = same & (
                    lax.broadcasted_iota(jnp.int32, (count, width), 0) + start
                    != lax.broadcasted_iota(jnp.int32, (count, width), 1) + some[0] * capacity
                )
            scores = jnp.where(same, scores, low)
            if both:
                best = row_ref[left, rows, :]
                for c in range(len(some)):
                    best = jnp.maximum(best, scores[:, c * LANES : (c + 1) * LANES])
                row_ref[left, rows, :] = best
            best = jnp.max(scores.reshape(count // 8, 8, width), axis=0)
            best_ref[right, :, columns] = jnp.maximum(best_ref[right, :, columns], best)
    for role, k in turns:
        rows = pl.ds(k * capacity, capacity)
        turned = jnp.transpose(row_ref[role, rows, :]).reshape(capacity // 8, 8, capacity)
        best_ref[role, :, rows] = jnp.maximum(best_ref[role, :, rows], jnp.max(turned, axis=0))
    for role, out_ref in zip(done, out_refs):
        out_ref[...] = jnp.max(best_ref[role], axis=0, keepdims=True)


def slot_shift(k):
    return (k + 1) // 2 if k % 2 else -(k // 2)


def spread_kernel(ring, offsets, groups, *refs):
    *partial_refs, out_ref = refs
    shards = len(ring)
    out_ref[...] = jnp.full(out_ref.shape, jnp.float32(LOW))
    shard, group = lax.axis_index("shard"), lax.axis_index("group")
    for offset, ref in zip(offsets, partial_refs):
        target = sum(
            jnp.where(shard == ring[e], ring[(e + offset) % shards], 0) for e in range(shards)
        )
        for k in range(groups):
            row = target * groups + ((group - slot_shift(k)) & (groups - 1))
            out_ref[pl.ds(row, 1)] = ref[:, k * LANES : (k + 1) * LANES].reshape(1, 1, LANES)


def place_kernel(groups, back_ref, place_ref, out_ref):
    place = place_ref[...]
    rows = place.shape[1]
    best = jnp.full((1, rows), jnp.float32(LOW))
    for g in range(groups):
        row = jnp.full((1, LANES), jnp.float32(-1.0))
        for s in range(back_ref.shape[0] // groups):
            row = jnp.maximum(row, back_ref[s * groups + g])
        values = jnp.concatenate([column_of(row)] * (rows // LANES), axis=1)
        here = lax.broadcasted_iota(jnp.int32, (LANES, rows), 0) + g * LANES == place
        best = jnp.maximum(
            best, jnp.max(jnp.where(here, values, jnp.float32(LOW)), axis=0, keepdims=True)
        )
    out_ref[...] = best


def in_vmem(count):
    return [pl.BlockSpec(memory_space=pltpu.VMEM)] * count


def call(
    kernel, out_shape, scratch, args, flops, bytes_accessed, in_specs=None, limit=24 * MIB
):
    return pl.pallas_call(
        kernel,
        out_shape=out_shape,
        in_specs=in_specs or in_vmem(len(args)),
        out_specs=in_vmem(len(out_shape)),
        scratch_shapes=scratch,
        compiler_params=pltpu.CompilerParams(vmem_limit_bytes=limit),
        cost_estimate=pl.CostEstimate(
            flops=flops, bytes_accessed=bytes_accessed, transcendentals=0
        ),
    )(*args)


def after(x, *earlier):
    return lax.optimization_barrier((x, *earlier))[0]


def stack(parts, wait):
    return call(
        stack_kernel,
        [jax.ShapeDtypeStruct((len(parts), *parts[0].shape), parts[0].dtype)],
        [],
        parts,
        wait,
        4 * len(parts) * parts[0].size,
    )[0]


def score(held, tasks, acc, flats, done, last, slots, width):
    roles = len(held)
    used = sorted(
        {(left, k) for left, ks, _, _, _ in tasks for k in ks}
        | {(right, k) for _, _, right, ks, _ in tasks for k in ks},
        key=lambda x: (x[0], -x[1]),
    )
    arrays, sources = [], {}
    for role, k in used:
        array, part = held[role][k]
        index = next((i for i, x in enumerate(arrays) if x is array), len(arrays))
        if index == len(arrays):
            arrays.append(array)
        sources[role, k] = (index, part)
    layout = sorted({role for role, k in used if (role, k) not in flats})
    tiles = sum(len(task[1]) * len(task[3]) for task in tasks)
    kept = [
        jax.ShapeDtypeStruct((roles, 8, slots), jnp.float32),
        jax.ShapeDtypeStruct((len(layout), slots, width), jnp.bfloat16),
    ]
    scratch = [pltpu.VMEM((roles, slots, LANES), jnp.float32)] * 2
    if last:
        scratch = [pltpu.VMEM(x.shape, x.dtype) for x in kept] + scratch
        kept = []
    known = dict(flats)
    got = call(
        lambda *refs: score_kernel(sources, known, layout, tasks, done, last, *refs),
        kept + [jax.ShapeDtypeStruct((1, slots), jnp.float32)] * len(done),
        scratch,
        arrays + list(acc),
        2 * tiles * LANES * LANES * width,
        2 * len(used) * LANES * width,
    )
    if last:
        return acc, got
    for role, k in used:
        if (role, k) not in flats:
            flats[role, k] = (max(len(acc) - 1, 0), layout.index(role))
    return [got[0], *acc[1:], got[1]], got[2:]


def per_device(embeddings, row_group, row_cluster):
    rows, width = embeddings.shape
    groups = lax.axis_size("group")
    shards = lax.axis_size("shard")
    capacity = rows // 4
    slots = groups * capacity
    ring = ring_order(shards)
    offsets, pairs = offset_cover(shards)
    roles = len(offsets)
    height = width * capacity // LANES + TAIL

    def from_offset(x, offset):
        perm = [(ring[(e + offset) % shards], ring[e]) for e in range(shards)]
        return lax.ppermute(x, "shard", perm)

    def exchange(blocks):
        got = list(blocks)
        for k in range(1, groups):
            shift = slot_shift(k)
            block = after(blocks[k], got[1]) if k > 2 else blocks[k]
            got[k] = lax.ppermute(block, "group", [(z, (z + shift) % groups) for z in range(groups)])
        return got

    (units,) = call(
        unit_kernel,
        [jax.ShapeDtypeStruct((rows, width), jnp.bfloat16)],
        [pltpu.VMEM((rows, width), embeddings.dtype), pltpu.SemaphoreType.DMA((2,))],
        (embeddings,),
        4 * rows * width,
        4 * rows * width,
        [pl.BlockSpec(memory_space=pltpu.HBM)],
        53 * MIB,
    )
    *send, place = call(
        lambda *refs: sort_kernel("group", *refs),
        [jax.ShapeDtypeStruct((height, LANES), jnp.bfloat16)] * groups
        + [jax.ShapeDtypeStruct((1, rows), jnp.int32)],
        [],
        (units, *lax.optimization_barrier((row_group.reshape(1, rows), row_cluster.reshape(1, rows)))),
        2 * rows * slots * width,
        4 * rows * width,
    )

    late = [groups - 1] if groups > 1 else []
    early = list(range(groups - len(late)))
    late = [groups - 1] if groups > 1 else []
    early = list(range(groups - len(late)))
    near = [r for r in range(1, roles) if 2 * offsets[r] != shards]
    far = [r for r in range(1, roles) if r not in near]
    first = {r: from_offset(send[0], offsets[r]) for r in near}
    own = exchange(send)
    held = [[None] * groups for _ in offsets]
    held[0] = [(x, None) for x in own]
    for r in near:
        held[r][0] = (first[r], None)
    for ks in (early[1:], late):
        if ks:
            block = stack([own[k] for k in ks], WAIT)
            for r in near:
                moved = from_offset(block, offsets[r])
                for i, k in enumerate(ks):
                    held[r][k] = (moved, i)
    got = {r: from_offset(stack(own, 0), offsets[r]) for r in far}
    for r in far:
        held[r] = [(got[r], k) for k in range(groups)]
    everything = [(0, 0, False)]
    everything += [(offsets.index(a), offsets.index(b), both) for a, b, both in pairs]
    steps = [[] for _ in range(4)]
    final = [0] * roles
    for left, right, both in everything:
        for left_ks in (early, late):
            for right_ks in (early, late):
                if left_ks and right_ks:
                    step = 0
                    for role, ks in ((left, left_ks), (right, right_ks)):
                        if role in near:
                            step = max(step, 1 if ks is early else 3 if role == near[0] else 2)
                    task = (left, left_ks, right, right_ks, both)
                    if both and right_ks is late and left_ks is early:
                        task = (right, right_ks, left, left_ks, both)
                    steps[step].append(task)
                    final[right] = max(final[right], step)
                    if both:
                        final[left] = max(final[left], step)
    acc, flats, partial = [], {}, [None] * roles
    for step, tasks in enumerate(steps):
        if tasks:
            done = [r for r in range(roles) if final[r] == step]
            last = not any(steps[step + 1 :])
            acc, ends = score(held, tasks, acc, flats, done, last, slots, width)
            for r, end in zip(done, ends):
                partial[r] = end
    (best,) = call(
        lambda *refs: spread_kernel(ring, offsets, groups, *refs),
        [jax.ShapeDtypeStruct((shards * groups, 1, capacity), jnp.float32)],
        [],
        partial,
        roles * slots,
        4 * roles * slots,
    )
    back = lax.all_to_all(best, ("shard", "group"), split_axis=0, concat_axis=0, tiled=True)
    (result,) = call(
        lambda *refs: place_kernel(groups, *refs),
        [jax.ShapeDtypeStruct((1, rows), jnp.float32)],
        [],
        [back, place],
        rows * slots,
        4 * slots,
    )
    return result.reshape(rows)


def solution(mesh):
    placed = (P(("shard", "group"), None), P(("shard", "group"), None), P(("shard", "group")))
    return jax.shard_map(
        per_device, mesh=mesh, in_specs=placed, out_specs=P(("shard", "group")), check_vma=False
    )
```

```python
import jax
import jax.numpy as jnp
from jax import lax
from jax.experimental import pallas as pl
from jax.experimental.pallas import tpu as pltpu
from jax.sharding import PartitionSpec as P

LANES = 128
TAIL = 16
LOW = -2.0
MIB = 1024 * 1024
WAIT = 2 * 10**10


def ring_order(size):
    if size % 2:
        return list(range(size))
    half = size // 2
    chips = [i ^ (i >> 1) for i in range(half)]
    if sorted(chips) != list(range(half)):
        chips = list(range(half))
    return [2 * chip + core for core in range(2) for chip in chips]


def offset_cover(size):
    offsets = list(dict.fromkeys([0, size // 2, 1 % size, (size - 1) % size]))

    def missing(chosen):
        have = {(a - b) % size for a in chosen for b in chosen}
        return [d for d in range(size) if d not in have]

    while missing(offsets):
        offsets.append(min(range(size), key=lambda x: len(missing(offsets + [x]))))
    pairs = []
    for diff in range(1, size // 2 + 1):
        found = [
            (a, b)
            for b in [(size - 1) % size] + offsets
            for a in offsets
            if (a - b) % size in (diff, size - diff)
        ]
        if 2 * diff == size:
            found = [(a, b) for a, b in found if b == 0] + found
        a, b = found[0]
        pairs.append((a, b, b != 0 or 2 * diff != size))
    return offsets, pairs


def column_of(row):
    size = row.shape[1]
    return jnp.transpose(jnp.broadcast_to(row, (size, size)))


def unit_kernel(far_ref, unit_ref, near_ref, sems):
    parts = sems.shape[0]
    size = far_ref.shape[0] // parts
    copies = [
        pltpu.make_async_copy(
            far_ref.at[pl.ds(i * size, size), :], near_ref.at[pl.ds(i * size, size), :], sems.at[i]
        )
        for i in range(parts)
    ]
    for copy in copies:
        copy.start()
    for i, copy in enumerate(copies):
        copy.wait()
        feats = near_ref[pl.ds(i * size, size), :].astype(jnp.float32)
        squares = jnp.sum(feats * feats, axis=1, keepdims=True) + 1e-06
        unit_ref[pl.ds(i * size, size), :] = (feats * lax.rsqrt(squares)).astype(jnp.bfloat16)


def sort_kernel(axis, unit_ref, group_ref, label_ref, *out_refs):
    *block_refs, place_ref = out_refs
    rows, width = unit_ref.shape
    groups = len(block_refs)
    capacity = (block_refs[0].shape[0] - TAIL) * LANES // width
    slots = groups * capacity
    chunks = width // LANES
    owner = group_ref[...]
    shift = (owner - lax.axis_index(axis)) & (groups - 1)
    rel = jnp.maximum(jnp.where(2 * shift > groups, 2 * (groups - shift), 2 * shift - 1), 0)
    lines = max(8, groups)
    onehot = lax.broadcasted_iota(jnp.int32, (lines, rows), 0) == rel
    before = lax.broadcasted_iota(jnp.int32, (rows, rows), 0) < lax.broadcasted_iota(
        jnp.int32, (rows, rows), 1
    )
    ranks = jnp.dot(
        jnp.where(onehot, 1.0, 0.0).astype(jnp.bfloat16),
        jnp.where(before, 1.0, 0.0).astype(jnp.bfloat16),
        preferred_element_type=jnp.float32,
    )
    rank = jnp.sum(jnp.where(onehot, ranks, 0.0), axis=0, keepdims=True).astype(jnp.int32)
    place_ref[...] = owner * capacity + rank
    move = jnp.where(
        lax.broadcasted_iota(jnp.int32, (slots, rows), 0) == rel * capacity + rank, 1.0, 0.0
    ).astype(jnp.bfloat16)
    labels = jnp.broadcast_to(label_ref[...] + 1, (TAIL, rows)).astype(jnp.bfloat16)
    sorted_labels = (
        lax.dot_general(
            labels, move, (((1,), (1,)), ((), ())), preferred_element_type=jnp.float32
        )
        - 1.0
    ).astype(jnp.bfloat16)
    for k, block_ref in enumerate(block_refs):
        part = slice(k * capacity, (k + 1) * capacity)
        block = jnp.dot(
            move[part], unit_ref[...], preferred_element_type=jnp.float32
        ).astype(jnp.bfloat16)
        for c in range(chunks):
            block_ref[pl.ds(c * capacity, capacity), :] = block[:, c * LANES : (c + 1) * LANES]
        block_ref[pl.ds(chunks * capacity, TAIL), :] = sorted_labels[:, part]


def stack_kernel(*refs):
    for k, ref in enumerate(refs[:-1]):
        refs[-1][k] = ref[...]


def score_kernel(sources, flats, layout, tasks, done, last, *refs):
    *refs, side_ref, row_ref = refs
    if last:
        *refs, best_ref, flat_ref = refs
        inputs, out_refs = refs[: -len(done)], refs[-len(done) :]
    else:
        outs = 2 + len(done)
        inputs, (best_ref, flat_ref, *out_refs) = refs[:-outs], refs[-outs:]
    capacity = LANES
    low = jnp.float32(LOW)
    arrays = 1 + max(index for index, _ in sources.values())
    best_ref[...] = inputs[arrays][...] if len(inputs) > arrays else jnp.full(best_ref.shape, low)

    def units(role, ks):
        rows = pl.ds(ks[0] * capacity, len(ks) * capacity)
        if (role, ks[0]) in flats:
            index, place = flats[role, ks[0]]
            return inputs[arrays + 1 + index][place, rows, :]
        return flat_ref[layout.index(role), rows, :]

    tops = {}
    for (role, k), (index, part) in sources.items():
        ref = inputs[index] if part is None else inputs[index].at[part]
        height = ref.shape[0] - TAIL
        rows = pl.ds(k * capacity, capacity)
        if (role, k) not in flats:
            for c in range(height // capacity):
                flat_ref[layout.index(role), rows, pl.ds(c * LANES, LANES)] = ref[
                    pl.ds(c * capacity, capacity), :
                ]
        tops[role, k] = ref[pl.ds(height, TAIL), :][0:1].astype(jnp.float32)
    for role, k in sorted({(left, k) for left, ks, _, _, _ in tasks for k in ks}):
        side_ref[role, pl.ds(k * capacity, capacity), :] = column_of(tops[role, k])
    turns = sorted({(left, k) for left, ks, _, _, both in tasks if both for k in ks})
    for role, k in turns:
        row_ref[role, pl.ds(k * capacity, capacity), :] = jnp.full((capacity, LANES), low)
    for left, left_ks, right, right_ks, both in tasks:
        start, count = left_ks[0] * capacity, len(left_ks) * capacity
        rows = pl.ds(start, count)
        for i in range(0, len(right_ks), 2):
            some = right_ks[i : i + 2]
            width = len(some) * capacity
            columns = pl.ds(some[0] * capacity, width)
            scores = lax.dot_general(
                units(left, left_ks),
                units(right, some),
                (((1,), (1,)), ((), ())),
                preferred_element_type=jnp.float32,
            )
            top = jnp.concatenate([tops[right, k] for k in some], axis=1)
            same = jnp.concatenate([side_ref[left, rows, :]] * len(some), axis=1) == top
            if left == right:
                same = same & (
                    lax.broadcasted_iota(jnp.int32, (count, width), 0) + start
                    != lax.broadcasted_iota(jnp.int32, (count, width), 1) + some[0] * capacity
                )
            scores = jnp.where(same, scores, low)
            if both:
                best = row_ref[left, rows, :]
                for c in range(len(some)):
                    best = jnp.maximum(best, scores[:, c * LANES : (c + 1) * LANES])
                row_ref[left, rows, :] = best
            best = jnp.max(scores.reshape(count // 8, 8, width), axis=0)
            best_ref[right, :, columns] = jnp.maximum(best_ref[right, :, columns], best)
    for role, k in turns:
        rows = pl.ds(k * capacity, capacity)
        turned = jnp.transpose(row_ref[role, rows, :]).reshape(capacity // 8, 8, capacity)
        best_ref[role, :, rows] = jnp.maximum(best_ref[role, :, rows], jnp.max(turned, axis=0))
    for role, out_ref in zip(done, out_refs):
        out_ref[...] = jnp.max(best_ref[role], axis=0, keepdims=True)


def slot_shift(k):
    return (k + 1) // 2 if k % 2 else -(k // 2)


def spread_kernel(ring, offsets, groups, *refs):
    *partial_refs, out_ref = refs
    shards = len(ring)
    out_ref[...] = jnp.full(out_ref.shape, jnp.float32(LOW))
    shard, group = lax.axis_index("shard"), lax.axis_index("group")
    for offset, ref in zip(offsets, partial_refs):
        target = sum(
            jnp.where(shard == ring[e], ring[(e + offset) % shards], 0) for e in range(shards)
        )
        for k in range(groups):
            row = target * groups + ((group - slot_shift(k)) & (groups - 1))
            out_ref[pl.ds(row, 1)] = ref[:, k * LANES : (k + 1) * LANES].reshape(1, 1, LANES)


def place_kernel(groups, back_ref, place_ref, out_ref):
    place = place_ref[...]
    rows = place.shape[1]
    best = jnp.full((1, rows), jnp.float32(LOW))
    for g in range(groups):
        row = jnp.full((1, LANES), jnp.float32(-1.0))
        for s in range(back_ref.shape[0] // groups):
            row = jnp.maximum(row, back_ref[s * groups + g])
        values = jnp.concatenate([column_of(row)] * (rows // LANES), axis=1)
        here = lax.broadcasted_iota(jnp.int32, (LANES, rows), 0) + g * LANES == place
        best = jnp.maximum(
            best, jnp.max(jnp.where(here, values, jnp.float32(LOW)), axis=0, keepdims=True)
        )
    out_ref[...] = best


def in_vmem(count):
    return [pl.BlockSpec(memory_space=pltpu.VMEM)] * count


def call(
    kernel, out_shape, scratch, args, flops, bytes_accessed, in_specs=None, limit=24 * MIB
):
    return pl.pallas_call(
        kernel,
        out_shape=out_shape,
        in_specs=in_specs or in_vmem(len(args)),
        out_specs=in_vmem(len(out_shape)),
        scratch_shapes=scratch,
        compiler_params=pltpu.CompilerParams(vmem_limit_bytes=limit),
        cost_estimate=pl.CostEstimate(
            flops=flops, bytes_accessed=bytes_accessed, transcendentals=0
        ),
    )(*args)


def after(x, *earlier):
    return lax.optimization_barrier((x, *earlier))[0]


def stack(parts, wait):
    return call(
        stack_kernel,
        [jax.ShapeDtypeStruct((len(parts), *parts[0].shape), parts[0].dtype)],
        [],
        parts,
        wait,
        4 * len(parts) * parts[0].size,
    )[0]


def score(held, tasks, acc, flats, done, last, slots, width):
    roles = len(held)
    used = sorted(
        {(left, k) for left, ks, _, _, _ in tasks for k in ks}
        | {(right, k) for _, _, right, ks, _ in tasks for k in ks},
        key=lambda x: (x[0], -x[1]),
    )
    arrays, sources = [], {}
    for role, k in used:
        array, part = held[role][k]
        index = next((i for i, x in enumerate(arrays) if x is array), len(arrays))
        if index == len(arrays):
            arrays.append(array)
        sources[role, k] = (index, part)
    layout = sorted({role for role, k in used if (role, k) not in flats})
    tiles = sum(len(task[1]) * len(task[3]) for task in tasks)
    kept = [
        jax.ShapeDtypeStruct((roles, 8, slots), jnp.float32),
        jax.ShapeDtypeStruct((len(layout), slots, width), jnp.bfloat16),
    ]
    scratch = [pltpu.VMEM((roles, slots, LANES), jnp.float32)] * 2
    if last:
        scratch = [pltpu.VMEM(x.shape, x.dtype) for x in kept] + scratch
        kept = []
    known = dict(flats)
    got = call(
        lambda *refs: score_kernel(sources, known, layout, tasks, done, last, *refs),
        kept + [jax.ShapeDtypeStruct((1, slots), jnp.float32)] * len(done),
        scratch,
        arrays + list(acc),
        2 * tiles * LANES * LANES * width,
        2 * len(used) * LANES * width,
    )
    if last:
        return acc, got
    for role, k in used:
        if (role, k) not in flats:
            flats[role, k] = (max(len(acc) - 1, 0), layout.index(role))
    return [got[0], *acc[1:], got[1]], got[2:]


def per_device(embeddings, row_group, row_cluster):
    rows, width = embeddings.shape
    groups = lax.axis_size("group")
    shards = lax.axis_size("shard")
    capacity = rows // 4
    slots = groups * capacity
    ring = ring_order(shards)
    offsets, pairs = offset_cover(shards)
    roles = len(offsets)
    height = width * capacity // LANES + TAIL

    def from_offset(x, offset):
        perm = [(ring[(e + offset) % shards], ring[e]) for e in range(shards)]
        return lax.ppermute(x, "shard", perm)

    def exchange(blocks):
        got = list(blocks)
        for k in range(1, groups):
            shift = slot_shift(k)
            block = after(blocks[k], got[1], got[2]) if k > 2 else blocks[k]
            got[k] = lax.ppermute(block, "group", [(z, (z + shift) % groups) for z in range(groups)])
        return got

    (units,) = call(
        unit_kernel,
        [jax.ShapeDtypeStruct((rows, width), jnp.bfloat16)],
        [pltpu.VMEM((rows, width), embeddings.dtype), pltpu.SemaphoreType.DMA((2,))],
        (embeddings,),
        4 * rows * width,
        4 * rows * width,
        [pl.BlockSpec(memory_space=pltpu.HBM)],
        53 * MIB,
    )
    *send, place = call(
        lambda *refs: sort_kernel("group", *refs),
        [jax.ShapeDtypeStruct((height, LANES), jnp.bfloat16)] * groups
        + [jax.ShapeDtypeStruct((1, rows), jnp.int32)],
        [],
        (units, *lax.optimization_barrier((row_group.reshape(1, rows), row_cluster.reshape(1, rows)))),
        2 * rows * slots * width,
        4 * rows * width,
    )

    late = [groups - 1] if groups > 1 else []
    early = list(range(groups - len(late)))
    late = [groups - 1] if groups > 1 else []
    early = list(range(groups - len(late)))
    near = [r for r in range(1, roles) if 2 * offsets[r] != shards]
    far = [r for r in range(1, roles) if r not in near]
    first = {r: from_offset(send[0], offsets[r]) for r in near}
    own = exchange(send)
    held = [[None] * groups for _ in offsets]
    held[0] = [(x, None) for x in own]
    for r in near:
        held[r][0] = (first[r], None)
    for ks in (early[1:], late):
        if ks:
            block = stack([own[k] for k in ks], WAIT)
            for r in near:
                moved = from_offset(block, offsets[r])
                for i, k in enumerate(ks):
                    held[r][k] = (moved, i)
    got = {r: from_offset(stack(own, 0), offsets[r]) for r in far}
    for r in far:
        held[r] = [(got[r], k) for k in range(groups)]
    everything = [(0, 0, False)]
    everything += [(offsets.index(a), offsets.index(b), both) for a, b, both in pairs]
    steps = [[] for _ in range(4)]
    final = [0] * roles
    for left, right, both in everything:
        for left_ks in (early, late):
            for right_ks in (early, late):
                if left_ks and right_ks:
                    step = 0
                    for role, ks in ((left, left_ks), (right, right_ks)):
                        if role in near:
                            step = max(step, 1 if ks is early else 3 if role == near[0] else 2)
                    task = (left, left_ks, right, right_ks, both)
                    if both and right_ks is late and left_ks is early:
                        task = (right, right_ks, left, left_ks, both)
                    steps[step].append(task)
                    final[right] = max(final[right], step)
                    if both:
                        final[left] = max(final[left], step)
    acc, flats, partial = [], {}, [None] * roles
    for step, tasks in enumerate(steps):
        if tasks:
            done = [r for r in range(roles) if final[r] == step]
            last = not any(steps[step + 1 :])
            acc, ends = score(held, tasks, acc, flats, done, last, slots, width)
            for r, end in zip(done, ends):
                partial[r] = end
    (best,) = call(
        lambda *refs: spread_kernel(ring, offsets, groups, *refs),
        [jax.ShapeDtypeStruct((shards * groups, 1, capacity), jnp.float32)],
        [],
        partial,
        roles * slots,
        4 * roles * slots,
    )
    back = lax.all_to_all(best, ("shard", "group"), split_axis=0, concat_axis=0, tiled=True)
    (result,) = call(
        lambda *refs: place_kernel(groups, *refs),
        [jax.ShapeDtypeStruct((1, rows), jnp.float32)],
        [],
        [back, place],
        rows * slots,
        4 * slots,
    )
    return result.reshape(rows)


def solution(mesh):
    placed = (P(("shard", "group"), None), P(("shard", "group"), None), P(("shard", "group")))
    return jax.shard_map(
        per_device, mesh=mesh, in_specs=placed, out_specs=P(("shard", "group")), check_vma=False
    )
```

```python
import jax
import jax.numpy as jnp
from jax import lax
from jax.experimental import pallas as pl
from jax.experimental.pallas import tpu as pltpu
from jax.sharding import PartitionSpec as P

LANES = 128
TAIL = 16
LOW = -2.0
MIB = 1024 * 1024
WAIT = 2 * 10**10


def ring_order(size):
    if size % 2:
        return list(range(size))
    half = size // 2
    chips = [i ^ (i >> 1) for i in range(half)]
    if sorted(chips) != list(range(half)):
        chips = list(range(half))
    return [2 * chip + core for core in range(2) for chip in chips]


def offset_cover(size):
    offsets = list(dict.fromkeys([0, size // 2, 1 % size, (size - 1) % size]))

    def missing(chosen):
        have = {(a - b) % size for a in chosen for b in chosen}
        return [d for d in range(size) if d not in have]

    while missing(offsets):
        offsets.append(min(range(size), key=lambda x: len(missing(offsets + [x]))))
    pairs = []
    for diff in range(1, size // 2 + 1):
        found = [
            (a, b)
            for b in [(size - 1) % size] + offsets
            for a in offsets
            if (a - b) % size in (diff, size - diff)
        ]
        if 2 * diff == size:
            found = [(a, b) for a, b in found if b == 0] + found
        a, b = found[0]
        pairs.append((a, b, b != 0 or 2 * diff != size))
    return offsets, pairs


def column_of(row):
    size = row.shape[1]
    return jnp.transpose(jnp.broadcast_to(row, (size, size)))


def unit_kernel(far_ref, unit_ref, near_ref, sems):
    parts = sems.shape[0]
    size = far_ref.shape[0] // parts
    copies = [
        pltpu.make_async_copy(
            far_ref.at[pl.ds(i * size, size), :], near_ref.at[pl.ds(i * size, size), :], sems.at[i]
        )
        for i in range(parts)
    ]
    for copy in copies:
        copy.start()
    for i, copy in enumerate(copies):
        copy.wait()
        feats = near_ref[pl.ds(i * size, size), :].astype(jnp.float32)
        squares = jnp.sum(feats * feats, axis=1, keepdims=True) + 1e-06
        unit_ref[pl.ds(i * size, size), :] = (feats * lax.rsqrt(squares)).astype(jnp.bfloat16)


def sort_kernel(axis, unit_ref, group_ref, label_ref, *out_refs):
    *block_refs, place_ref = out_refs
    rows, width = unit_ref.shape
    groups = len(block_refs)
    capacity = (block_refs[0].shape[0] - TAIL) * LANES // width
    slots = groups * capacity
    chunks = width // LANES
    owner = group_ref[...]
    shift = (owner - lax.axis_index(axis)) & (groups - 1)
    rel = jnp.maximum(jnp.where(2 * shift > groups, 2 * (groups - shift), 2 * shift - 1), 0)
    lines = max(8, groups)
    onehot = lax.broadcasted_iota(jnp.int32, (lines, rows), 0) == rel
    before = lax.broadcasted_iota(jnp.int32, (rows, rows), 0) < lax.broadcasted_iota(
        jnp.int32, (rows, rows), 1
    )
    ranks = jnp.dot(
        jnp.where(onehot, 1.0, 0.0).astype(jnp.bfloat16),
        jnp.where(before, 1.0, 0.0).astype(jnp.bfloat16),
        preferred_element_type=jnp.float32,
    )
    rank = jnp.sum(jnp.where(onehot, ranks, 0.0), axis=0, keepdims=True).astype(jnp.int32)
    place_ref[...] = owner * capacity + rank
    move = jnp.where(
        lax.broadcasted_iota(jnp.int32, (slots, rows), 0) == rel * capacity + rank, 1.0, 0.0
    ).astype(jnp.bfloat16)
    labels = jnp.broadcast_to(label_ref[...] + 1, (TAIL, rows)).astype(jnp.bfloat16)
    sorted_labels = (
        lax.dot_general(
            labels, move, (((1,), (1,)), ((), ())), preferred_element_type=jnp.float32
        )
        - 1.0
    ).astype(jnp.bfloat16)
    for k, block_ref in enumerate(block_refs):
        part = slice(k * capacity, (k + 1) * capacity)
        block = jnp.dot(
            move[part], unit_ref[...], preferred_element_type=jnp.float32
        ).astype(jnp.bfloat16)
        for c in range(chunks):
            block_ref[pl.ds(c * capacity, capacity), :] = block[:, c * LANES : (c + 1) * LANES]
        block_ref[pl.ds(chunks * capacity, TAIL), :] = sorted_labels[:, part]


def stack_kernel(*refs):
    for k, ref in enumerate(refs[:-1]):
        refs[-1][k] = ref[...]


def score_kernel(sources, flats, layout, tasks, done, last, *refs):
    *refs, side_ref, row_ref = refs
    if last:
        *refs, best_ref, flat_ref = refs
        inputs, out_refs = refs[: -len(done)], refs[-len(done) :]
    else:
        outs = 2 + len(done)
        inputs, (best_ref, flat_ref, *out_refs) = refs[:-outs], refs[-outs:]
    capacity = LANES
    low = jnp.float32(LOW)
    arrays = 1 + max(index for index, _ in sources.values())
    best_ref[...] = inputs[arrays][...] if len(inputs) > arrays else jnp.full(best_ref.shape, low)

    def units(role, ks):
        rows = pl.ds(ks[0] * capacity, len(ks) * capacity)
        if (role, ks[0]) in flats:
            index, place = flats[role, ks[0]]
            return inputs[arrays + 1 + index][place, rows, :]
        return flat_ref[layout.index(role), rows, :]

    tops = {}
    for (role, k), (index, part) in sources.items():
        ref = inputs[index] if part is None else inputs[index].at[part]
        height = ref.shape[0] - TAIL
        rows = pl.ds(k * capacity, capacity)
        if (role, k) not in flats:
            for c in range(height // capacity):
                flat_ref[layout.index(role), rows, pl.ds(c * LANES, LANES)] = ref[
                    pl.ds(c * capacity, capacity), :
                ]
        tops[role, k] = ref[pl.ds(height, TAIL), :][0:1].astype(jnp.float32)
    for role, k in sorted({(left, k) for left, ks, _, _, _ in tasks for k in ks}):
        side_ref[role, pl.ds(k * capacity, capacity), :] = column_of(tops[role, k])
    turns = sorted({(left, k) for left, ks, _, _, both in tasks if both for k in ks})
    for role, k in turns:
        row_ref[role, pl.ds(k * capacity, capacity), :] = jnp.full((capacity, LANES), low)
    for left, left_ks, right, right_ks, both in tasks:
        start, count = left_ks[0] * capacity, len(left_ks) * capacity
        rows = pl.ds(start, count)
        for i in range(0, len(right_ks), 2):
            some = right_ks[i : i + 2]
            width = len(some) * capacity
            columns = pl.ds(some[0] * capacity, width)
            scores = lax.dot_general(
                units(left, left_ks),
                units(right, some),
                (((1,), (1,)), ((), ())),
                preferred_element_type=jnp.float32,
            )
            top = jnp.concatenate([tops[right, k] for k in some], axis=1)
            same = jnp.concatenate([side_ref[left, rows, :]] * len(some), axis=1) == top
            if left == right:
                same = same & (
                    lax.broadcasted_iota(jnp.int32, (count, width), 0) + start
                    != lax.broadcasted_iota(jnp.int32, (count, width), 1) + some[0] * capacity
                )
            scores = jnp.where(same, scores, low)
            if both:
                best = row_ref[left, rows, :]
                for c in range(len(some)):
                    best = jnp.maximum(best, scores[:, c * LANES : (c + 1) * LANES])
                row_ref[left, rows, :] = best
            best = jnp.max(scores.reshape(count // 8, 8, width), axis=0)
            best_ref[right, :, columns] = jnp.maximum(best_ref[right, :, columns], best)
    for role, k in turns:
        rows = pl.ds(k * capacity, capacity)
        turned = jnp.transpose(row_ref[role, rows, :]).reshape(capacity // 8, 8, capacity)
        best_ref[role, :, rows] = jnp.maximum(best_ref[role, :, rows], jnp.max(turned, axis=0))
    for role, out_ref in zip(done, out_refs):
        out_ref[...] = jnp.max(best_ref[role], axis=0, keepdims=True)


def slot_shift(k):
    return (k + 1) // 2 if k % 2 else -(k // 2)


def spread_kernel(ring, offsets, groups, *refs):
    *partial_refs, out_ref = refs
    shards = len(ring)
    out_ref[...] = jnp.full(out_ref.shape, jnp.float32(LOW))
    shard, group = lax.axis_index("shard"), lax.axis_index("group")
    for offset, ref in zip(offsets, partial_refs):
        target = sum(
            jnp.where(shard == ring[e], ring[(e + offset) % shards], 0) for e in range(shards)
        )
        for k in range(groups):
            row = target * groups + ((group - slot_shift(k)) & (groups - 1))
            out_ref[pl.ds(row, 1)] = ref[:, k * LANES : (k + 1) * LANES].reshape(1, 1, LANES)


def place_kernel(groups, back_ref, place_ref, out_ref):
    place = place_ref[...]
    rows = place.shape[1]
    best = jnp.full((1, rows), jnp.float32(LOW))
    for g in range(groups):
        row = jnp.full((1, LANES), jnp.float32(-1.0))
        for s in range(back_ref.shape[0] // groups):
            row = jnp.maximum(row, back_ref[s * groups + g])
        values = jnp.concatenate([column_of(row)] * (rows // LANES), axis=1)
        here = lax.broadcasted_iota(jnp.int32, (LANES, rows), 0) + g * LANES == place
        best = jnp.maximum(
            best, jnp.max(jnp.where(here, values, jnp.float32(LOW)), axis=0, keepdims=True)
        )
    out_ref[...] = best


def in_vmem(count):
    return [pl.BlockSpec(memory_space=pltpu.VMEM)] * count


def call(
    kernel, out_shape, scratch, args, flops, bytes_accessed, in_specs=None, limit=24 * MIB
):
    return pl.pallas_call(
        kernel,
        out_shape=out_shape,
        in_specs=in_specs or in_vmem(len(args)),
        out_specs=in_vmem(len(out_shape)),
        scratch_shapes=scratch,
        compiler_params=pltpu.CompilerParams(vmem_limit_bytes=limit),
        cost_estimate=pl.CostEstimate(
            flops=flops, bytes_accessed=bytes_accessed, transcendentals=0
        ),
    )(*args)


def after(x, *earlier):
    return lax.optimization_barrier((x, *earlier))[0]


def stack(parts, wait):
    return call(
        stack_kernel,
        [jax.ShapeDtypeStruct((len(parts), *parts[0].shape), parts[0].dtype)],
        [],
        parts,
        wait,
        4 * len(parts) * parts[0].size,
    )[0]


def score(held, tasks, acc, flats, done, last, slots, width):
    roles = len(held)
    used = sorted(
        {(left, k) for left, ks, _, _, _ in tasks for k in ks}
        | {(right, k) for _, _, right, ks, _ in tasks for k in ks},
        key=lambda x: (x[0], -x[1]),
    )
    arrays, sources = [], {}
    for role, k in used:
        array, part = held[role][k]
        index = next((i for i, x in enumerate(arrays) if x is array), len(arrays))
        if index == len(arrays):
            arrays.append(array)
        sources[role, k] = (index, part)
    layout = sorted({role for role, k in used if (role, k) not in flats})
    tiles = sum(len(task[1]) * len(task[3]) for task in tasks)
    kept = [
        jax.ShapeDtypeStruct((roles, 8, slots), jnp.float32),
        jax.ShapeDtypeStruct((len(layout), slots, width), jnp.bfloat16),
    ]
    scratch = [pltpu.VMEM((roles, slots, LANES), jnp.float32)] * 2
    if last:
        scratch = [pltpu.VMEM(x.shape, x.dtype) for x in kept] + scratch
        kept = []
    known = dict(flats)
    got = call(
        lambda *refs: score_kernel(sources, known, layout, tasks, done, last, *refs),
        kept + [jax.ShapeDtypeStruct((1, slots), jnp.float32)] * len(done),
        scratch,
        arrays + list(acc),
        2 * tiles * LANES * LANES * width,
        2 * len(used) * LANES * width,
    )
    if last:
        return acc, got
    for role, k in used:
        if (role, k) not in flats:
            flats[role, k] = (max(len(acc) - 1, 0), layout.index(role))
    return [got[0], *acc[1:], got[1]], got[2:]


def per_device(embeddings, row_group, row_cluster):
    rows, width = embeddings.shape
    groups = lax.axis_size("group")
    shards = lax.axis_size("shard")
    capacity = rows // 4
    slots = groups * capacity
    ring = ring_order(shards)
    offsets, pairs = offset_cover(shards)
    roles = len(offsets)
    height = width * capacity // LANES + TAIL

    def from_offset(x, offset):
        perm = [(ring[(e + offset) % shards], ring[e]) for e in range(shards)]
        return lax.ppermute(x, "shard", perm)

    def exchange(blocks):
        got = list(blocks)
        for k in range(1, groups):
            shift = slot_shift(k)
            block = after(blocks[k], got[2]) if k > 2 else blocks[k]
            got[k] = lax.ppermute(block, "group", [(z, (z + shift) % groups) for z in range(groups)])
        return got

    (units,) = call(
        unit_kernel,
        [jax.ShapeDtypeStruct((rows, width), jnp.bfloat16)],
        [pltpu.VMEM((rows, width), embeddings.dtype), pltpu.SemaphoreType.DMA((2,))],
        (embeddings,),
        4 * rows * width,
        4 * rows * width,
        [pl.BlockSpec(memory_space=pltpu.HBM)],
        53 * MIB,
    )
    *send, place = call(
        lambda *refs: sort_kernel("group", *refs),
        [jax.ShapeDtypeStruct((height, LANES), jnp.bfloat16)] * groups
        + [jax.ShapeDtypeStruct((1, rows), jnp.int32)],
        [],
        (units, *lax.optimization_barrier((row_group.reshape(1, rows), row_cluster.reshape(1, rows)))),
        2 * rows * slots * width,
        4 * rows * width,
    )

    late = [groups - 1] if groups > 1 else []
    early = list(range(groups - len(late)))
    late = [groups - 1] if groups > 1 else []
    early = list(range(groups - len(late)))
    near = [r for r in range(1, roles) if 2 * offsets[r] != shards]
    far = [r for r in range(1, roles) if r not in near]
    first = {r: from_offset(send[0], offsets[r]) for r in near}
    own = exchange(send)
    held = [[None] * groups for _ in offsets]
    held[0] = [(x, None) for x in own]
    for r in near:
        held[r][0] = (first[r], None)
    for ks in (early[1:], late):
        if ks:
            block = stack([own[k] for k in ks], WAIT)
            for r in near:
                moved = from_offset(block, offsets[r])
                for i, k in enumerate(ks):
                    held[r][k] = (moved, i)
    got = {r: from_offset(stack(own, 0), offsets[r]) for r in far}
    for r in far:
        held[r] = [(got[r], k) for k in range(groups)]
    everything = [(0, 0, False)]
    everything += [(offsets.index(a), offsets.index(b), both) for a, b, both in pairs]
    steps = [[] for _ in range(4)]
    final = [0] * roles
    for left, right, both in everything:
        for left_ks in (early, late):
            for right_ks in (early, late):
                if left_ks and right_ks:
                    step = 0
                    for role, ks in ((left, left_ks), (right, right_ks)):
                        if role in near:
                            step = max(step, 1 if ks is early else 3 if role == near[0] else 2)
                    task = (left, left_ks, right, right_ks, both)
                    if both and right_ks is late and left_ks is early:
                        task = (right, right_ks, left, left_ks, both)
                    steps[step].append(task)
                    final[right] = max(final[right], step)
                    if both:
                        final[left] = max(final[left], step)
    acc, flats, partial = [], {}, [None] * roles
    for step, tasks in enumerate(steps):
        if tasks:
            done = [r for r in range(roles) if final[r] == step]
            last = not any(steps[step + 1 :])
            acc, ends = score(held, tasks, acc, flats, done, last, slots, width)
            for r, end in zip(done, ends):
                partial[r] = end
    (best,) = call(
        lambda *refs: spread_kernel(ring, offsets, groups, *refs),
        [jax.ShapeDtypeStruct((shards * groups, 1, capacity), jnp.float32)],
        [],
        partial,
        roles * slots,
        4 * roles * slots,
    )
    back = lax.all_to_all(best, ("shard", "group"), split_axis=0, concat_axis=0, tiled=True)
    (result,) = call(
        lambda *refs: place_kernel(groups, *refs),
        [jax.ShapeDtypeStruct((1, rows), jnp.float32)],
        [],
        [back, place],
        rows * slots,
        4 * slots,
    )
    return result.reshape(rows)


def solution(mesh):
    placed = (P(("shard", "group"), None), P(("shard", "group"), None), P(("shard", "group")))
    return jax.shard_map(
        per_device, mesh=mesh, in_specs=placed, out_specs=P(("shard", "group")), check_vma=False
    )
```

```python
import jax
import jax.numpy as jnp
from jax import lax
from jax.experimental import pallas as pl
from jax.experimental.pallas import tpu as pltpu
from jax.sharding import PartitionSpec as P

LANES = 128
TAIL = 16
LOW = -2.0
MIB = 1024 * 1024
WAIT = 2 * 10**10


def ring_order(size):
    if size % 2:
        return list(range(size))
    half = size // 2
    chips = [i ^ (i >> 1) for i in range(half)]
    if sorted(chips) != list(range(half)):
        chips = list(range(half))
    return [2 * chip + core for core in range(2) for chip in chips]


def offset_cover(size):
    offsets = list(dict.fromkeys([0, size // 2, 1 % size, (size - 1) % size]))

    def missing(chosen):
        have = {(a - b) % size for a in chosen for b in chosen}
        return [d for d in range(size) if d not in have]

    while missing(offsets):
        offsets.append(min(range(size), key=lambda x: len(missing(offsets + [x]))))
    pairs = []
    for diff in range(1, size // 2 + 1):
        found = [
            (a, b)
            for b in [(size - 1) % size] + offsets
            for a in offsets
            if (a - b) % size in (diff, size - diff)
        ]
        if 2 * diff == size:
            found = [(a, b) for a, b in found if b == 0] + found
        a, b = found[0]
        pairs.append((a, b, b != 0 or 2 * diff != size))
    return offsets, pairs


def column_of(row):
    size = row.shape[1]
    return jnp.transpose(jnp.broadcast_to(row, (size, size)))


def unit_kernel(far_ref, unit_ref, near_ref, sems):
    parts = sems.shape[0]
    size = far_ref.shape[0] // parts
    copies = [
        pltpu.make_async_copy(
            far_ref.at[pl.ds(i * size, size), :], near_ref.at[pl.ds(i * size, size), :], sems.at[i]
        )
        for i in range(parts)
    ]
    for copy in copies:
        copy.start()
    for i, copy in enumerate(copies):
        copy.wait()
        feats = near_ref[pl.ds(i * size, size), :].astype(jnp.float32)
        squares = jnp.sum(feats * feats, axis=1, keepdims=True) + 1e-06
        unit_ref[pl.ds(i * size, size), :] = (feats * lax.rsqrt(squares)).astype(jnp.bfloat16)


def sort_kernel(axis, unit_ref, group_ref, label_ref, *out_refs):
    *block_refs, place_ref = out_refs
    rows, width = unit_ref.shape
    groups = len(block_refs)
    capacity = (block_refs[0].shape[0] - TAIL) * LANES // width
    slots = groups * capacity
    chunks = width // LANES
    owner = group_ref[...]
    shift = (owner - lax.axis_index(axis)) & (groups - 1)
    rel = jnp.maximum(jnp.where(2 * shift > groups, 2 * (groups - shift), 2 * shift - 1), 0)
    lines = max(8, groups)
    onehot = lax.broadcasted_iota(jnp.int32, (lines, rows), 0) == rel
    before = lax.broadcasted_iota(jnp.int32, (rows, rows), 0) < lax.broadcasted_iota(
        jnp.int32, (rows, rows), 1
    )
    ranks = jnp.dot(
        jnp.where(onehot, 1.0, 0.0).astype(jnp.bfloat16),
        jnp.where(before, 1.0, 0.0).astype(jnp.bfloat16),
        preferred_element_type=jnp.float32,
    )
    rank = jnp.sum(jnp.where(onehot, ranks, 0.0), axis=0, keepdims=True).astype(jnp.int32)
    place_ref[...] = owner * capacity + rank
    move = jnp.where(
        lax.broadcasted_iota(jnp.int32, (slots, rows), 0) == rel * capacity + rank, 1.0, 0.0
    ).astype(jnp.bfloat16)
    labels = jnp.broadcast_to(label_ref[...] + 1, (TAIL, rows)).astype(jnp.bfloat16)
    sorted_labels = (
        lax.dot_general(
            labels, move, (((1,), (1,)), ((), ())), preferred_element_type=jnp.float32
        )
        - 1.0
    ).astype(jnp.bfloat16)
    for k, block_ref in enumerate(block_refs):
        part = slice(k * capacity, (k + 1) * capacity)
        block = jnp.dot(
            move[part], unit_ref[...], preferred_element_type=jnp.float32
        ).astype(jnp.bfloat16)
        for c in range(chunks):
            block_ref[pl.ds(c * capacity, capacity), :] = block[:, c * LANES : (c + 1) * LANES]
        block_ref[pl.ds(chunks * capacity, TAIL), :] = sorted_labels[:, part]


def stack_kernel(*refs):
    for k, ref in enumerate(refs[:-1]):
        refs[-1][k] = ref[...]


def score_kernel(sources, flats, layout, tasks, done, last, *refs):
    *refs, side_ref, row_ref = refs
    if last:
        *refs, best_ref, flat_ref = refs
        inputs, out_refs = refs[: -len(done)], refs[-len(done) :]
    else:
        outs = 2 + len(done)
        inputs, (best_ref, flat_ref, *out_refs) = refs[:-outs], refs[-outs:]
    capacity = LANES
    low = jnp.float32(LOW)
    arrays = 1 + max(index for index, _ in sources.values())
    best_ref[...] = inputs[arrays][...] if len(inputs) > arrays else jnp.full(best_ref.shape, low)

    def units(role, ks):
        rows = pl.ds(ks[0] * capacity, len(ks) * capacity)
        if (role, ks[0]) in flats:
            index, place = flats[role, ks[0]]
            return inputs[arrays + 1 + index][place, rows, :]
        return flat_ref[layout.index(role), rows, :]

    tops = {}
    for (role, k), (index, part) in sources.items():
        ref = inputs[index] if part is None else inputs[index].at[part]
        height = ref.shape[0] - TAIL
        rows = pl.ds(k * capacity, capacity)
        if (role, k) not in flats:
            for c in range(height // capacity):
                flat_ref[layout.index(role), rows, pl.ds(c * LANES, LANES)] = ref[
                    pl.ds(c * capacity, capacity), :
                ]
        tops[role, k] = ref[pl.ds(height, TAIL), :][0:1].astype(jnp.float32)
    for role, k in sorted({(left, k) for left, ks, _, _, _ in tasks for k in ks}):
        side_ref[role, pl.ds(k * capacity, capacity), :] = column_of(tops[role, k])
    turns = sorted({(left, k) for left, ks, _, _, both in tasks if both for k in ks})
    for role, k in turns:
        row_ref[role, pl.ds(k * capacity, capacity), :] = jnp.full((capacity, LANES), low)
    for left, left_ks, right, right_ks, both in tasks:
        start, count = left_ks[0] * capacity, len(left_ks) * capacity
        rows = pl.ds(start, count)
        for i in range(0, len(right_ks), 2):
            some = right_ks[i : i + 2]
            width = len(some) * capacity
            columns = pl.ds(some[0] * capacity, width)
            scores = lax.dot_general(
                units(left, left_ks),
                units(right, some),
                (((1,), (1,)), ((), ())),
                preferred_element_type=jnp.float32,
            )
            top = jnp.concatenate([tops[right, k] for k in some], axis=1)
            same = jnp.concatenate([side_ref[left, rows, :]] * len(some), axis=1) == top
            if left == right:
                same = same & (
                    lax.broadcasted_iota(jnp.int32, (count, width), 0) + start
                    != lax.broadcasted_iota(jnp.int32, (count, width), 1) + some[0] * capacity
                )
            scores = jnp.where(same, scores, low)
            if both:
                best = row_ref[left, rows, :]
                for c in range(len(some)):
                    best = jnp.maximum(best, scores[:, c * LANES : (c + 1) * LANES])
                row_ref[left, rows, :] = best
            best = jnp.max(scores.reshape(count // 8, 8, width), axis=0)
            best_ref[right, :, columns] = jnp.maximum(best_ref[right, :, columns], best)
    for role, k in turns:
        rows = pl.ds(k * capacity, capacity)
        turned = jnp.transpose(row_ref[role, rows, :]).reshape(capacity // 8, 8, capacity)
        best_ref[role, :, rows] = jnp.maximum(best_ref[role, :, rows], jnp.max(turned, axis=0))
    for role, out_ref in zip(done, out_refs):
        out_ref[...] = jnp.max(best_ref[role], axis=0, keepdims=True)


def slot_shift(k):
    return (k + 1) // 2 if k % 2 else -(k // 2)


def spread_kernel(ring, offsets, groups, *refs):
    *partial_refs, out_ref = refs
    shards = len(ring)
    out_ref[...] = jnp.full(out_ref.shape, jnp.float32(LOW))
    shard, group = lax.axis_index("shard"), lax.axis_index("group")
    for offset, ref in zip(offsets, partial_refs):
        target = sum(
            jnp.where(shard == ring[e], ring[(e + offset) % shards], 0) for e in range(shards)
        )
        for k in range(groups):
            row = target * groups + ((group - slot_shift(k)) & (groups - 1))
            out_ref[pl.ds(row, 1)] = ref[:, k * LANES : (k + 1) * LANES].reshape(1, 1, LANES)


def place_kernel(groups, back_ref, place_ref, out_ref):
    place = place_ref[...]
    rows = place.shape[1]
    best = jnp.full((1, rows), jnp.float32(LOW))
    for g in range(groups):
        row = jnp.full((1, LANES), jnp.float32(-1.0))
        for s in range(back_ref.shape[0] // groups):
            row = jnp.maximum(row, back_ref[s * groups + g])
        values = jnp.concatenate([column_of(row)] * (rows // LANES), axis=1)
        here = lax.broadcasted_iota(jnp.int32, (LANES, rows), 0) + g * LANES == place
        best = jnp.maximum(
            best, jnp.max(jnp.where(here, values, jnp.float32(LOW)), axis=0, keepdims=True)
        )
    out_ref[...] = best


def in_vmem(count):
    return [pl.BlockSpec(memory_space=pltpu.VMEM)] * count


def call(
    kernel, out_shape, scratch, args, flops, bytes_accessed, in_specs=None, limit=24 * MIB
):
    return pl.pallas_call(
        kernel,
        out_shape=out_shape,
        in_specs=in_specs or in_vmem(len(args)),
        out_specs=in_vmem(len(out_shape)),
        scratch_shapes=scratch,
        compiler_params=pltpu.CompilerParams(vmem_limit_bytes=limit),
        cost_estimate=pl.CostEstimate(
            flops=flops, bytes_accessed=bytes_accessed, transcendentals=0
        ),
    )(*args)


def after(x, *earlier):
    return lax.optimization_barrier((x, *earlier))[0]


def stack(parts, wait):
    return call(
        stack_kernel,
        [jax.ShapeDtypeStruct((len(parts), *parts[0].shape), parts[0].dtype)],
        [],
        parts,
        wait,
        4 * len(parts) * parts[0].size,
    )[0]


def score(held, tasks, acc, flats, done, last, slots, width):
    roles = len(held)
    used = sorted(
        {(left, k) for left, ks, _, _, _ in tasks for k in ks}
        | {(right, k) for _, _, right, ks, _ in tasks for k in ks},
        key=lambda x: (x[0], -x[1]),
    )
    arrays, sources = [], {}
    for role, k in used:
        array, part = held[role][k]
        index = next((i for i, x in enumerate(arrays) if x is array), len(arrays))
        if index == len(arrays):
            arrays.append(array)
        sources[role, k] = (index, part)
    layout = sorted({role for role, k in used if (role, k) not in flats})
    tiles = sum(len(task[1]) * len(task[3]) for task in tasks)
    kept = [
        jax.ShapeDtypeStruct((roles, 8, slots), jnp.float32),
        jax.ShapeDtypeStruct((len(layout), slots, width), jnp.bfloat16),
    ]
    scratch = [pltpu.VMEM((roles, slots, LANES), jnp.float32)] * 2
    if last:
        scratch = [pltpu.VMEM(x.shape, x.dtype) for x in kept] + scratch
        kept = []
    known = dict(flats)
    got = call(
        lambda *refs: score_kernel(sources, known, layout, tasks, done, last, *refs),
        kept + [jax.ShapeDtypeStruct((1, slots), jnp.float32)] * len(done),
        scratch,
        arrays + list(acc),
        2 * tiles * LANES * LANES * width,
        2 * len(used) * LANES * width,
    )
    if last:
        return acc, got
    for role, k in used:
        if (role, k) not in flats:
            flats[role, k] = (max(len(acc) - 1, 0), layout.index(role))
    return [got[0], *acc[1:], got[1]], got[2:]


def per_device(embeddings, row_group, row_cluster):
    rows, width = embeddings.shape
    groups = lax.axis_size("group")
    shards = lax.axis_size("shard")
    capacity = rows // 4
    slots = groups * capacity
    ring = ring_order(shards)
    offsets, pairs = offset_cover(shards)
    roles = len(offsets)
    height = width * capacity // LANES + TAIL

    def from_offset(x, offset):
        perm = [(ring[(e + offset) % shards], ring[e]) for e in range(shards)]
        return lax.ppermute(x, "shard", perm)

    def exchange(blocks):
        got = list(blocks)
        for k in range(1, groups):
            shift = slot_shift(k)
            block = after(blocks[k], got[1]) if k > 2 else blocks[k]
            got[k] = lax.ppermute(block, "group", [(z, (z + shift) % groups) for z in range(groups)])
        return got

    (units,) = call(
        unit_kernel,
        [jax.ShapeDtypeStruct((rows, width), jnp.bfloat16)],
        [pltpu.VMEM((rows, width), embeddings.dtype), pltpu.SemaphoreType.DMA((1,))],
        (embeddings,),
        4 * rows * width,
        4 * rows * width,
        [pl.BlockSpec(memory_space=pltpu.HBM)],
        53 * MIB,
    )
    *send, place = call(
        lambda *refs: sort_kernel("group", *refs),
        [jax.ShapeDtypeStruct((height, LANES), jnp.bfloat16)] * groups
        + [jax.ShapeDtypeStruct((1, rows), jnp.int32)],
        [],
        (units, *lax.optimization_barrier((row_group.reshape(1, rows), row_cluster.reshape(1, rows)))),
        2 * rows * slots * width,
        4 * rows * width,
    )

    late = [groups - 1] if groups > 1 else []
    early = list(range(groups - len(late)))
    late = [groups - 1] if groups > 1 else []
    early = list(range(groups - len(late)))
    near = [r for r in range(1, roles) if 2 * offsets[r] != shards]
    far = [r for r in range(1, roles) if r not in near]
    first = {r: from_offset(send[0], offsets[r]) for r in near}
    own = exchange(send)
    held = [[None] * groups for _ in offsets]
    held[0] = [(x, None) for x in own]
    for r in near:
        held[r][0] = (first[r], None)
    for ks in (early[1:], late):
        if ks:
            block = stack([own[k] for k in ks], WAIT)
            for r in near:
                moved = from_offset(block, offsets[r])
                for i, k in enumerate(ks):
                    held[r][k] = (moved, i)
    got = {r: from_offset(stack(own, 0), offsets[r]) for r in far}
    for r in far:
        held[r] = [(got[r], k) for k in range(groups)]
    everything = [(0, 0, False)]
    everything += [(offsets.index(a), offsets.index(b), both) for a, b, both in pairs]
    steps = [[] for _ in range(4)]
    final = [0] * roles
    for left, right, both in everything:
        for left_ks in (early, late):
            for right_ks in (early, late):
                if left_ks and right_ks:
                    step = 0
                    for role, ks in ((left, left_ks), (right, right_ks)):
                        if role in near:
                            step = max(step, 1 if ks is early else 3 if role == near[0] else 2)
                    task = (left, left_ks, right, right_ks, both)
                    if both and right_ks is late and left_ks is early:
                        task = (right, right_ks, left, left_ks, both)
                    steps[step].append(task)
                    final[right] = max(final[right], step)
                    if both:
                        final[left] = max(final[left], step)
    acc, flats, partial = [], {}, [None] * roles
    for step, tasks in enumerate(steps):
        if tasks:
            done = [r for r in range(roles) if final[r] == step]
            last = not any(steps[step + 1 :])
            acc, ends = score(held, tasks, acc, flats, done, last, slots, width)
            for r, end in zip(done, ends):
                partial[r] = end
    (best,) = call(
        lambda *refs: spread_kernel(ring, offsets, groups, *refs),
        [jax.ShapeDtypeStruct((shards * groups, 1, capacity), jnp.float32)],
        [],
        partial,
        roles * slots,
        4 * roles * slots,
    )
    back = lax.all_to_all(best, ("shard", "group"), split_axis=0, concat_axis=0, tiled=True)
    (result,) = call(
        lambda *refs: place_kernel(groups, *refs),
        [jax.ShapeDtypeStruct((1, rows), jnp.float32)],
        [],
        [back, place],
        rows * slots,
        4 * slots,
    )
    return result.reshape(rows)


def solution(mesh):
    placed = (P(("shard", "group"), None), P(("shard", "group"), None), P(("shard", "group")))
    return jax.shard_map(
        per_device, mesh=mesh, in_specs=placed, out_specs=P(("shard", "group")), check_vma=False
    )
```
